32 devices in a mesh: dp: 8 (over z, x), psg: 4 (over y, core).
Axes of the slice: x: 2, y: 2, z: 4, core: 2. Of those that a mesh axis runs over, the one named last changes fastest.
Arguments:
- passage_states: bfloat16 [64, 512, 768], P(('dp', 'psg')), may hold values from -6 to 6
- segment_ids: int32 [64, 512], P(('dp', 'psg')), may hold values from 0 to 2, never falling along the last dimension, each value on 1 to 180 neighbouring positions
- query_states: bfloat16 [128, 32, 768], P(('dp', 'psg')), may hold values from -6 to 6
- teacher_scores: float32 [128, 24], P('dp', 'psg'), may hold values from -18 to 18
- w_qkv: bfloat16 [768, 2304], replicated, may hold values from -0.21875 to 0.21875
- bias_q: float32 [768], replicated, may hold values from -1.5 to 1.5
- bias_v: float32 [768], replicated, may hold values from -1.5 to 1.5
- w_out: bfloat16 [768, 768], replicated, may hold values from -1.75 to 1.75
- bias_out: float32 [768], replicated, may hold values from -1.5 to 1.5
- ln1_gain: float32 [768], replicated, may hold values from 0.5 to 1.5
- ln1_bias: float32 [768], replicated, may hold values from -1.5 to 1.5
- w_up: bfloat16 [768, 3072], replicated, may hold values from -0.21875 to 0.21875
- bias_up: float32 [3072], replicated, may hold values from -1.5 to 1.5
- w_down: bfloat16 [3072, 768], replicated, may hold values from -0.109375 to 0.109375
- bias_down: float32 [768], replicated, may hold values from -1.5 to 1.5
- ln2_gain: float32 [768], replicated, may hold values from 0.5 to 1.5
- ln2_bias: float32 [768], replicated, may hold values from -1.5 to 1.5
- w_proj: bfloat16 [768, 128], replicated, may hold values from -0.21875 to 0.21875
Outputs:
- passage_embed: bfloat16 [64, 512, 128], P(('dp', 'psg'))
- query_embed: bfloat16 [128, 32, 128], P(('dp', 'psg'))
- loss: float32 [], replicated
- grad_passages: float32 [64, 512, 768], P(('dp', 'psg'))
- grad_queries: float32 [128, 32, 768], P(('dp', 'psg'))
- grad_w_qkv: float32 [768, 2304], P(('dp', 'psg'))
- grad_bias_q: float32 [768], P(('dp', 'psg'))
- grad_bias_v: float32 [768], P(('dp', 'psg'))
- grad_w_out: float32 [768, 768], P(('dp', 'psg'))
- grad_bias_out: float32 [768], P(('dp', 'psg'))
- grad_ln1_gain: float32 [768], P(('dp', 'psg'))
- grad_ln1_bias: float32 [768], P(('dp', 'psg'))
- grad_w_up: float32 [768, 3072], P(('dp', 'psg'))
- grad_bias_up: float32 [3072], P(('dp', 'psg'))
- grad_w_down: float32 [3072, 768], P(('dp', 'psg'))
- grad_bias_down: float32 [768], P(('dp', 'psg'))
- grad_ln2_gain: float32 [768], P(('dp', 'psg'))
- grad_ln2_bias: float32 [768], P(('dp', 'psg'))
- grad_w_proj: float32 [768, 128], P(('dp', 'psg'))
The draws below stay inside these ranges and needn't reach their ends.
Inputs may be any that keep to these rules, and one draw needn't show every extreme that they name: `segment_ids`: in each row the passage numbers 0 to 2 follow in order, each passage 1 to 180 positions long, one of them exactly 180.
All inputs are finite; a program needn't handle non-finite values.
Results may differ from the reference program's by a relative error of at most 0.015.
Values may be sent and summed in bfloat16 or wider, within the bound.
A program may use at most 256 MiB of HBM per device.

```python
import math
import jax
import jax.numpy as jnp
import numpy as np
from jax import lax

D = 768
H = 12
HD = 64
FF = 3072
EMB = 128
SEQ = 512
SEGS = 3
PASS_MAX = 180
QLEN = 32
ROWS = 64
QUERIES = 128
Q_GRP = 16
P_GRP = 24
N_DP = 8


def draw_teacher_scores(key, part):
    key = jax.random.fold_in(key, 7)
    position = (jnp.arange(QUERIES, dtype=jnp.int32) // Q_GRP).astype(jnp.float32) / max(N_DP - 1, 1)
    spread = 0.3 * jnp.exp(position * 2.9957)
    values = jnp.clip(jax.random.normal(key, (QUERIES, P_GRP), jnp.float32), -3.0, 3.0)
    return values * spread[:, None]


def spiked(values, own_key, source, target, parts, factor):
    def block_of(dim):
        return (jnp.arange(values.shape[dim]) // (values.shape[dim] // parts)).reshape((-1,) + (1,) * (values.ndim - 1 - dim))

    first = jax.random.permutation(own_key, parts)[block_of(target)]
    other_side = (block_of(target) + parts // 2) % parts
    return jnp.where((block_of(source) == first) | (block_of(source) == other_side), factor * values, values)


def levels(own_key, dims, split, smallest, top_value):
    factor_of = 1.0
    for dim, parts in split:
        steps = jax.random.uniform(jax.random.fold_in(jax.random.fold_in(own_key, 6), dim), (parts,), jnp.float32, smallest / len(split), top_value / len(split))
        factor_of = factor_of * jnp.repeat(jnp.exp(steps), dims[dim] // parts).reshape((-1,) + (1,) * (len(dims) - 1 - dim))
    return factor_of


def profile(amount, total, bound, skew):
    weights = [(1 << 20) // math.isqrt(rank ** skew) + 1 for rank in range(2, amount + 1)]
    surplus, holding = total - bound - (amount - 1), [1] * (amount - 1)
    while surplus > 0:
        movable = [i for i in range(amount - 1) if holding[i] < bound]
        mass, left = sum([weights[i] for i in movable]), surplus
        for i in movable:
            extra = min(bound - holding[i], max(1, left * weights[i] // mass), surplus)
            holding[i] = holding[i] + extra
            surplus = surplus - extra
    return np.array([bound] + holding)


def ragged_sizes(key, amount, total, bound, lean):
    if amount == 2:
        one = jax.random.randint(key, (), max(1, total - bound), min(bound, total - 1) + 1)
        return jnp.stack([one, total - one])
    sizes = jnp.asarray(profile(amount, total, bound, lean), jnp.int32)
    couples = (amount - 1) // 2
    giver, taker = sizes[1:1 + 2 * couples:2], sizes[2:2 + 2 * couples:2]
    margin = jnp.minimum(giver - 1, bound - taker)
    passed = jax.random.randint(jax.random.fold_in(key, 1), (couples,), 0, 1 << 20) % (margin + 1)
    sizes = sizes.at[1:1 + 2 * couples:2].set(giver - passed).at[2:2 + 2 * couples:2].set(taker + passed)
    return sizes[jax.random.permutation(jax.random.fold_in(key, 2), amount)]


def bell_draw(stream_key, dims, scale, reach, split=(), kind=jnp.bfloat16):
    drawn = jax.random.normal(stream_key, dims, jnp.float32) * scale
    if len(split) > 0:
        drawn = levels(stream_key, dims, split, -0.22, 0.18) * drawn
    return jnp.clip(drawn, min=-reach, max=reach).astype(kind)


def noise_with(own_key, extent, scale, most, pieces, heavy, kind=jnp.bfloat16):
    entries = scale * jax.random.normal(own_key, extent, jnp.float32)
    if pieces:
        entries = entries * levels(own_key, extent, pieces, -0.22, 0.18)
    return jnp.clip(spiked(entries, jax.random.fold_in(own_key, 3), *heavy), -most, most).astype(kind)


def setup_inputs(seed: int = 0) -> dict:
    seeds = jax.random.split(jax.random.key(seed), 19)
    return {
        "passage_states": noise_with(seeds[0], (ROWS, SEQ, D), 1.0, 6.0, ((0, 32),), (0, 2, 32, 2.75)),
        "segment_ids": jax.vmap(lambda own: jnp.searchsorted(jnp.cumsum(ragged_sizes(own, SEGS, SEQ, PASS_MAX, 0)), jnp.arange(SEQ), side="right"))(jax.random.split(seeds[1], ROWS)).reshape((ROWS, SEQ)).astype(jnp.int32),
        "query_states": bell_draw(seeds[2], (QUERIES, QLEN, D), 1.0, 6.0, ((0, 32),)),
        "teacher_scores": draw_teacher_scores(jax.random.fold_in(seeds[18], 71), 0),
        "w_qkv": bell_draw(seeds[4], (D, 3 * D), D ** -0.5, 0.21875),
        "bias_q": bell_draw(seeds[5], (D,), 0.3, 1.5, (), jnp.float32),
        "bias_v": bell_draw(seeds[6], (D,), 0.3, 1.5, (), jnp.float32),
        "w_out": bell_draw(seeds[7], (D, D), (D // 64) ** -0.5, 1.75),
        "bias_out": bell_draw(seeds[8], (D,), 0.3, 1.5, (), jnp.float32),
        "ln1_gain": jnp.clip(1.0 + 0.1 * jax.random.normal(seeds[9], (D,), jnp.float32), 0.5, 1.5),
        "ln1_bias": bell_draw(seeds[10], (D,), 0.3, 1.5, (), jnp.float32),
        "w_up": bell_draw(seeds[11], (D, FF), D ** -0.5, 0.21875),
        "bias_up": bell_draw(seeds[12], (FF,), 0.3, 1.5, (), jnp.float32),
        "w_down": bell_draw(seeds[13], (FF, D), FF ** -0.5, 0.109375),
        "bias_down": bell_draw(seeds[14], (D,), 0.3, 1.5, (), jnp.float32),
        "ln2_gain": jnp.clip(1.0 + 0.1 * jax.random.normal(seeds[15], (D,), jnp.float32), 0.5, 1.5),
        "ln2_bias": bell_draw(seeds[16], (D,), 0.3, 1.5, (), jnp.float32),
        "w_proj": bell_draw(seeds[17], (D, EMB), D ** -0.5, 0.21875),
    }


@jax.custom_vjp
def low(v):
    return lax.optimization_barrier(v.astype(jnp.bfloat16)).astype(jnp.float32)

@jax.custom_vjp
def low_back(v):
    return v

def low_keep(v):
    return (low(v), None)

def low_pass(kept, grad):
    return (grad,)

def back_keep(v):
    return (v, None)

def back_low(kept, grad):
    return (low(grad),)
low.defvjp(low_keep, low_pass)
low_back.defvjp(back_keep, back_low)
largest_score = lax.Precision.HIGHEST
sharpness_divisor = 0.1
root_half = 0.7071067811865476

def gelu(values):
    return 0.5 * values * (1.0 + jax.scipy.special.erf(values * root_half))

def layer_norm(values, gain, shift):
    average = lax.optimization_barrier(jnp.mean(values, -1, keepdims=True))
    centred = values - average
    inverse_std = lax.rsqrt(lax.optimization_barrier(jnp.mean(centred * centred, -1, keepdims=True)) + 1e-12)
    return centred * inverse_std * gain + shift

def log_norm(values):
    top = lax.optimization_barrier(jnp.max(values, -1, keepdims=True))
    shifted = values - top
    return shifted - jnp.log(lax.optimization_barrier(jnp.sum(jnp.exp(shifted), -1, keepdims=True)))

def encode(states, segments, weights):
    w_qkv, bias_q, bias_v, w_out, bias_out, ln1_gain, ln1_bias, w_up, bias_up, w_down, bias_down, ln2_gain, ln2_bias, w_proj = weights
    length = states.shape[0]
    width = states.shape[1]
    bias_mixed = jnp.concatenate([bias_q, jnp.zeros_like(bias_q), bias_v])
    mixed = low(low_back(jnp.dot(states, w_qkv, precision=largest_score) + bias_mixed))
    query_h = mixed[:, :width].reshape(length, H, HD)
    key_h = mixed[:, width:2 * width].reshape(length, H, HD)
    content_headwise = mixed[:, 2 * width:].reshape(length, H, HD)
    scores = low_back(jnp.einsum('qhe,khe->hqk', query_h, key_h, precision=largest_score) * 0.125)
    same_seg = segments[:, None] == segments[None, :]
    masked = jnp.where(same_seg[None], scores, -1e+30)
    top = lax.optimization_barrier(jnp.max(masked, -1, keepdims=True))
    power_entries = jnp.exp(masked - top)
    probs = low(power_entries / lax.optimization_barrier(jnp.sum(power_entries, -1, keepdims=True)))
    context = low(low_back(jnp.einsum('hqk,khe->qhe', probs, content_headwise, precision=largest_score).reshape(length, width)))
    attended = low_back(jnp.dot(context, w_out, precision=largest_score) + bias_out)
    first = layer_norm(states + attended, ln1_gain, ln1_bias)
    hidden_pre = low_back(jnp.dot(low(first), w_up, precision=largest_score) + bias_up)
    hidden = low(gelu(hidden_pre))
    branch = low_back(jnp.dot(hidden, w_down, precision=largest_score) + bias_down)
    second = layer_norm(first + branch, ln2_gain, ln2_bias)
    project = low_back(jnp.dot(low(second), w_proj, precision=largest_score))
    unit = project * lax.rsqrt(lax.optimization_barrier(jnp.sum(project * project, -1, keepdims=True)) + 1e-06)
    return low(unit)

def group_kl(pack):
    query_group, pass_group, index_group, teach_group = pack
    affinity_entries = low_back(jnp.dot(query_group, pass_group.T, precision=largest_score))
    power_entries = jnp.exp((affinity_entries - 1.0) / sharpness_divisor)
    indicator_matrix = (index_group[:, None] == jnp.arange(P_GRP, dtype=jnp.int32)[None, :]).astype(jnp.float32)
    cumulative_totals = jnp.dot(power_entries, indicator_matrix, precision=largest_score)
    piece_tallies = lax.optimization_barrier(jnp.sum(indicator_matrix, 0))
    aggregated_lines = jnp.log(cumulative_totals / piece_tallies) + 1.0 / sharpness_divisor
    logits = lax.optimization_barrier(jnp.sum(aggregated_lines.reshape(Q_GRP, QLEN, P_GRP), 1))
    student = log_norm(logits)
    teacher = log_norm(teach_group)
    return jnp.sum(jnp.exp(teacher) * (teacher - student))

def reference(passage_states, segment_ids, query_states, teacher_scores, w_qkv, bias_q, bias_v, w_out, bias_out, ln1_gain, ln1_bias, w_up, bias_up, w_down, bias_down, ln2_gain, ln2_bias, w_proj):
    weights = tuple((member.astype(jnp.float32) for member in (w_qkv, bias_q, bias_v, w_out, bias_out, ln1_gain, ln1_bias, w_up, bias_up, w_down, bias_down, ln2_gain, ln2_bias, w_proj)))
    pass_float = passage_states.astype(jnp.float32)
    query_float = query_states.astype(jnp.float32)
    query_segs = jnp.zeros((QUERIES, QLEN), jnp.int32)
    rows_group = ROWS // N_DP
    group_index = (jnp.arange(rows_group, dtype=jnp.int32)[None, :, None] * SEGS + segment_ids.reshape(N_DP, rows_group, SEQ)).reshape(N_DP, rows_group * SEQ)
    teach_groups = teacher_scores.astype(jnp.float32).reshape(N_DP, Q_GRP, P_GRP)

    def forward(pass_in, query_in, params):

        def encode_one(pair):
            return encode(pair[0], pair[1], params)
        pass_emb = lax.map(jax.checkpoint(encode_one), (pass_in, segment_ids))
        query_emb = lax.map(jax.checkpoint(encode_one), (query_in, query_segs))
        per_group = lax.map(jax.checkpoint(group_kl), (query_emb.reshape(N_DP, Q_GRP * QLEN, EMB), pass_emb.reshape(N_DP, rows_group * SEQ, EMB), group_index, teach_groups))
        return (jnp.sum(per_group) / N_DP, (pass_emb, query_emb))
    loss, back_fn, embeds = jax.vjp(forward, pass_float, query_float, weights, has_aux=True)
    grad_pass, grad_query, derivative_coefficients = back_fn(jnp.ones_like(loss))
    return (embeds[0].astype(jnp.bfloat16), embeds[1].astype(jnp.bfloat16), loss, grad_pass, grad_query, derivative_coefficients[0], derivative_coefficients[1], derivative_coefficients[2], derivative_coefficients[3], derivative_coefficients[4], derivative_coefficients[5], derivative_coefficients[6], derivative_coefficients[7], derivative_coefficients[8], derivative_coefficients[9], derivative_coefficients[10], derivative_coefficients[11], derivative_coefficients[12], derivative_coefficients[13])
```

```python
import functools

import jax
import jax.numpy as jnp
from jax import lax
from jax.experimental import pallas as pl
from jax.experimental.pallas import tpu as pltpu
from jax.sharding import PartitionSpec as P

F32 = jnp.float32
BF = jnp.bfloat16
MESH = pl.DeviceIdType.MESH
H = 12
HD = 64
SEGS = 3
LOG2E = 1.4426950408889634
SHARP = 0.1
TILES = ((0, 0, 256, 0), (128, 0, 384, 256), (256, 128, 384, 640), (384, 256, 256, 1024))
PW = 1280
LEN = 512


def nn(a, b):
    return lax.dot_general(a, b, (((1,), (0,)), ((), ())), preferred_element_type=F32)


def nt(a, b):
    return lax.dot_general(a, b, (((1,), (1,)), ((), ())), preferred_element_type=F32)


def tn(a, b):
    return lax.dot_general(a, b, (((0,), (0,)), ((), ())), preferred_element_type=F32)


def at(i, n):
    return pl.ds(pl.multiple_of(i * n, n), n)


def rows_at(start, n, unit):
    return pl.ds(pl.multiple_of(start, unit), n)


class Space:
    pass


def norm_stats(v):
    mean = jnp.mean(v, -1, keepdims=True)
    c = v - mean
    inv = lax.rsqrt(jnp.mean(c * c, -1, keepdims=True) + 1e-12)
    return c * inv, inv


class Ring:
    def __init__(self, s, u, g, b, half, places, f, rd, where):
        self.s, self.u, self.g, self.b, self.half = s, u, g, b, half
        self.c_at, self.a_at, self.b_at, self.z_at = places
        self.f, self.rd = f, rd
        dp, psg = where
        self.z, self.x, self.y, self.c = dp // 2, lax.rem(dp, 2), psg // 2, lax.rem(psg, 2)
        self.core = {"psg": self.y * 2 + 1 - self.c}
        self.xn = {"dp": self.z * 2 + 1 - self.x}
        self.yn = {"psg": (1 - self.y) * 2 + self.c}
        self.zn = [{"dp": lax.rem(self.z + k, 4) * 2 + self.x} for k in range(1, 4)]

    def cols(self, c):
        return pl.ds(pl.multiple_of(c * self.half, 128), self.half)

    def part(self, row, n, c):
        return self.g.at[pl.ds(pl.multiple_of(row * self.b, 16), n * self.b), self.cols(c)]

    def remote(self, i, src, dst, dev):
        return pltpu.make_async_remote_copy(
            src_ref=src, dst_ref=dst, send_sem=self.s.gss.at[self.u, i], recv_sem=self.s.grs.at[self.u, i],
            device_id=dev, device_id_type=MESH,
        )

    def copy_c(self, z):
        return self.remote(z, self.part(4 * z, 4, 1 - self.c), self.c_at(z), self.core)

    def copy_a(self, z):
        if z % 2 == 0:
            return [self.remote(4 + z // 2, self.part(4 * z + 2 * (1 - self.x), 2, self.c), self.a_at(z, 0, 2), self.xn)]
        return [
            self.remote(
                6 + z - 1 + x, self.part(4 * z + 2 * x + 1 - self.y, 1, self.c), self.a_at(z, x, 1), self.yn
            )
            for x in range(2)
        ]

    def copy_b(self, z):
        if z % 2 == 0:
            return self.remote(10 + z, self.part(4 * z + 2 * self.x + 1 - self.y, 1, self.c), self.b_at(z), self.yn)
        return self.remote(10 + z, self.part(4 * z + 2 * (1 - self.x) + self.y, 1, self.c), self.b_at(z), self.xn)

    def copy_z(self, k):
        z = lax.rem(self.z + k + 1, 4)
        return self.remote(14 + k, self.part(4 * z + 2 * self.x + self.y, 1, self.c), self.z_at(k), self.zn[k])

    def copy_d(self):
        h = self.b // 2
        src = self.f.at[pl.ds(pl.multiple_of((1 - self.c) * h, 8), h), :]
        return self.remote(17, src, self.rd, self.core)

    def add(self, part, got):
        part[...] = part[...] + got[...]

    def step1(self):
        for z in range(4):
            self.copy_c(z).start()

    def step2(self):
        for z in range(4):
            self.copy_c(z).wait_recv()
            self.add(self.part(4 * z, 4, self.c), self.c_at(z))
            for c in self.copy_a(z):
                c.start()

    def step3(self):
        for z in range(4):
            for c in self.copy_a(z):
                c.wait_recv()
            if z % 2 == 0:
                self.add(self.part(4 * z + 2 * self.x, 2, self.c), self.a_at(z, 0, 2))
            else:
                for x in range(2):
                    self.add(self.part(4 * z + 2 * x + self.y, 1, self.c), self.a_at(z, x, 1))
            self.copy_b(z).start()

    def step4(self):
        for z in range(4):
            self.copy_b(z).wait_recv()
            self.add(self.part(4 * z + 2 * self.x + self.y, 1, self.c), self.b_at(z))
        for k in range(3):
            self.copy_z(k).start()

    def step5(self):
        v = self.part(4 * self.z + 2 * self.x + self.y, 1, self.c)[...].astype(F32)
        for k in range(3):
            self.copy_z(k).wait_recv()
            v = v + self.z_at(k)[...].astype(F32)
        self.f[...] = v
        self.copy_d().start()

    def step6(self, put):
        self.copy_d().wait_recv()
        h = self.b // 2
        put(self.c, self.f[pl.ds(pl.multiple_of(self.c * h, 8), h), :])
        put(1 - self.c, self.rd[...])

    def finish(self):
        for z in range(4):
            self.copy_c(z).wait_send()
            for c in self.copy_a(z):
                c.wait_send()
            self.copy_b(z).wait_send()
        for k in range(3):
            self.copy_z(k).wait_send()
        self.copy_d().wait_send()


def place(ref, f, n, width):
    def ref_at(i, x=0, m=1):
        row, col = f(i)
        return ref.at[row + x * n : row + x * n + m * n, col : col + width]

    return ref_at


def make_rings(s, cfg, where):
    D, FF = cfg.D, cfg.FF
    h, w, b, e = D // 2, FF // 2, D // 16, FF // 16
    low = D
    spots = lambda r, k: (
        place(r, lambda z: (low + 4 * b * (z % 2), (k + z // 2) * h), 4 * b, h),
        place(r, lambda z: (low + 2 * b * z, (k + 2) * h), b, h),
        place(r, lambda z: (low + b * z, (k + 3) * h), b, h),
        place(r, lambda z: (low + b * (4 + z), (k + 3) * h), b, h),
    )
    down = (
        place(s.hid, lambda z: (0, z * h), 4 * e, h),
        place(s.hid, lambda z: (2 * e * (z % 2), (4 + z // 2) * h), e, h),
        place(s.hid, lambda z: (e * z, 6 * h), e, h),
        place(s.hid, lambda z: (e * z, 7 * h), e, h),
    )
    up = (
        place(s.slo, lambda z: (4 * b * z, 0), 4 * b, w),
        place(s.slo, lambda z: (2 * b * z, w), b, w),
        place(s.slo, lambda z: (b * (8 + z), w), b, w),
        place(s.slo, lambda z: (b * (12 + z), w), b, w),
    )
    second = (
        place(s.y1, lambda z: (4 * b * z, 0), 4 * b, h),
        place(s.y1, lambda z: (low + 2 * b * z, 0), b, h),
        place(s.y1, lambda z: (b * z, h), b, h),
        place(s.y1, lambda z: (b * (4 + z), h), b, h),
    )
    third = (
        place(s.y1, lambda z: (b * (7 + 4 * z), h), 4 * b, h),
        place(s.hid, lambda z: (low + 2 * b * z, 4 * h), b, h),
        place(s.hid, lambda z: (low + b * z, 5 * h), b, h),
        place(s.hid, lambda z: (low + b * (4 + z), 5 * h), b, h),
    )
    small = (
        place(s.mrecv, lambda z: (4 * b * z, 0), 4 * b, 128),
        place(s.mrecv, lambda z: (b * (16 + 2 * z), 0), b, 128),
        place(s.mrecv, lambda z: (b * (24 + z), 0), b, 128),
        place(s.mrecv, lambda z: (b * (28 + z), 0), b, 128),
    )
    mk = lambda u, g, bb, half, places, f, rd: Ring(s, u, g, bb, half, places, f, rd, where)
    return (
        mk(0, s.wdn, e, h, down, s.fd, s.rd),
        mk(1, s.wup, b, w, up, s.fu, s.ru),
        mk(2, s.wout, b, h, spots(s.hid, 0), s.fq.at[0], s.rq.at[0]),
        mk(3, s.ctx, b, h, spots(s.slo, 0), s.fq.at[1], s.rq.at[1]),
        mk(4, s.fb, b, h, second, s.fq.at[2], s.rq.at[2]),
        mk(5, s.gb, b, h, third, s.fq.at[3], s.rq.at[3]),
        mk(6, s.misc, b, 128, small, s.fm, s.rm),
    )


def kernel(cfg, *refs):
    s = Space()
    for name, ref in zip(cfg.names, refs):
        setattr(s, name, ref)
    T, NP, NQ, TT = cfg.T, cfg.NP, cfg.NQ, cfg.TT
    D, FF = cfg.D, cfg.FF
    nrow = NP // LEN
    me_dp = lax.axis_index("dp")
    me_psg = lax.axis_index("psg")
    n_psg, n_dp = cfg.n_psg, cfg.n_dp

    def load(k, src, dst):
        c = pltpu.make_async_copy(src, dst, s.lsem.at[k])
        c.start()
        return c

    l_x = load(0, s.i_pass, s.x.at[0:NP])
    l_q = load(1, s.i_query, s.x.at[NP:T])
    l_wqkv = load(2, s.i_wqkv, s.wqkv)
    l_wout = load(3, s.i_wout, s.wout)
    l_wup = load(4, s.i_wup, s.wup)
    l_wdn = load(5, s.i_wdn, s.wdn)
    l_wpj = load(6, s.i_wproj, s.wproj)

    bar = pltpu.get_barrier_semaphore()
    peers = []
    for k in range(1, n_psg):
        peers.append({"psg": lax.rem(me_psg + k, n_psg)})
    if cfg.loss_here:
        for k in range(1, n_dp):
            peers.append({"dp": lax.rem(me_dp + k, n_dp)})
    for p in peers:
        pl.semaphore_signal(bar, inc=1, device_id=p, device_id_type=MESH)

    sums = cfg.sums
    if sums:
        ring_d, ring_u, ring_o, ring_1, ring_2, ring_3, ring_m = rings = make_rings(s, cfg, (me_dp, me_psg))

        def epoch_signal(k):
            for dev in [ring_d.core, ring_d.xn, ring_d.yn] + ring_d.zn:
                pl.semaphore_signal(s.epoch.at[k], inc=1, device_id=dev, device_id_type=MESH)

        def epoch_wait(k):
            pl.semaphore_wait(s.epoch.at[k], 6)

    def put_in(ref):
        def put(c, v):
            ref[:, pl.ds(pl.multiple_of(c * v.shape[1], 128), v.shape[1])] = v

        return put

    def put_group(g):
        def put(c, v):
            for i in range(v.shape[1] // 128):
                k = c * (v.shape[1] // 128) + i
                col = (k // 2) * D + g * 256 + lax.rem(k, 2) * 128
                s.o_qkv[:, pl.ds(pl.multiple_of(col, 128), 128)] = v[:, i * 128 : i * 128 + 128]

        return put

    lane = lax.broadcasted_iota(jnp.int32, (128, 128), 1)
    low_half = lane < 64
    zero_b = jnp.zeros((), BF)

    def halves(a):
        keep = lax.broadcasted_iota(jnp.int32, a.shape, 1) < 64
        return jnp.where(keep, a, zero_b), jnp.where(keep, zero_b, a)

    bounds = []
    for r in range(nrow):
        seg = s.i_seg[r : r + 1, :]
        bounds.append(
            (
                jnp.sum(jnp.where(seg < 1, 1.0, 0.0), axis=1, keepdims=True),
                jnp.sum(jnp.where(seg < 2, 1.0, 0.0), axis=1, keepdims=True),
            )
        )

    s.bqkv[...] = jnp.zeros_like(s.bqkv)
    s.bqkv[0:1, 0:D] = s.i_bq[...]
    s.bqkv[0:1, 2 * D : 3 * D] = s.i_bv[...]
    l_x.wait()
    l_q.wait()
    l_wqkv.wait()

    def qkv_body(n, _):
        c = at(n, 256)
        s.mixed[:, c] = (nn(s.x[...], s.wqkv[:, c]) + s.bqkv[0:1, c]).astype(BF)
        return 0

    lax.fori_loop(0, 3 * D // 256, qkv_body, 0)

    scale = 0.125 * LOG2E

    def p_copy_out(i, slot):
        return pltpu.make_async_copy(s.pbuf.at[slot], s.o_p.at[i], s.psem.at[slot])

    for r in range(nrow):
        b0, b1 = bounds[r]
        for qs, ks, kw, off in TILES:
            qi = (lax.broadcasted_iota(jnp.int32, (128, kw), 0) + qs).astype(F32)
            ki = (lax.broadcasted_iota(jnp.int32, (128, kw), 1) + ks).astype(F32)
            sq = jnp.where(qi >= b0, 1.0, 0.0) + jnp.where(qi >= b1, 1.0, 0.0)
            sk = jnp.where(ki >= b0, 1.0, 0.0) + jnp.where(ki >= b1, 1.0, 0.0)
            s.bias[:, off : off + kw] = jnp.where(sq == sk, 0.0, -1e30)

        def att_body(hp, _, r=r):
            i = r * (H // 2) + hp
            slot = lax.rem(i, 2)

            @pl.when(i >= 2)
            def _():
                p_copy_out(i - 2, slot).wait()

            cq, ck, cv = at(hp, 128), at(hp + D // 128, 128), at(hp + 2 * D // 128, 128)
            for qs, ks, kw, off in TILES:
                qh = halves(s.mixed[r * LEN + qs : r * LEN + qs + 128, cq])
                kt = s.mixed[r * LEN + ks : r * LEN + ks + kw, ck]
                vt = s.mixed[r * LEN + ks : r * LEN + ks + kw, cv]
                o = []
                for h in range(2):
                    sc = nt(qh[h], kt) * scale + s.bias[:, off : off + kw]
                    e = jnp.exp2(sc - jnp.max(sc, -1, keepdims=True))
                    p = (e * (1.0 / jnp.sum(e, -1, keepdims=True))).astype(BF)
                    s.pbuf[slot, h, :, off : off + kw] = p
                    o.append(nn(p, vt))
                s.ctx[r * LEN + qs : r * LEN + qs + 128, cq] = jnp.where(low_half, o[0], o[1]).astype(BF)
            p_copy_out(i, slot).start()
            return 0

        lax.fori_loop(0, H // 2, att_body, 0)

    qi = lax.broadcasted_iota(jnp.int32, (NQ, NQ), 0)
    ki = lax.broadcasted_iota(jnp.int32, (NQ, NQ), 1)
    ql = cfg.qlen
    qbias = jnp.where((qi // ql) == (ki // ql), 0.0, -1e30)
    for hp in range(H // 2):
        cq = slice(hp * 128, hp * 128 + 128)
        qh = halves(s.mixed[NP:T, hp * 128 : hp * 128 + 128])
        kt = s.mixed[NP:T, D + hp * 128 : D + hp * 128 + 128]
        vt = s.mixed[NP:T, 2 * D + hp * 128 : 2 * D + hp * 128 + 128]
        o = []
        for h in range(2):
            sc = nt(qh[h], kt) * scale + qbias
            e = jnp.exp2(sc - jnp.max(sc, -1, keepdims=True))
            p = (e * (1.0 / jnp.sum(e, -1, keepdims=True))).astype(BF)
            s.pq[hp, h] = p
            o.append(nn(p, vt))
        s.ctx[NP:T, cq] = jnp.where(low_half, o[0], o[1]).astype(BF)
    last = nrow * (H // 2)
    p_copy_out(last - 2, (last - 2) % 2).wait()
    p_copy_out(last - 1, (last - 1) % 2).wait()

    l_wout.wait()

    def out_body(t, _):
        rr = at(t, TT)
        v = nn(s.ctx[rr, :], s.wout[...]) + s.i_bout[...] + s.x[rr, :].astype(F32)
        y, inv = norm_stats(v)
        s.y1[rr, :] = y.astype(BF)
        s.st[rr, 0:1] = inv
        s.fb[rr, :] = (y * s.i_g1[...] + s.i_b1[...]).astype(BF)
        return 0

    lax.fori_loop(0, T // TT, out_body, 0)

    l_wup.wait()

    def up_body(n, _):
        c = at(n, 256)
        for m in range(T // TT):
            rr = slice(m * TT, m * TT + TT)
            h = nn(s.fb[rr, :], s.wup[:, c]) + s.i_bup[:, c]
            cdf = 0.5 * (1.0 + lax.erf(h * 0.7071067811865476))
            s.hid[rr, c] = (h * cdf).astype(BF)
            s.slo[rr, c] = (cdf + h * jnp.exp2(h * h * (-0.5 * LOG2E)) * 0.3989422804014327).astype(BF)
        return 0

    lax.fori_loop(0, FF // 256, up_body, 0)

    l_wdn.wait()
    l_wpj.wait()

    def down_body(t, _):
        rr = at(t, TT)
        first = s.y1[rr, :].astype(F32) * s.i_g1[...] + s.i_b1[...]
        v = first + (nn(s.hid[rr, :], s.wdn[...]) + s.i_bdn[...])
        y, inv = norm_stats(v)
        s.gs[rr, :] = y
        s.st[rr, 1:2] = inv
        sec = (y * s.i_g2[...] + s.i_b2[...]).astype(BF)
        s.gb[rr, :] = sec
        pj = nn(sec, s.wproj[...])
        il = lax.rsqrt(jnp.sum(pj * pj, -1, keepdims=True) + 1e-06)
        s.st[rr, 2:3] = il
        u = pj * il
        s.unit[rr, :] = u
        s.unitb[rr, :] = u.astype(BF)
        return 0

    lax.fori_loop(0, T // TT, down_body, 0)

    o_pe = pltpu.make_async_copy(s.unitb.at[0:NP], s.o_pe, s.osem.at[0])
    o_pe.start()
    o_qe = pltpu.make_async_copy(s.unitb.at[NP:T], s.o_qe, s.osem.at[1])
    o_qe.start()

    pl.semaphore_wait(bar, len(peers))
    sends = []

    def remote(src, dst, ssem, rsem, dev):
        c = pltpu.make_async_remote_copy(
            src_ref=src, dst_ref=dst, send_sem=ssem, recv_sem=rsem, device_id=dev, device_id_type=MESH
        )
        return c

    q_copies = []
    for k in range(1, n_psg):
        c = remote(
            s.unitb.at[NP:T], s.aq.at[k], s.ss.at[0, k], s.rs.at[0, k], {"psg": lax.rem(me_psg + k, n_psg)}
        )
        c.start()
        q_copies.append(c)
    s.aq[0] = s.unitb[NP:T, :]

    for r in range(nrow):
        b0, b1 = bounds[r]
        ti = lax.broadcasted_iota(jnp.int32, (LEN, 128), 0).astype(F32)
        li = lax.broadcasted_iota(jnp.int32, (LEN, 128), 1).astype(F32)
        pid = SEGS * r + jnp.where(ti >= b0, 1.0, 0.0) + jnp.where(ti >= b1, 1.0, 0.0)
        s.ind[r * LEN : (r + 1) * LEN, :] = jnp.where(pid == li, 1.0, 0.0).astype(BF)
    count = jnp.sum(s.ind[...].astype(F32), axis=0, keepdims=True)
    slots = nrow * SEGS
    valid = lax.broadcasted_iota(jnp.int32, (1, 128), 1) < slots
    count = jnp.where(valid, count, 1.0)
    nqg = NQ // ql
    s.lg[0] = jnp.zeros(s.lg.shape[1:], F32)

    def powers(k):
        sim = nt(s.aq[k], s.unitb[0:NP, :])
        return jnp.exp2((sim - 1.0) * (LOG2E / SHARP))

    for k in range(n_psg):
        if k:
            q_copies[k - 1].wait_recv()
        pw = powers(k)
        hi = pw.astype(BF)
        lo = (pw - hi.astype(F32)).astype(BF)
        tot = nn(hi, s.ind[...]) + nn(lo, s.ind[...])
        tot = jnp.where(valid, tot, 1.0)
        s.tot[k] = tot
        line = jnp.log(tot / count) + 1.0 / SHARP
        line = jnp.where(valid, line, 0.0)
        src = lax.rem(me_psg + n_psg - k, n_psg)
        s.line[rows_at(src * NQ, NQ, NQ), :] = line

    nq_all = n_psg * nqg
    qrow = lax.broadcasted_iota(jnp.int32, (nq_all, n_psg * NQ), 0) * ql
    qcol = lax.broadcasted_iota(jnp.int32, (nq_all, n_psg * NQ), 1)
    sel = jnp.where(jnp.logical_and(qcol >= qrow, qcol < qrow + ql), 1.0, 0.0).astype(BF)
    line = s.line[...]
    hi = line.astype(BF)
    line = line - hi.astype(F32)
    mid = line.astype(BF)
    lo = (line - mid.astype(F32)).astype(BF)
    s.lg[0, 0:nq_all, :] = nn(sel, hi) + (nn(sel, mid) + nn(sel, lo))
    s.lg[0, nq_all : 2 * nq_all, 0:slots] = s.i_teach[...]
    l_copies = []
    for k in range(1, n_psg):
        c = remote(
            s.lg.at[0], s.lg.at[k], s.ss.at[1, k], s.rs.at[1, k], {"psg": lax.rem(me_psg + k, n_psg)}
        )
        c.start()
        l_copies.append(c)
    for c in l_copies:
        c.wait_recv()
    ok = valid[None]
    lg = s.lg[...]
    half = nq_all

    def log_norm(v):
        vm = jnp.where(valid[None], v, -1e30)
        top = jnp.max(jnp.max(vm, axis=-1, keepdims=True), axis=0, keepdims=True)
        sh = v - top
        ex = jnp.where(valid[None], jnp.exp(sh), 0.0)
        tot = jnp.sum(jnp.sum(ex, axis=-1, keepdims=True), axis=0, keepdims=True)
        return sh - jnp.log(tot)

    stu = log_norm(lg[:, 0:half, :])
    tea = log_norm(lg[:, half : 2 * half, :])
    pt = jnp.exp(tea)
    kl = jnp.where(ok, pt * (tea - stu), 0.0)
    group_sum = jnp.sum(jnp.sum(jnp.sum(kl, axis=0), axis=-1, keepdims=True), axis=0, keepdims=True)
    s.ls[0] = jnp.broadcast_to(group_sum / n_dp, (8, 128))
    loss_copies = []
    if cfg.loss_here:
        for k in range(1, n_dp):
            c = remote(
                s.ls.at[0], s.ls.at[k], s.lss.at[k], s.lrs.at[k], {"dp": lax.rem(me_dp + k, n_dp)}
            )
            c.start()
            loss_copies.append(c)
    s.gl[...] = jnp.where(valid, (jnp.exp(stu[0]) - pt[0]) / n_dp, 0.0)
    for q in range(nq_all):
        s.line[q * ql : q * ql + ql, :] = jnp.broadcast_to(s.gl[q : q + 1, :], (ql, 128))

    g_copies = []
    for k in list(range(1, n_psg)) + [0]:
        pw = powers(k)
        src = lax.rem(me_psg + n_psg - k, n_psg)
        ratio = s.line[rows_at(src * NQ, NQ, NQ), :] / s.tot[k]
        ratio = ratio * (1.0 / SHARP)
        hi = ratio.astype(BF)
        lo = (ratio - hi.astype(F32)).astype(BF)
        g = ((nt(hi, s.ind[...]) + nt(lo, s.ind[...])) * pw).astype(BF)
        s.gsim[k * NQ : (k + 1) * NQ, :] = g
        qp = nn(g, s.unitb[0:NP, :])
        if k:
            s.qs[k] = qp.astype(BF)
            c = remote(s.qs.at[k], s.qr.at[k], s.ss.at[2, k], s.rs.at[2, k], {"psg": src})
            c.start()
            g_copies.append(c)
        else:
            s.own[...] = qp

    def unit_back(gu, rr):
        u = s.unit[rr, :]
        return (s.st[rr, 2:3] * (gu - u * jnp.sum(gu * u, -1, keepdims=True))).astype(BF)

    aq = s.aq[...].reshape(n_psg * NQ, 128)
    for m in range(NP // 256):
        rr = slice(m * 256, m * 256 + 256)
        gu = tn(s.gsim[:, rr], aq)
        s.gp[rr, :] = unit_back(gu, rr)
    for c in g_copies:
        c.wait_recv()
    gu = s.own[...]
    for k in range(1, n_psg):
        gu = gu + s.qr[k].astype(F32)
    s.gp[NP:T, :] = unit_back(gu, slice(NP, T))

    s.misc[:, 0:128] = tn(s.gb[...], s.gp[...]).astype(BF)

    s.vr[...] = jnp.zeros_like(s.vr)

    def addrow(k, v):
        s.vr[k : k + 1, :] = s.vr[k : k + 1, :] + jnp.sum(v, axis=0, keepdims=True)

    def norm2_body(t, _):
        rr = at(t, TT)
        g = nt(s.gp[rr, :], s.wproj[...])
        y = s.gs[rr, :]
        addrow(6, g * y)
        addrow(7, g)
        d = g * s.i_g2[...]
        gs = s.st[rr, 1:2] * (d - jnp.mean(d, -1, keepdims=True) - y * jnp.mean(d * y, -1, keepdims=True))
        s.gs[rr, :] = gs
        b = gs.astype(BF)
        s.gb[rr, :] = b
        addrow(5, b.astype(F32))
        return 0

    lax.fori_loop(0, T // TT, norm2_body, 0)

    def ff_body(n, _):
        c = at(n, 256)
        w = s.wdn[c, :]
        tot = jnp.zeros((1, 256), F32)
        for m in range(T // TT):
            rr = slice(m * TT, m * TT + TT)
            g = (nt(s.gb[rr, :], w) * s.slo[rr, c].astype(F32)).astype(BF)
            s.slo[rr, c] = g
            tot = tot + jnp.sum(g.astype(F32), axis=0, keepdims=True)
        s.bup[0:1, c] = tot
        s.wdn[c, :] = tn(s.hid[:, c], s.gb[...]).astype(BF)
        return 0

    lax.fori_loop(0, FF // 256, ff_body, 0)

    if sums:
        epoch_signal(0)

    def norm1_body(t, _):
        rr = at(t, TT)
        g = s.gs[rr, :] + nt(s.slo[rr, :], s.wup[...])
        y = s.y1[rr, :].astype(F32)
        addrow(3, g * y)
        addrow(4, g)
        d = g * s.i_g1[...]
        gs = s.st[rr, 0:1] * (d - jnp.mean(d, -1, keepdims=True) - y * jnp.mean(d * y, -1, keepdims=True))
        s.gs[rr, :] = gs
        b = gs.astype(BF)
        s.gb[rr, :] = b
        addrow(2, b.astype(F32))
        return 0

    lax.fori_loop(0, T // TT, norm1_body, 0)

    def gup_body(n, _):
        c = at(n, 256)
        s.wup[:, c] = tn(s.fb[...], s.slo[:, c]).astype(BF)
        return 0

    if sums:
        epoch_wait(0)
        ring_d.step1()
    lax.fori_loop(0, FF // 512, gup_body, 0)
    if sums:
        ring_d.step2()
    lax.fori_loop(FF // 512, FF // 256, gup_body, 0)
    if sums:
        epoch_signal(1)
        ring_d.step3()

    def dctx_body(t, _):
        rr = at(t, TT)
        s.dctx[rr, :] = nt(s.gb[rr, :], s.wout[...]).astype(BF)
        return 0

    lax.fori_loop(0, T // TT, dctx_body, 0)
    if sums:
        ring_d.step4()
        epoch_wait(1)
        ring_u.step1()
    s.wout[...] = tn(s.ctx[...], s.gb[...]).astype(BF)
    if sums:
        ring_o.step1()
        ring_d.step5()

    def p_copy_in(j):
        g, rest = j // (2 * nrow), lax.rem(j, 2 * nrow)
        i = (rest // 2) * (H // 2) + 2 * g + lax.rem(rest, 2)
        slot = lax.rem(j, 2)
        return pltpu.make_async_copy(s.o_p.at[i], s.pbuf.at[slot], s.psem.at[slot])

    steps = nrow * (H // 2)
    p_copy_in(0).start()

    def att_back(j, _):
        g, rest = j // (2 * nrow), lax.rem(j, 2 * nrow)
        r = rest // 2
        hp = 2 * g + lax.rem(rest, 2)
        slot = lax.rem(j, 2)

        @pl.when(j + 1 < steps)
        def _():
            p_copy_in(j + 1).start()

        p_copy_in(j).wait()
        cq, ck, cv = at(hp, 128), at(hp + D // 128, 128), at(hp + 2 * D // 128, 128)
        base = r * LEN

        def rws(a, n):
            return pl.ds(pl.multiple_of(base + a, 128), n)

        for qs, ks, kw, off in TILES:
            do = halves(s.dctx[rws(qs, 128), cq])
            kt = s.mixed[rws(ks, kw), ck]
            vt = s.mixed[rws(ks, kw), cv]
            dq = []
            for h in range(2):
                p = s.pbuf[slot, h, :, off : off + kw].astype(F32)
                dp = nt(do[h], vt)
                pd = p * dp
                ds = (pd - p * jnp.sum(pd, -1, keepdims=True)).astype(BF)
                s.ds[h, :, off : off + kw] = ds
                dq.append(nn(ds, kt))
            s.dq[qs : qs + 128, :] = (jnp.where(low_half, dq[0], dq[1]) * 0.125).astype(BF)
        for kk in range(4):
            dk = [None, None]
            dv = [None, None]
            for h in range(2):
                for qs, ks, kw, off in TILES:
                    rel = kk * 128 - ks
                    if rel < 0 or rel >= kw:
                        continue
                    qt = s.mixed[rws(qs, 128), cq]
                    ot = s.dctx[rws(qs, 128), cq]
                    a = tn(s.ds[h, :, off + rel : off + rel + 128], qt)
                    b = tn(s.pbuf[slot, h, :, off + rel : off + rel + 128], ot)
                    dk[h] = a if dk[h] is None else dk[h] + a
                    dv[h] = b if dv[h] is None else dv[h] + b
            s.dk[kk * 128 : kk * 128 + 128, :] = (jnp.where(low_half, dk[0], dk[1]) * 0.125).astype(BF)
            s.dv[kk * 128 : kk * 128 + 128, :] = jnp.where(low_half, dv[0], dv[1]).astype(BF)
        s.mixed[rws(0, LEN), cq] = s.dq[...]
        s.mixed[rws(0, LEN), ck] = s.dk[...]
        s.mixed[rws(0, LEN), cv] = s.dv[...]
        return 0

    def att_back_q(hp, _):
        cq, ck, cv = at(hp, 128), at(hp + D // 128, 128), at(hp + 2 * D // 128, 128)
        qt = s.mixed[NP:T, cq]
        kt = s.mixed[NP:T, ck]
        vt = s.mixed[NP:T, cv]
        ot = s.dctx[NP:T, cq]
        do = halves(ot)
        dq, dk, dv = [], [], []
        for h in range(2):
            pb = s.pq[hp, h]
            p = pb.astype(F32)
            pd = p * nt(do[h], vt)
            ds = (pd - p * jnp.sum(pd, -1, keepdims=True)).astype(BF)
            dq.append(nn(ds, kt))
            dk.append(tn(ds, qt))
            dv.append(tn(pb, ot))
        s.mixed[NP:T, cq] = (jnp.where(low_half, dq[0], dq[1]) * 0.125).astype(BF)
        s.mixed[NP:T, ck] = (jnp.where(low_half, dk[0], dk[1]) * 0.125).astype(BF)
        s.mixed[NP:T, cv] = jnp.where(low_half, dv[0], dv[1]).astype(BF)
        return 0

    lax.fori_loop(0, H // 2, att_back_q, 0)

    groups = (s.ctx, s.fb, s.gb)

    def group_grad(g):
        for w in range(3):
            c = w * D + g * 256
            groups[g][0:D, w * 256 : w * 256 + 256] = tn(s.x[...], s.mixed[:, c : c + 256]).astype(BF)

    def step(j, _):
        att_back(j, 0)
        if sums:

            @pl.when(j == 1)
            def _():
                ring_u.step2()
                ring_o.step2()

            @pl.when(j == 2)
            def _():
                ring_d.step6(put_in(s.o_dn))

        @pl.when(j == 3)
        def _():
            group_grad(0)
            if sums:
                ring_1.step1()

        if sums:

            @pl.when(j == 5)
            def _():
                ring_u.step3()
                ring_o.step3()
                ring_1.step2()

        @pl.when(j == 7)
        def _():
            group_grad(1)
            if sums:
                ring_2.step1()
                ring_u.step4()
                ring_o.step4()
                ring_1.step3()

        if sums:

            @pl.when(j == 9)
            def _():
                ring_u.step5()
                ring_o.step5()
                ring_1.step4()
                ring_2.step2()

        return 0

    lax.fori_loop(0, steps, step, 0)
    group_grad(2)
    if sums:
        ring_3.step1()
    for w, k in ((0, 0), (2, 1)):
        s.vr[k : k + 1, :] = jnp.sum(s.mixed[:, w * D : w * D + D].astype(F32), axis=0, keepdims=True)

    if sums:
        pad = jnp.zeros((120, 128), F32)
        for i in range(D // 128):
            v = s.vr[:, i * 128 : i * 128 + 128]
            s.vcol[i * 128 : i * 128 + 128, :] = jnp.concatenate([v, pad], 0).T
        q = D // 32
        lane = lax.broadcasted_iota(jnp.int32, (q, 128), 1)
        for i in range(FF // 384):
            for k in range(3):
                v = s.bup[0:1, i * 384 + k * 128 : i * 384 + k * 128 + 128]
                s.tcol[k * 128 : k * 128 + 128, :] = jnp.broadcast_to(v, (128, 128)).T
            for d in range(4):
                rr = slice((4 * i + d) * q, (4 * i + d) * q + q)
                v = s.vcol[rr, :]
                for k in range(4):
                    v = jnp.where(lane == 8 + k, s.tcol[(4 * d + k) * q : (4 * d + k) * q + q, :], v)
                s.vcol[rr, :] = v
        s.misc[:, 128:256] = s.vcol[...].astype(BF)
        ring_m.step1()
        ring_u.step6(put_in(s.o_up))
        ring_o.step6(put_in(s.o_out))
        ring_1.step5()
        ring_2.step3()

    def dx_body(t, _):
        rr = at(t, TT)
        s.gs[rr, :] = s.gs[rr, :] + nt(s.mixed[rr, :], s.wqkv[...])
        return 0

    lax.fori_loop(0, T // TT // 2, dx_body, 0)
    if sums:
        ring_3.step2()
        ring_m.step2()
        ring_2.step4()
        ring_1.step6(put_group(0))
    lax.fori_loop(T // TT // 2, T // TT, dx_body, 0)
    outs = [
        pltpu.make_async_copy(s.gs.at[0:NP], s.o_gp, s.osem.at[2]),
        pltpu.make_async_copy(s.gs.at[NP:T], s.o_gq, s.osem.at[3]),
    ]
    if not sums:
        outs += [
            pltpu.make_async_copy(s.wdn, s.o_dn, s.osem.at[4]),
            pltpu.make_async_copy(s.wup, s.o_up, s.osem.at[5]),
            pltpu.make_async_copy(s.wout, s.o_out, s.osem.at[6]),
            pltpu.make_async_copy(s.ctx.at[0:D], s.o_q.at[0], s.osem.at[7]),
            pltpu.make_async_copy(s.fb.at[0:D], s.o_q.at[1], s.osem.at[8]),
            pltpu.make_async_copy(s.gb.at[0:D], s.o_q.at[2], s.osem.at[9]),
            pltpu.make_async_copy(s.misc, s.o_misc, s.osem.at[10]),
        ]
        s.o_bup[...] = s.bup[0:1, :]
        s.o_vr[...] = s.vr[...]
    for c in outs:
        c.start()
    if sums:
        ring_3.step3()
        ring_m.step3()
        ring_2.step5()
        ring_3.step4()
        ring_m.step4()
        ring_2.step6(put_group(1))
        ring_3.step5()
        ring_m.step5()
        ring_3.step6(put_group(2))
        ring_m.step6(put_in(s.o_misc))
        for r in rings:
            r.finish()
    for c in q_copies + l_copies + g_copies + loss_copies:
        c.wait_send()
    for c in loss_copies:
        c.wait_recv()
    if cfg.loss_here:
        s.o_loss[...] = jnp.sum(s.ls[...], axis=0)
    else:
        s.o_loss[...] = s.ls[0]
    for c in [o_pe, o_qe] + outs:
        c.wait()


def make_body(n_dp, n_psg):
    def body(
        passage_states, segment_ids, query_states, teacher_scores,
        w_qkv, bias_q, bias_v, w_out, bias_out, ln1_gain, ln1_bias,
        w_up, bias_up, w_down, bias_down, ln2_gain, ln2_bias, w_proj,
    ):
        D, FF = w_up.shape
        E = w_proj.shape[1]
        rows, length, _ = passage_states.shape
        qn, ql, _ = query_states.shape
        NP, NQ = rows * length, qn * ql
        T = NP + NQ
        cfg = Space()
        cfg.T, cfg.NP, cfg.NQ, cfg.TT = T, NP, NQ, T // 4
        cfg.D, cfg.FF, cfg.qlen = D, FF, ql
        cfg.n_dp, cfg.n_psg = n_dp, n_psg
        cfg.loss_here = n_dp <= 16
        cfg.sums = n_dp == 8 and n_psg == 4
        npair = rows * (H // 2)
        any_spec = pl.BlockSpec(memory_space=pl.ANY)
        vm = pl.BlockSpec(memory_space=pltpu.VMEM)
        row = lambda v: v.reshape(1, -1)
        ins = [
            ("i_pass", passage_states.reshape(NP, D), any_spec),
            ("i_query", query_states.reshape(NQ, D), any_spec),
            ("i_seg", segment_ids, vm),
            ("i_teach", teacher_scores, vm),
            ("i_wqkv", w_qkv, any_spec),
            ("i_bq", row(bias_q), vm),
            ("i_bv", row(bias_v), vm),
            ("i_wout", w_out, any_spec),
            ("i_bout", row(bias_out), vm),
            ("i_g1", row(ln1_gain), vm),
            ("i_b1", row(ln1_bias), vm),
            ("i_wup", w_up, any_spec),
            ("i_bup", row(bias_up), vm),
            ("i_wdn", w_down, any_spec),
            ("i_bdn", row(bias_down), vm),
            ("i_g2", row(ln2_gain), vm),
            ("i_b2", row(ln2_bias), vm),
            ("i_wproj", w_proj, any_spec),
        ]
        sd = jax.ShapeDtypeStruct
        outs = [
            ("o_pe", sd((NP, E), BF), any_spec),
            ("o_qe", sd((NQ, E), BF), any_spec),
            ("o_loss", sd((8, 128), F32), vm),
            ("o_gp", sd((NP, D), F32), any_spec),
            ("o_gq", sd((NQ, D), F32), any_spec),
            ("o_p", sd((npair, 2, 128, PW), BF), any_spec),
        ]
        n_dev = n_dp * n_psg
        if cfg.sums:
            outs += [
                ("o_dn", sd((FF // n_dev, D), F32), vm),
                ("o_up", sd((D // n_dev, FF), F32), vm),
                ("o_out", sd((D // n_dev, D), F32), vm),
                ("o_qkv", sd((D // n_dev, 3 * D), F32), vm),
                ("o_misc", sd((D // n_dev, 256), F32), vm),
            ]
        else:
            outs += [
                ("o_dn", sd((FF, D), BF), any_spec),
                ("o_up", sd((D, FF), BF), any_spec),
                ("o_out", sd((D, D), BF), any_spec),
                ("o_q", sd((3, D, D), BF), any_spec),
                ("o_misc", sd((D, 256), BF), any_spec),
                ("o_bup", sd((1, FF), F32), vm),
                ("o_vr", sd((8, D), F32), vm),
            ]
        V = pltpu.VMEM
        DMA = pltpu.SemaphoreType.DMA
        scratch = [
            ("x", V((T, D), BF)),
            ("wqkv", V((D, 3 * D), BF)),
            ("wout", V((D, D), BF)),
            ("wup", V((D, FF), BF)),
            ("wdn", V((FF, D), BF)),
            ("wproj", V((D, E), BF)),
            ("bqkv", V((8, 3 * D), F32)),
            ("mixed", V((T, 3 * D), BF)),
            ("pbuf", V((2, 2, 128, PW), BF)),
            ("pq", V((H // 2, 2, NQ, NQ), BF)),
            ("bias", V((128, PW), F32)),
            ("ctx", V((T, D), BF)),
            ("y1", V((T, D), BF)),
            ("fb", V((T, D), BF)),
            ("hid", V((T, FF), BF)),
            ("slo", V((T, FF), BF)),
            ("gs", V((T, D), F32)),
            ("gb", V((T, D), BF)),
            ("st", V((T, 128), F32)),
            ("unit", V((T, E), F32)),
            ("unitb", V((T, E), BF)),
            ("aq", V((n_psg, NQ, E), BF)),
            ("ind", V((NP, 128), BF)),
            ("tot", V((n_psg, NQ, 128), F32)),
            ("lg", V((n_psg, 2 * n_psg * qn, 128), F32)),
            ("line", V((n_psg * NQ, 128), F32)),
            ("gl", V((n_psg * qn, 128), F32)),
            ("ls", V((n_dp if cfg.loss_here else 1, 8, 128), F32)),
            ("gsim", V((n_psg * NQ, NP), BF)),
            ("qs", V((n_psg, NQ, E), BF)),
            ("qr", V((n_psg, NQ, E), BF)),
            ("own", V((NQ, E), F32)),
            ("gp", V((T, E), BF)),
            ("misc", V((D, 256), BF)),
            ("vr", V((8, D), F32)),
            ("vcol", V((D, 128), F32)),
            ("bup", V((8, FF), F32)),
            ("dctx", V((T, D), BF)),
            ("ds", V((2, 128, PW), BF)),
            ("dq", V((LEN, 128), BF)),
            ("dk", V((LEN, 128), BF)),
            ("dv", V((LEN, 128), BF)),
            ("lsem", DMA((7,))),
            ("psem", DMA((2,))),
            ("osem", DMA((11,))),
            ("ss", DMA((3, n_psg))),
            ("rs", DMA((3, n_psg))),
            ("lss", DMA((n_dp,))),
            ("lrs", DMA((n_dp,))),
        ]
        if cfg.sums:
            b, e = D // 16, FF // 16
            scratch += [
                ("tcol", V((384, 128), F32)),
                ("mrecv", V((31 * b, 128), BF)),
                ("fd", V((e, D // 2), F32)),
                ("rd", V((e // 2, D // 2), F32)),
                ("fu", V((b, FF // 2), F32)),
                ("ru", V((b // 2, FF // 2), F32)),
                ("fq", V((4, b, D // 2), F32)),
                ("rq", V((4, b // 2, D // 2), F32)),
                ("fm", V((b, 128), F32)),
                ("rm", V((b // 2, 128), F32)),
                ("gss", DMA((7, 18))),
                ("grs", DMA((7, 18))),
                ("epoch", pltpu.SemaphoreType.REGULAR((2,))),
            ]
        cfg.names = [a for a, *_ in ins] + [a for a, *_ in outs] + [a for a, _ in scratch]
        res = pl.pallas_call(
            functools.partial(kernel, cfg),
            out_shape=[o[1] for o in outs],
            in_specs=[i[2] for i in ins],
            out_specs=[o[2] for o in outs],
            scratch_shapes=[v for _, v in scratch],
            compiler_params=pltpu.CompilerParams(
                collective_id=0, has_side_effects=True, vmem_limit_bytes=64 * 1024 * 1024 - 65536
            ),
        )(*[i[1] for i in ins])
        o = dict(zip([a for a, *_ in outs], res))
        loss = o["o_loss"][0, 0]
        if not cfg.loss_here:
            loss = lax.psum(loss, "dp")
        head = (
            o["o_pe"].reshape(rows, length, E),
            o["o_qe"].reshape(qn, ql, E),
            loss,
            o["o_gp"].reshape(rows, length, D),
            o["o_gq"].reshape(qn, ql, D),
        )
        if cfg.sums:
            m = o["o_misc"]
            vec = [m[:, 128 + k] for k in range(8)]
            g_bup = m[:, 136:140].T.reshape(-1)
            g_qkv, g_out, g_up, g_dn, g_proj = o["o_qkv"], o["o_out"], o["o_up"], o["o_dn"], m[:, 0:128]
        else:
            q3 = o["o_q"].reshape(3, D, 3, 256)
            q3 = jnp.transpose(q3, (1, 2, 0, 3)).reshape(D, 3 * D)

            def scat(v):
                return lax.psum_scatter(v, ("dp", "psg"), scatter_dimension=0, tiled=True)

            vec = scat(o["o_vr"].T)
            vec = [vec[:, k] for k in range(8)]
            g_bup = scat(o["o_bup"].reshape(-1))
            g_qkv, g_out, g_up, g_dn, g_proj = [
                scat(v.astype(F32)) for v in (q3, o["o_out"], o["o_up"], o["o_dn"], o["o_misc"][:, 0:128])
            ]
        return head + (
            g_qkv, vec[0], vec[1], g_out, vec[2], vec[3], vec[4],
            g_up, g_bup, g_dn, vec[5], vec[6], vec[7], g_proj,
        )

    return body


def solution(mesh):
    rowspec = P(("dp", "psg"))
    three = P(("dp", "psg"), None, None)
    two = P(("dp", "psg"), None)
    in_specs = (three, two, three, P("dp", "psg")) + (P(),) * 14
    out_specs = (
        three, three, P(), three, three,
        two, rowspec, rowspec, two, rowspec, rowspec, rowspec,
        two, rowspec, two, rowspec, rowspec, rowspec, two,
    )
    body = make_body(mesh.shape["dp"], mesh.shape["psg"])
    return jax.shard_map(body, mesh=mesh, in_specs=in_specs, out_specs=out_specs, check_vma=False)
```

```python
import functools

import jax
import jax.numpy as jnp
from jax import lax
from jax.experimental import pallas as pl
from jax.experimental.pallas import tpu as pltpu
from jax.sharding import PartitionSpec as P

F32 = jnp.float32
BF = jnp.bfloat16
MESH = pl.DeviceIdType.MESH
H = 12
HD = 64
SEGS = 3
LOG2E = 1.4426950408889634
SHARP = 0.1
TILES = ((0, 0, 256, 0), (128, 0, 384, 256), (256, 128, 384, 640), (384, 256, 256, 1024))
PW = 1280
LEN = 512


def nn(a, b):
    return lax.dot_general(a, b, (((1,), (0,)), ((), ())), preferred_element_type=F32)


def nt(a, b):
    return lax.dot_general(a, b, (((1,), (1,)), ((), ())), preferred_element_type=F32)


def tn(a, b):
    return lax.dot_general(a, b, (((0,), (0,)), ((), ())), preferred_element_type=F32)


def at(i, n):
    return pl.ds(pl.multiple_of(i * n, n), n)


def rows_at(start, n, unit):
    return pl.ds(pl.multiple_of(start, unit), n)


class Space:
    pass


def norm_stats(v):
    mean = jnp.mean(v, -1, keepdims=True)
    c = v - mean
    inv = lax.rsqrt(jnp.mean(c * c, -1, keepdims=True) + 1e-12)
    return c * inv, inv


class Ring:
    def __init__(self, s, u, g, b, half, places, f, rd, where):
        self.s, self.u, self.g, self.b, self.half = s, u, g, b, half
        self.c_at, self.a_at, self.b_at, self.z_at = places
        self.f, self.rd = f, rd
        dp, psg = where
        self.z, self.x, self.y, self.c = dp // 2, lax.rem(dp, 2), psg // 2, lax.rem(psg, 2)
        self.core = {"psg": self.y * 2 + 1 - self.c}
        self.xn = {"dp": self.z * 2 + 1 - self.x}
        self.yn = {"psg": (1 - self.y) * 2 + self.c}
        self.zn = [{"dp": lax.rem(self.z + k, 4) * 2 + self.x} for k in range(1, 4)]

    def cols(self, c):
        return pl.ds(pl.multiple_of(c * self.half, 128), self.half)

    def part(self, row, n, c):
        return self.g.at[pl.ds(pl.multiple_of(row * self.b, 16), n * self.b), self.cols(c)]

    def remote(self, i, src, dst, dev):
        return pltpu.make_async_remote_copy(
            src_ref=src, dst_ref=dst, send_sem=self.s.gss.at[self.u, i], recv_sem=self.s.grs.at[self.u, i],
            device_id=dev, device_id_type=MESH,
        )

    def copy_c(self, z):
        return self.remote(z, self.part(4 * z, 4, 1 - self.c), self.c_at(z), self.core)

    def copy_a(self, z):
        if z % 2 == 0:
            return [self.remote(4 + z // 2, self.part(4 * z + 2 * (1 - self.x), 2, self.c), self.a_at(z, 0, 2), self.xn)]
        return [
            self.remote(
                6 + z - 1 + x, self.part(4 * z + 2 * x + 1 - self.y, 1, self.c), self.a_at(z, x, 1), self.yn
            )
            for x in range(2)
        ]

    def copy_b(self, z):
        if z % 2 == 0:
            return self.remote(10 + z, self.part(4 * z + 2 * self.x + 1 - self.y, 1, self.c), self.b_at(z), self.yn)
        return self.remote(10 + z, self.part(4 * z + 2 * (1 - self.x) + self.y, 1, self.c), self.b_at(z), self.xn)

    def copy_z(self, k):
        z = lax.rem(self.z + k + 1, 4)
        return self.remote(14 + k, self.part(4 * z + 2 * self.x + self.y, 1, self.c), self.z_at(k), self.zn[k])

    def copy_d(self):
        h = self.b // 2
        src = self.f.at[pl.ds(pl.multiple_of((1 - self.c) * h, 8), h), :]
        return self.remote(17, src, self.rd, self.core)

    def add(self, part, got):
        part[...] = part[...] + got[...]

    def start(self, *zs):
        for z in zs:
            self.copy_c(z).start()

    def to_a(self, *zs):
        for z in zs:
            self.copy_c(z).wait_recv()
            self.add(self.part(4 * z, 4, self.c), self.c_at(z))
            for c in self.copy_a(z):
                c.start()

    def to_b(self, *zs):
        for z in zs:
            for c in self.copy_a(z):
                c.wait_recv()
            if z % 2 == 0:
                self.add(self.part(4 * z + 2 * self.x, 2, self.c), self.a_at(z, 0, 2))
            else:
                for x in range(2):
                    self.add(self.part(4 * z + 2 * x + self.y, 1, self.c), self.a_at(z, x, 1))
            self.copy_b(z).start()

    def to_z(self, *zs):
        for z in zs:
            self.copy_b(z).wait_recv()
            self.add(self.part(4 * z + 2 * self.x + self.y, 1, self.c), self.b_at(z))
        if zs[-1] == 3:
            for k in range(3):
                self.copy_z(k).start()

    def to_core(self):
        v = self.part(4 * self.z + 2 * self.x + self.y, 1, self.c)[...].astype(F32)
        for k in range(3):
            self.copy_z(k).wait_recv()
            v = v + self.z_at(k)[...].astype(F32)
        self.f[...] = v
        self.copy_d().start()

    def out(self, put):
        self.copy_d().wait_recv()
        h = self.b // 2
        put(self.c, self.f[pl.ds(pl.multiple_of(self.c * h, 8), h), :])
        put(1 - self.c, self.rd[...])

    def finish(self):
        for z in range(4):
            self.copy_c(z).wait_send()
            for c in self.copy_a(z):
                c.wait_send()
            self.copy_b(z).wait_send()
        for k in range(3):
            self.copy_z(k).wait_send()
        self.copy_d().wait_send()


def place(ref, f, n, width):
    def ref_at(i, x=0, m=1):
        row, col = f(i)
        return ref.at[row + x * n : row + x * n + m * n, col : col + width]

    return ref_at


def make_rings(s, cfg, where):
    D, FF = cfg.D, cfg.FF
    h, w, b, e = D // 2, FF // 2, D // 16, FF // 16
    low = D
    spots = lambda r, k: (
        place(r, lambda z: (low + 4 * b * (z % 2), (k + z // 2) * h), 4 * b, h),
        place(r, lambda z: (low + 2 * b * z, (k + 2) * h), b, h),
        place(r, lambda z: (low + b * z, (k + 3) * h), b, h),
        place(r, lambda z: (low + b * (4 + z), (k + 3) * h), b, h),
    )
    down = (
        place(s.hid, lambda z: (0, z * h), 4 * e, h),
        place(s.hid, lambda z: (2 * e * (z % 2), (4 + z // 2) * h), e, h),
        place(s.hid, lambda z: (e * z, 6 * h), e, h),
        place(s.hid, lambda z: (e * z, 7 * h), e, h),
    )
    up = (
        place(s.slo, lambda z: (4 * b * z, 0), 4 * b, w),
        place(s.slo, lambda z: (2 * b * z, w), b, w),
        place(s.slo, lambda z: (b * (8 + z), w), b, w),
        place(s.slo, lambda z: (b * (12 + z), w), b, w),
    )
    second = (
        place(s.y1, lambda z: (4 * b * z, 0), 4 * b, h),
        place(s.y1, lambda z: (low + 2 * b * z, 0), b, h),
        place(s.y1, lambda z: (b * z, h), b, h),
        place(s.y1, lambda z: (b * (4 + z), h), b, h),
    )
    third = (
        place(s.y1, lambda z: (b * (7 + 4 * z), h), 4 * b, h),
        place(s.hid, lambda z: (low + 2 * b * z, 4 * h), b, h),
        place(s.hid, lambda z: (low + b * z, 5 * h), b, h),
        place(s.hid, lambda z: (low + b * (4 + z), 5 * h), b, h),
    )
    small = (
        place(s.mrecv, lambda z: (4 * b * z, 0), 4 * b, 128),
        place(s.mrecv, lambda z: (b * (16 + 2 * z), 0), b, 128),
        place(s.mrecv, lambda z: (b * (24 + z), 0), b, 128),
        place(s.mrecv, lambda z: (b * (28 + z), 0), b, 128),
    )
    mk = lambda u, g, bb, half, places, f, rd: Ring(s, u, g, bb, half, places, f, rd, where)
    return (
        mk(0, s.wdn, e, h, down, s.fd, s.rd),
        mk(1, s.wup, b, w, up, s.fu, s.ru),
        mk(2, s.wout, b, h, spots(s.hid, 0), s.fq.at[0], s.rq.at[0]),
        mk(3, s.fb, b, h, spots(s.slo, 0), s.fq.at[1], s.rq.at[1]),
        mk(4, s.gb, b, h, second, s.fq.at[2], s.rq.at[2]),
        mk(5, s.ctx, b, h, third, s.fq.at[3], s.rq.at[3]),
        mk(6, s.misc, b, 128, small, s.fm, s.rm),
    )


def kernel(cfg, *refs):
    s = Space()
    for name, ref in zip(cfg.names, refs):
        setattr(s, name, ref)
    T, NP, NQ, TT = cfg.T, cfg.NP, cfg.NQ, cfg.TT
    D, FF = cfg.D, cfg.FF
    nrow = NP // LEN
    me_dp = lax.axis_index("dp")
    me_psg = lax.axis_index("psg")
    n_psg, n_dp = cfg.n_psg, cfg.n_dp

    def load(k, src, dst):
        c = pltpu.make_async_copy(src, dst, s.lsem.at[k])
        c.start()
        return c

    l_x = load(0, s.i_pass, s.x.at[0:NP])
    l_q = load(1, s.i_query, s.x.at[NP:T])
    l_wqkv = load(2, s.i_wqkv, s.wqkv)
    l_wout = load(3, s.i_wout, s.wout)
    l_wup = load(4, s.i_wup, s.wup)
    l_wdn = load(5, s.i_wdn, s.wdn)
    l_wpj = load(6, s.i_wproj, s.wproj)

    for k, v in enumerate((s.i_bout, s.i_g1, s.i_b1, s.i_bdn, s.i_g2, s.i_b2)):
        s.vin[k : k + 1, :] = v[...][None, :]
    v_bout, v_g1, v_b1, v_bdn, v_g2, v_b2 = [s.vin.at[k : k + 1] for k in range(6)]
    bar = pltpu.get_barrier_semaphore()
    peers = []
    for k in range(1, n_psg):
        peers.append({"psg": lax.rem(me_psg + k, n_psg)})
    if cfg.loss_here:
        for k in range(1, n_dp):
            peers.append({"dp": lax.rem(me_dp + k, n_dp)})
    for p in peers:
        pl.semaphore_signal(bar, inc=1, device_id=p, device_id_type=MESH)

    sums = cfg.sums
    if sums:
        ring_d, ring_u, ring_o, ring_1, ring_2, ring_3, ring_m = rings = make_rings(s, cfg, (me_dp, me_psg))

        def epoch_signal(k):
            for dev in [ring_d.core, ring_d.xn, ring_d.yn] + ring_d.zn:
                pl.semaphore_signal(s.epoch.at[k], inc=1, device_id=dev, device_id_type=MESH)

        def give_credit(z):
            pl.semaphore_signal(s.credit.at[z], inc=1, device_id=ring_d.core, device_id_type=MESH)

        def take_credit(z):
            pl.semaphore_wait(s.credit.at[z], 1)
            ring_d.start(z)

        def epoch_wait(k):
            pl.semaphore_wait(s.epoch.at[k], 6)

    plan = {}

    def loop(name, n, body):
        todo = plan.get(name, {})

        def with_plan(i, carry):
            body(i, carry)
            for k in sorted(todo):

                @pl.when(i == k)
                def _(k=k):
                    for act in todo[k]:
                        act()

            return 0

        lax.fori_loop(0, n, with_plan, 0)

    def put_in(ref):
        def put(c, v):
            ref[:, pl.ds(pl.multiple_of(c * v.shape[1], 128), v.shape[1])] = v

        return put

    def put_group(g):
        def put(c, v):
            for i in range(v.shape[1] // 128):
                k = c * (v.shape[1] // 128) + i
                col = (k // 2) * D + g * 256 + lax.rem(k, 2) * 128
                s.o_qkv[:, pl.ds(pl.multiple_of(col, 128), 128)] = v[:, i * 128 : i * 128 + 128]

        return put

    bounds = []
    for r in range(nrow):
        seg = s.i_seg[r : r + 1, :]
        bounds.append(
            (
                jnp.sum(jnp.where(seg < 1, 1.0, 0.0), axis=1, keepdims=True),
                jnp.sum(jnp.where(seg < 2, 1.0, 0.0), axis=1, keepdims=True),
            )
        )

    s.bqkv[...] = jnp.zeros_like(s.bqkv)
    s.bqkv[0:1, 0:D] = s.i_bq[...][None, :]
    s.bqkv[0:1, 2 * D : 3 * D] = s.i_bv[...][None, :]
    s.bup[0:1, :] = s.i_bup[...][None, :]
    l_x.wait()
    l_q.wait()
    l_wqkv.wait()

    def qkv_body(n, _):
        c = at(n, 256)
        s.mixed[:, c] = (nn(s.x[...], s.wqkv[:, c]) + s.bqkv[0:1, c]).astype(BF)
        return 0

    lax.fori_loop(0, 3 * D // 256, qkv_body, 0)

    scale = 0.125 * LOG2E
    li = lax.rem(lax.broadcasted_iota(jnp.int32, (LEN, 128), 1), 64).astype(F32)
    for r in range(nrow):
        b0, b1 = bounds[r]
        ti = lax.broadcasted_iota(jnp.int32, (LEN, 128), 0).astype(F32)
        seg = jnp.where(ti >= b0, 1.0, 0.0) + jnp.where(ti >= b1, 1.0, 0.0)
        s.koh[r * LEN : (r + 1) * LEN, :] = jnp.where(seg == li, 1.0, 0.0).astype(BF)
        s.qoh[r * LEN : (r + 1) * LEN, :] = jnp.where(jnp.logical_or(seg == li, li >= SEGS), 0.0, -1e30).astype(BF)
    ql = cfg.qlen
    ti = lax.broadcasted_iota(jnp.int32, (NQ, 128), 0)
    li = lax.rem(lax.broadcasted_iota(jnp.int32, (NQ, 128), 1), 64)
    mine = jnp.logical_and(ti >= li * ql, ti < li * ql + ql)
    s.koh[NP:T, :] = jnp.where(mine, 1.0, 0.0).astype(BF)
    s.qoh[NP:T, :] = jnp.where(jnp.logical_or(mine, li * ql >= NQ), 0.0, -1e30).astype(BF)
    one_b = jnp.ones((), BF)

    def mix(h, a, b):
        keep = lax.broadcasted_iota(jnp.int32, a.shape, 1) < 64
        return jnp.where(keep, a, b) if h == 0 else jnp.where(keep, b, a)

    def att_tile(qr, kr, cq, ck, cv, keep_e):
        q, k, v = s.mixed[qr, cq], s.mixed[kr, ck], s.mixed[kr, cv]
        qo, ko = s.qoh[qr, :], s.koh[kr, :]
        o = []
        for h in range(2):
            sc = nt(mix(h, q, qo), mix(h, k, ko))
            e = jnp.exp2(sc * scale - jnp.max(sc, -1, keepdims=True) * scale).astype(BF)
            keep_e(h, e)
            o.append(nn(e, mix(h, v, one_b)))
        inv = pltpu.roll(1.0 / mix(1, o[0], o[1]), 64, 1)
        s.ctx[qr, cq] = (mix(0, o[0], o[1]) * inv).astype(BF)
        s.dctx[qr, cq] = inv.astype(BF)

    def pair_cols(hp):
        return at(hp, 128), at(hp + D // 128, 128), at(hp + 2 * D // 128, 128)

    def p_copy_out(i, slot):
        return pltpu.make_async_copy(s.pbuf.at[slot], s.o_p.at[i], s.psem.at[slot])

    def att_body(i, _):
        r, hp = i // (H // 2), lax.rem(i, H // 2)
        slot = lax.rem(i, 2)

        @pl.when(i >= 2)
        def _():
            p_copy_out(i - 2, slot).wait()

        for qs, ks, kw, off in TILES:

            def keep_e(h, e):
                s.pbuf[slot, h, :, off : off + kw] = e

            att_tile(rows_at(r * LEN + qs, 128, 128), rows_at(r * LEN + ks, kw, 128), *pair_cols(hp), keep_e)
        p_copy_out(i, slot).start()
        return 0

    lax.fori_loop(0, nrow * (H // 2), att_body, 0)

    def att_q_body(hp, _):
        def keep_e(h, e):
            s.pq[hp, h] = e

        att_tile(slice(NP, T), slice(NP, T), *pair_cols(hp), keep_e)
        return 0

    lax.fori_loop(0, H // 2, att_q_body, 0)
    last = nrow * (H // 2)
    p_copy_out(last - 2, (last - 2) % 2).wait()
    p_copy_out(last - 1, (last - 1) % 2).wait()

    l_wout.wait()

    def out_body(t, _):
        rr = at(t, TT)
        v = nn(s.ctx[rr, :], s.wout[...]) + v_bout[...] + s.x[rr, :].astype(F32)
        y, inv = norm_stats(v)
        s.y1[rr, :] = y.astype(BF)
        s.st[rr, 0:1] = inv
        s.fb[rr, :] = (y * v_g1[...] + v_b1[...]).astype(BF)
        return 0

    lax.fori_loop(0, T // TT, out_body, 0)

    l_wup.wait()

    def up_body(n, _):
        c = at(n, 256)
        for m in range(T // TT):
            rr = slice(m * TT, m * TT + TT)
            h = nn(s.fb[rr, :], s.wup[:, c]) + s.bup[0:1, c]
            cdf = 0.5 * (1.0 + lax.erf(h * 0.7071067811865476))
            s.hid[rr, c] = (h * cdf).astype(BF)
            s.slo[rr, c] = (cdf + h * jnp.exp2(h * h * (-0.5 * LOG2E)) * 0.3989422804014327).astype(BF)
        return 0

    lax.fori_loop(0, FF // 256, up_body, 0)

    l_wdn.wait()
    l_wpj.wait()

    def down_body(t, _):
        rr = at(t, TT)
        first = s.y1[rr, :].astype(F32) * v_g1[...] + v_b1[...]
        v = first + (nn(s.hid[rr, :], s.wdn[...]) + v_bdn[...])
        y, inv = norm_stats(v)
        s.gs[rr, :] = y
        s.st[rr, 1:2] = inv
        sec = (y * v_g2[...] + v_b2[...]).astype(BF)
        s.gb[rr, :] = sec
        pj = nn(sec, s.wproj[...])
        il = lax.rsqrt(jnp.sum(pj * pj, -1, keepdims=True) + 1e-06)
        s.st[rr, 2:3] = il
        u = pj * il
        s.unit[rr, :] = u
        s.unitb[rr, :] = u.astype(BF)
        return 0

    lax.fori_loop(0, T // TT, down_body, 0)

    o_pe = pltpu.make_async_copy(s.unitb.at[0:NP], s.o_pe, s.osem.at[0])
    o_pe.start()
    o_qe = pltpu.make_async_copy(s.unitb.at[NP:T], s.o_qe, s.osem.at[1])
    o_qe.start()

    pl.semaphore_wait(bar, len(peers))
    sends = []

    def remote(src, dst, ssem, rsem, dev):
        c = pltpu.make_async_remote_copy(
            src_ref=src, dst_ref=dst, send_sem=ssem, recv_sem=rsem, device_id=dev, device_id_type=MESH
        )
        return c

    q_copies = []
    for k in range(1, n_psg):
        c = remote(
            s.unitb.at[NP:T], s.aq.at[k], s.ss.at[0, k], s.rs.at[0, k], {"psg": lax.rem(me_psg + k, n_psg)}
        )
        c.start()
        q_copies.append(c)
    s.aq[0] = s.unitb[NP:T, :]

    for r in range(nrow):
        b0, b1 = bounds[r]
        ti = lax.broadcasted_iota(jnp.int32, (LEN, 128), 0).astype(F32)
        li = lax.broadcasted_iota(jnp.int32, (LEN, 128), 1).astype(F32)
        pid = SEGS * r + jnp.where(ti >= b0, 1.0, 0.0) + jnp.where(ti >= b1, 1.0, 0.0)
        s.ind[r * LEN : (r + 1) * LEN, :] = jnp.where(pid == li, 1.0, 0.0).astype(BF)
    count = jnp.sum(s.ind[...].astype(F32), axis=0, keepdims=True)
    slots = nrow * SEGS
    valid = lax.broadcasted_iota(jnp.int32, (1, 128), 1) < slots
    count = jnp.where(valid, count, 1.0)
    nqg = NQ // ql
    s.lg[0] = jnp.zeros(s.lg.shape[1:], F32)

    def powers(k):
        sim = nt(s.aq[k], s.unitb[0:NP, :])
        return jnp.exp2((sim - 1.0) * (LOG2E / SHARP))

    for k in range(n_psg):
        if k:
            q_copies[k - 1].wait_recv()
        pw = powers(k)
        hi = pw.astype(BF)
        lo = (pw - hi.astype(F32)).astype(BF)
        tot = nn(hi, s.ind[...]) + nn(lo, s.ind[...])
        tot = jnp.where(valid, tot, 1.0)
        s.tot[k] = tot
        line = jnp.log(tot / count) + 1.0 / SHARP
        line = jnp.where(valid, line, 0.0)
        src = lax.rem(me_psg + n_psg - k, n_psg)
        s.line[rows_at(src * NQ, NQ, NQ), :] = line

    nq_all = n_psg * nqg
    qrow = lax.broadcasted_iota(jnp.int32, (nq_all, n_psg * NQ), 0) * ql
    qcol = lax.broadcasted_iota(jnp.int32, (nq_all, n_psg * NQ), 1)
    sel = jnp.where(jnp.logical_and(qcol >= qrow, qcol < qrow + ql), 1.0, 0.0).astype(BF)
    line = s.line[...]
    hi = line.astype(BF)
    line = line - hi.astype(F32)
    mid = line.astype(BF)
    lo = (line - mid.astype(F32)).astype(BF)
    s.lg[0, 0:nq_all, :] = nn(sel, hi) + (nn(sel, mid) + nn(sel, lo))
    s.tsq[...] = jnp.zeros_like(s.tsq)
    s.tsq[0:slots, 0:nq_all] = s.i_teach[...]
    s.lg[0, nq_all : 2 * nq_all, :] = s.tsq[...].T[0:nq_all, :]
    l_copies = []
    for k in range(1, n_psg):
        c = remote(
            s.lg.at[0], s.lg.at[k], s.ss.at[1, k], s.rs.at[1, k], {"psg": lax.rem(me_psg + k, n_psg)}
        )
        c.start()
        l_copies.append(c)
    for c in l_copies:
        c.wait_recv()
    ok = valid[None]
    lg = s.lg[...]
    half = nq_all

    def log_norm(v):
        vm = jnp.where(valid[None], v, -1e30)
        top = jnp.max(jnp.max(vm, axis=-1, keepdims=True), axis=0, keepdims=True)
        sh = v - top
        ex = jnp.where(valid[None], jnp.exp(sh), 0.0)
        tot = jnp.sum(jnp.sum(ex, axis=-1, keepdims=True), axis=0, keepdims=True)
        return sh - jnp.log(tot)

    stu = log_norm(lg[:, 0:half, :])
    tea = log_norm(lg[:, half : 2 * half, :])
    pt = jnp.exp(tea)
    kl = jnp.where(ok, pt * (tea - stu), 0.0)
    group_sum = jnp.sum(jnp.sum(jnp.sum(kl, axis=0), axis=-1, keepdims=True), axis=0, keepdims=True)
    s.ls[0] = jnp.broadcast_to(group_sum / n_dp, (8, 128))
    loss_copies = []
    if cfg.loss_here:
        for k in range(1, n_dp):
            c = remote(
                s.ls.at[0], s.ls.at[k], s.lss.at[k], s.lrs.at[k], {"dp": lax.rem(me_dp + k, n_dp)}
            )
            c.start()
            loss_copies.append(c)
    s.gl[...] = jnp.where(valid, (jnp.exp(stu[0]) - pt[0]) / n_dp, 0.0)
    for q in range(nq_all):
        s.line[q * ql : q * ql + ql, :] = jnp.broadcast_to(s.gl[q : q + 1, :], (ql, 128))

    g_copies = []
    for k in list(range(1, n_psg)) + [0]:
        pw = powers(k)
        src = lax.rem(me_psg + n_psg - k, n_psg)
        ratio = s.line[rows_at(src * NQ, NQ, NQ), :] / s.tot[k]
        ratio = ratio * (1.0 / SHARP)
        hi = ratio.astype(BF)
        lo = (ratio - hi.astype(F32)).astype(BF)
        g = ((nt(hi, s.ind[...]) + nt(lo, s.ind[...])) * pw).astype(BF)
        s.gsim[k * NQ : (k + 1) * NQ, :] = g
        qp = nn(g, s.unitb[0:NP, :])
        if k:
            s.qs[k] = qp.astype(BF)
            c = remote(s.qs.at[k], s.qr.at[k], s.ss.at[2, k], s.rs.at[2, k], {"psg": src})
            c.start()
            g_copies.append(c)
        else:
            s.own[...] = qp

    def unit_back(gu, rr):
        u = s.unit[rr, :]
        return (s.st[rr, 2:3] * (gu - u * jnp.sum(gu * u, -1, keepdims=True))).astype(BF)

    aq = s.aq[...].reshape(n_psg * NQ, 128)
    for m in range(NP // 256):
        rr = slice(m * 256, m * 256 + 256)
        gu = tn(s.gsim[:, rr], aq)
        s.gp[rr, :] = unit_back(gu, rr)
    for c in g_copies:
        c.wait_recv()
    gu = s.own[...]
    for k in range(1, n_psg):
        gu = gu + s.qr[k].astype(F32)
    s.gp[NP:T, :] = unit_back(gu, slice(NP, T))

    s.misc[:, 0:128] = tn(s.gb[...], s.gp[...]).astype(BF)

    if sums:
        al = (0, 1, 2, 3)

        def at_step(name, k, f, *args):
            plan.setdefault(name, {}).setdefault(k, []).append(lambda: f(*args))

        for z in range(4):
            at_step("ff", 3 * z + 2, give_credit, z)
        for z in range(3):
            at_step("ff", 3 * z + 3, take_credit, z)
        at_step("norm1", 2, ring_d.to_b, 0, 1)
        at_step("gup", 6, ring_d.to_b, 2, 3)
        at_step("gout", 0, ring_d.to_z, 0, 1)
        at_step("gout", 2, ring_d.to_z, 2, 3)
        at_step("att0", 1, ring_u.to_b, 0, 1)
        at_step("att0", 1, ring_o.to_a, *al)
        at_step("att0", 3, ring_u.to_b, 2, 3)
        at_step("att1", 0, ring_d.to_core)
        at_step("att1", 0, ring_1.to_a, *al)
        at_step("att1", 1, ring_u.to_z, 0, 1)
        at_step("att1", 1, ring_o.to_b, *al)
        at_step("att1", 2, ring_u.to_z, 2, 3)
        at_step("att1", 2, ring_d.out, put_in(s.o_dn))
        at_step("att1", 3, ring_o.to_z, *al)
        at_step("att1", 3, ring_1.to_b, *al)
        at_step("att2", 0, ring_2.to_a, *al)
        at_step("att2", 1, ring_1.to_z, *al)
        at_step("att2", 2, ring_u.to_core)
        at_step("att2", 2, ring_o.to_core)
        at_step("att2", 2, ring_2.to_b, *al)
        at_step("att2", 3, ring_u.out, put_in(s.o_up))
        at_step("att2", 3, ring_o.out, put_in(s.o_out))
        at_step("att2", 3, ring_1.to_core)
        at_step("dx", 0, ring_3.to_a, *al)
        at_step("dx", 0, ring_m.to_a, *al)
        at_step("dx", 0, ring_2.to_z, *al)
        at_step("dx", 1, ring_1.out, put_group(0))
        at_step("dx", 2, ring_3.to_b, *al)
        at_step("dx", 2, ring_m.to_b, *al)
        at_step("dx", 3, ring_2.to_core)

    s.vr[...] = jnp.zeros_like(s.vr)

    def addrow(k, v):
        s.vr[k : k + 1, :] = s.vr[k : k + 1, :] + jnp.sum(v, axis=0, keepdims=True)

    def norm2_body(t, _):
        rr = at(t, TT)
        g = nt(s.gp[rr, :], s.wproj[...])
        y = s.gs[rr, :]
        addrow(6, g * y)
        addrow(7, g)
        d = g * v_g2[...]
        gs = s.st[rr, 1:2] * (d - jnp.mean(d, -1, keepdims=True) - y * jnp.mean(d * y, -1, keepdims=True))
        s.gs[rr, :] = gs
        b = gs.astype(BF)
        s.gb[rr, :] = b
        addrow(5, b.astype(F32))
        return 0

    loop('norm2', T // TT, norm2_body)

    def ff_body(n, _):
        c = at(n, 256)
        w = s.wdn[c, :]
        tot = jnp.zeros((1, 256), F32)
        for m in range(T // TT):
            rr = slice(m * TT, m * TT + TT)
            g = (nt(s.gb[rr, :], w) * s.slo[rr, c].astype(F32)).astype(BF)
            s.slo[rr, c] = g
            tot = tot + jnp.sum(g.astype(F32), axis=0, keepdims=True)
        s.bup[0:1, c] = tot
        s.wdn[c, :] = tn(s.hid[:, c], s.gb[...]).astype(BF)
        return 0

    loop('ff', FF // 256, ff_body)
    if sums:
        epoch_signal(0)
        take_credit(3)
        epoch_wait(0)
        ring_d.to_a(*al)

    def norm1_body(t, _):
        rr = at(t, TT)
        g = s.gs[rr, :] + nt(s.slo[rr, :], s.wup[...])
        y = s.y1[rr, :].astype(F32)
        addrow(3, g * y)
        addrow(4, g)
        d = g * v_g1[...]
        gs = s.st[rr, 0:1] * (d - jnp.mean(d, -1, keepdims=True) - y * jnp.mean(d * y, -1, keepdims=True))
        s.gs[rr, :] = gs
        b = gs.astype(BF)
        s.gb[rr, :] = b
        addrow(2, b.astype(F32))
        return 0

    loop('norm1', T // TT, norm1_body)

    def gup_body(n, _):
        c = at(n, 256)
        s.wup[:, c] = tn(s.fb[...], s.slo[:, c]).astype(BF)
        return 0

    loop('gup', FF // 256, gup_body)
    if sums:
        epoch_signal(1)
        epoch_wait(1)
        ring_u.start(*al)

    def dctx_body(t, _):
        rr = at(t, TT)
        s.dctx[rr, :] = (nt(s.gb[rr, :], s.wout[...]) * s.dctx[rr, :].astype(F32)).astype(BF)
        return 0

    loop('dctx', T // TT, dctx_body)
    if sums:
        ring_u.to_a(*al)

    def gout_body(n, _):
        c = at(n, 256)
        s.wout[:, c] = tn(s.ctx[...], s.gb[:, c]).astype(BF)
        return 0

    loop('gout', D // 256, gout_body)
    if sums:
        ring_o.start(*al)

    def p_copy_in(j):
        g, rest = j // (2 * nrow), lax.rem(j, 2 * nrow)
        i = (rest // 2) * (H // 2) + 2 * g + lax.rem(rest, 2)
        slot = lax.rem(j, 2)
        return pltpu.make_async_copy(s.o_p.at[i], s.pbuf.at[slot], s.psem.at[slot])

    steps = nrow * (H // 2)
    p_copy_in(0).start()

    def back_tile(qr, kr, cq, ck, cv, e_of, keep_ds):
        do, k, v = s.dctx[qr, cq], s.mixed[kr, ck], s.mixed[kr, cv]
        prod = (-pltpu.roll(do.astype(F32) * s.ctx[qr, cq].astype(F32), 64, 1)).astype(BF)
        dq = []
        for h in range(2):
            ds = (e_of(h).astype(F32) * nt(mix(h, do, prod), mix(h, v, one_b))).astype(BF)
            keep_ds(h, ds)
            dq.append(nn(ds, k))
        return (mix(0, dq[0], dq[1]) * 0.125).astype(BF)

    def att_back(j, _):
        g, rest = j // (2 * nrow), lax.rem(j, 2 * nrow)
        r = rest // 2
        hp = 2 * g + lax.rem(rest, 2)
        slot = lax.rem(j, 2)

        @pl.when(j + 1 < steps)
        def _():
            p_copy_in(j + 1).start()

        p_copy_in(j).wait()
        cq, ck, cv = pair_cols(hp)
        base = r * LEN

        def rws(a, n):
            return rows_at(base + a, n, 128)

        for qs, ks, kw, off in TILES:

            def keep_ds(h, ds):
                s.ds[h, :, off : off + kw] = ds

            s.dq[qs : qs + 128, :] = back_tile(
                rws(qs, 128), rws(ks, kw), cq, ck, cv, lambda h: s.pbuf[slot, h, :, off : off + kw], keep_ds
            )
        for kk in range(4):
            dk = [None, None]
            dv = [None, None]
            for h in range(2):
                for qs, ks, kw, off in TILES:
                    rel = kk * 128 - ks
                    if rel < 0 or rel >= kw:
                        continue
                    qt = s.mixed[rws(qs, 128), cq]
                    ot = s.dctx[rws(qs, 128), cq]
                    a = tn(s.ds[h, :, off + rel : off + rel + 128], qt)
                    b = tn(s.pbuf[slot, h, :, off + rel : off + rel + 128], ot)
                    dk[h] = a if dk[h] is None else dk[h] + a
                    dv[h] = b if dv[h] is None else dv[h] + b
            s.dk[kk * 128 : kk * 128 + 128, :] = (mix(0, dk[0], dk[1]) * 0.125).astype(BF)
            s.dv[kk * 128 : kk * 128 + 128, :] = mix(0, dv[0], dv[1]).astype(BF)
        s.mixed[rws(0, LEN), cq] = s.dq[...]
        s.mixed[rws(0, LEN), ck] = s.dk[...]
        s.mixed[rws(0, LEN), cv] = s.dv[...]
        return 0

    def att_back_q(hp, _):
        cq, ck, cv = pair_cols(hp)
        rr = slice(NP, T)
        q, do = s.mixed[rr, cq], s.dctx[rr, cq]
        grads = [None, None]

        def keep_ds(h, ds):
            grads[h] = ds

        dq = back_tile(rr, rr, cq, ck, cv, lambda h: s.pq[hp, h], keep_ds)
        dk = [tn(grads[h], q) for h in range(2)]
        dv = [tn(s.pq[hp, h], do) for h in range(2)]
        s.mixed[rr, cq] = dq
        s.mixed[rr, ck] = (mix(0, dk[0], dk[1]) * 0.125).astype(BF)
        s.mixed[rr, cv] = mix(0, dv[0], dv[1]).astype(BF)
        return 0

    lax.fori_loop(0, H // 2, att_back_q, 0)

    groups = (s.fb, s.gb, s.ctx)

    def group_grad(g):
        for w in range(3):
            c = w * D + g * 256
            groups[g][0:D, w * 256 : w * 256 + 256] = tn(s.x[...], s.mixed[:, c : c + 256]).astype(BF)

    for g in range(3):

        @functools.partial(loop, 'att%d' % g, 2 * nrow)
        def _(j, _, g=g):
            att_back(2 * nrow * g + j, 0)

        group_grad(g)
        if sums:
            (ring_1, ring_2, ring_3)[g].start(*al)
    for w, k in ((0, 0), (2, 1)):
        s.vr[k : k + 1, :] = jnp.sum(s.mixed[:, w * D : w * D + D].astype(F32), axis=0, keepdims=True)

    if sums:
        pad = jnp.zeros((120, 128), F32)
        for i in range(D // 128):
            v = s.vr[:, i * 128 : i * 128 + 128]
            s.vcol[i * 128 : i * 128 + 128, :] = jnp.concatenate([v, pad], 0).T
        q = D // 32
        lane = lax.broadcasted_iota(jnp.int32, (q, 128), 1)
        for i in range(FF // 384):
            for k in range(3):
                v = s.bup[0:1, i * 384 + k * 128 : i * 384 + k * 128 + 128]
                s.tcol[k * 128 : k * 128 + 128, :] = jnp.broadcast_to(v, (128, 128)).T
            for d in range(4):
                rr = slice((4 * i + d) * q, (4 * i + d) * q + q)
                v = s.vcol[rr, :]
                for k in range(4):
                    v = jnp.where(lane == 8 + k, s.tcol[(4 * d + k) * q : (4 * d + k) * q + q, :], v)
                s.vcol[rr, :] = v
        s.misc[:, 128:256] = s.vcol[...].astype(BF)
        ring_m.start(*al)

    def dx_body(t, _):
        rr = at(t, TT)
        s.gs[rr, :] = s.gs[rr, :] + nt(s.mixed[rr, :], s.wqkv[...])
        return 0

    loop('dx', T // TT, dx_body)
    outs = [
        pltpu.make_async_copy(s.gs.at[0:NP], s.o_gp, s.osem.at[2]),
        pltpu.make_async_copy(s.gs.at[NP:T], s.o_gq, s.osem.at[3]),
    ]
    if not sums:
        outs += [
            pltpu.make_async_copy(s.wdn, s.o_dn, s.osem.at[4]),
            pltpu.make_async_copy(s.wup, s.o_up, s.osem.at[5]),
            pltpu.make_async_copy(s.wout, s.o_out, s.osem.at[6]),
            pltpu.make_async_copy(s.ctx.at[0:D], s.o_q.at[0], s.osem.at[7]),
            pltpu.make_async_copy(s.fb.at[0:D], s.o_q.at[1], s.osem.at[8]),
            pltpu.make_async_copy(s.gb.at[0:D], s.o_q.at[2], s.osem.at[9]),
            pltpu.make_async_copy(s.misc, s.o_misc, s.osem.at[10]),
        ]
        s.o_bup[...] = s.bup[0:1, :]
        s.o_vr[...] = s.vr[...]
    for c in outs:
        c.start()
    if sums:
        ring_3.to_z(*al)
        ring_m.to_z(*al)
        ring_2.out(put_group(1))
        ring_3.to_core()
        ring_m.to_core()
        ring_3.out(put_group(2))
        ring_m.out(put_in(s.o_misc))
        for r in rings:
            r.finish()
    for c in q_copies + l_copies + g_copies + loss_copies:
        c.wait_send()
    for c in loss_copies:
        c.wait_recv()
    if cfg.loss_here:
        s.o_loss[...] = jnp.sum(s.ls[...], axis=0)
    else:
        s.o_loss[...] = s.ls[0]
    for c in [o_pe, o_qe] + outs:
        c.wait()


def finish_kernel(names, *refs):
    s = Space()
    for name, ref in zip(names, refs):
        setattr(s, name, ref)
    pairs = ((s.pe, s.o_pe), (s.qe, s.o_qe), (s.gp, s.o_gp), (s.gq, s.o_gq))
    pairs += ((s.dn, s.o_dn), (s.up, s.o_up), (s.out, s.o_out), (s.qkv, s.o_qkv))
    ways = []
    for (src, dst), buf in zip(pairs, (s.bpe, s.bqe, s.bgp, s.bgq, s.bdn, s.bup, s.bout, s.bqkv)):
        n = src.shape[0] // 4 if src.shape[0] > 512 else src.shape[0]
        for i in range(src.shape[0] // n):
            k = len(ways)
            rr = slice(i * n, i * n + n)
            ways.append(
                (
                    pltpu.make_async_copy(src.at[rr], buf.at[rr], s.sem.at[0, k]),
                    pltpu.make_async_copy(buf.at[rr], dst.at[rr], s.sem.at[1, k]),
                )
            )
    for c, _ in ways:
        c.start()
    s.o_loss[...] = s.loss[0, 0]
    s.o_proj[...] = s.misc[:, 0:128]
    q = s.misc.shape[0]
    s.sq[...] = jnp.zeros_like(s.sq)
    s.sq[0:q, :] = s.misc[:, 128:256]
    s.sq[...] = s.sq[...].T
    for k in range(8):
        getattr(s, "o_v%d" % k)[...] = s.sq[k, 0:q]
    s.o_bup[...] = jnp.concatenate([s.sq[8 + k : 9 + k, 0:q] for k in range(4)], 1)[0]
    for c, d in ways:
        c.wait()
        d.start()
    for _, d in ways:
        d.wait()


def finish(o):
    sd = jax.ShapeDtypeStruct
    any_spec = pl.BlockSpec(memory_space=pl.ANY)
    vm = pl.BlockSpec(memory_space=pltpu.VMEM)
    names = ["pe", "qe", "gp", "gq", "dn", "up", "out", "qkv"]
    ins = [(n, o["o_" + n], any_spec) for n in names] + [("loss", o["o_loss"], vm), ("misc", o["o_misc"], vm)]
    outs = [("o_" + n, sd(o["o_" + n].shape, o["o_" + n].dtype), any_spec) for n in names]
    q = o["o_misc"].shape[0]
    outs += [("o_loss", sd((), F32), pl.BlockSpec(memory_space=pltpu.SMEM)), ("o_proj", sd((q, 128), F32), vm)]
    outs += [("o_v%d" % k, sd((q,), F32), vm) for k in range(8)] + [("o_bup", sd((4 * q,), F32), vm)]
    scratch = [("sq", pltpu.VMEM((128, 128), F32)), ("sem", pltpu.SemaphoreType.DMA((2, 14)))]
    scratch += [("b" + n, pltpu.VMEM(o["o_" + n].shape, o["o_" + n].dtype)) for n in names]
    all_names = [n for n, *_ in ins] + [n for n, *_ in outs] + [n for n, _ in scratch]
    res = pl.pallas_call(
        functools.partial(finish_kernel, all_names),
        out_shape=[v[1] for v in outs],
        in_specs=[v[2] for v in ins],
        out_specs=[v[2] for v in outs],
        scratch_shapes=[v for _, v in scratch],
    )(*[v[1] for v in ins])
    return dict(zip([n for n, *_ in outs], res))


def make_body(n_dp, n_psg):
    def body(
        passage_states, segment_ids, query_states, teacher_scores,
        w_qkv, bias_q, bias_v, w_out, bias_out, ln1_gain, ln1_bias,
        w_up, bias_up, w_down, bias_down, ln2_gain, ln2_bias, w_proj,
    ):
        D, FF = w_up.shape
        E = w_proj.shape[1]
        rows, length, _ = passage_states.shape
        qn, ql, _ = query_states.shape
        NP, NQ = rows * length, qn * ql
        T = NP + NQ
        cfg = Space()
        cfg.T, cfg.NP, cfg.NQ, cfg.TT = T, NP, NQ, T // 4
        cfg.D, cfg.FF, cfg.qlen = D, FF, ql
        cfg.n_dp, cfg.n_psg = n_dp, n_psg
        cfg.loss_here = n_dp <= 16
        cfg.sums = n_dp == 8 and n_psg == 4
        npair = rows * (H // 2)
        any_spec = pl.BlockSpec(memory_space=pl.ANY)
        vm = pl.BlockSpec(memory_space=pltpu.VMEM)
        ins = [
            ("i_pass", passage_states.reshape(NP, D), any_spec),
            ("i_query", query_states.reshape(NQ, D), any_spec),
            ("i_seg", segment_ids, vm),
            ("i_teach", teacher_scores.T, vm),
            ("i_wqkv", w_qkv, any_spec),
            ("i_bq", bias_q, vm),
            ("i_bv", bias_v, vm),
            ("i_wout", w_out, any_spec),
            ("i_bout", bias_out, vm),
            ("i_g1", ln1_gain, vm),
            ("i_b1", ln1_bias, vm),
            ("i_wup", w_up, any_spec),
            ("i_bup", bias_up, vm),
            ("i_wdn", w_down, any_spec),
            ("i_bdn", bias_down, vm),
            ("i_g2", ln2_gain, vm),
            ("i_b2", ln2_bias, vm),
            ("i_wproj", w_proj, any_spec),
        ]
        sd = jax.ShapeDtypeStruct
        outs = [
            ("o_pe", sd((NP, E), BF), any_spec),
            ("o_qe", sd((NQ, E), BF), any_spec),
            ("o_loss", sd((8, 128), F32), vm),
            ("o_gp", sd((NP, D), F32), any_spec),
            ("o_gq", sd((NQ, D), F32), any_spec),
            ("o_p", sd((npair, 2, 128, PW), BF), any_spec),
        ]
        n_dev = n_dp * n_psg
        if cfg.sums:
            outs += [
                ("o_dn", sd((FF // n_dev, D), F32), vm),
                ("o_up", sd((D // n_dev, FF), F32), vm),
                ("o_out", sd((D // n_dev, D), F32), vm),
                ("o_qkv", sd((D // n_dev, 3 * D), F32), vm),
                ("o_misc", sd((D // n_dev, 256), F32), vm),
            ]
        else:
            outs += [
                ("o_dn", sd((FF, D), BF), any_spec),
                ("o_up", sd((D, FF), BF), any_spec),
                ("o_out", sd((D, D), BF), any_spec),
                ("o_q", sd((3, D, D), BF), any_spec),
                ("o_misc", sd((D, 256), BF), any_spec),
                ("o_bup", sd((1, FF), F32), vm),
                ("o_vr", sd((8, D), F32), vm),
            ]
        V = pltpu.VMEM
        DMA = pltpu.SemaphoreType.DMA
        scratch = [
            ("x", V((T, D), BF)),
            ("wqkv", V((D, 3 * D), BF)),
            ("wout", V((D, D), BF)),
            ("wup", V((D, FF), BF)),
            ("wdn", V((FF, D), BF)),
            ("wproj", V((D, E), BF)),
            ("bqkv", V((8, 3 * D), F32)),
            ("vin", V((8, D), F32)),
            ("tsq", V((128, 128), F32)),
            ("mixed", V((T, 3 * D), BF)),
            ("pbuf", V((2, 2, 128, PW), BF)),
            ("pq", V((H // 2, 2, NQ, NQ), BF)),
            ("koh", V((T, 128), BF)),
            ("qoh", V((T, 128), BF)),
            ("ctx", V((T, D), BF)),
            ("y1", V((T, D), BF)),
            ("fb", V((T, D), BF)),
            ("hid", V((T, FF), BF)),
            ("slo", V((T, FF), BF)),
            ("gs", V((T, D), F32)),
            ("gb", V((T, D), BF)),
            ("st", V((T, 128), F32)),
            ("unit", V((T, E), F32)),
            ("unitb", V((T, E), BF)),
            ("aq", V((n_psg, NQ, E), BF)),
            ("ind", V((NP, 128), BF)),
            ("tot", V((n_psg, NQ, 128), F32)),
            ("lg", V((n_psg, 2 * n_psg * qn, 128), F32)),
            ("line", V((n_psg * NQ, 128), F32)),
            ("gl", V((n_psg * qn, 128), F32)),
            ("ls", V((n_dp if cfg.loss_here else 1, 8, 128), F32)),
            ("gsim", V((n_psg * NQ, NP), BF)),
            ("qs", V((n_psg, NQ, E), BF)),
            ("qr", V((n_psg, NQ, E), BF)),
            ("own", V((NQ, E), F32)),
            ("gp", V((T, E), BF)),
            ("misc", V((D, 256), BF)),
            ("vr", V((8, D), F32)),
            ("vcol", V((D, 128), F32)),
            ("bup", V((8, FF), F32)),
            ("dctx", V((T, D), BF)),
            ("ds", V((2, 128, PW), BF)),
            ("dq", V((LEN, 128), BF)),
            ("dk", V((LEN, 128), BF)),
            ("dv", V((LEN, 128), BF)),
            ("lsem", DMA((7,))),
            ("psem", DMA((2,))),
            ("osem", DMA((11,))),
            ("ss", DMA((3, n_psg))),
            ("rs", DMA((3, n_psg))),
            ("lss", DMA((n_dp,))),
            ("lrs", DMA((n_dp,))),
        ]
        if cfg.sums:
            b, e = D // 16, FF // 16
            scratch += [
                ("tcol", V((384, 128), F32)),
                ("mrecv", V((31 * b, 128), BF)),
                ("fd", V((e, D // 2), F32)),
                ("rd", V((e // 2, D // 2), F32)),
                ("fu", V((b, FF // 2), F32)),
                ("ru", V((b // 2, FF // 2), F32)),
                ("fq", V((4, b, D // 2), F32)),
                ("rq", V((4, b // 2, D // 2), F32)),
                ("fm", V((b, 128), F32)),
                ("rm", V((b // 2, 128), F32)),
                ("gss", DMA((7, 18))),
                ("grs", DMA((7, 18))),
                ("credit", pltpu.SemaphoreType.REGULAR((4,))),
                ("epoch", pltpu.SemaphoreType.REGULAR((2,))),
            ]
        cfg.names = [a for a, *_ in ins] + [a for a, *_ in outs] + [a for a, _ in scratch]
        res = pl.pallas_call(
            functools.partial(kernel, cfg),
            out_shape=[o[1] for o in outs],
            in_specs=[i[2] for i in ins],
            out_specs=[o[2] for o in outs],
            scratch_shapes=[v for _, v in scratch],
            compiler_params=pltpu.CompilerParams(
                collective_id=0, has_side_effects=True, vmem_limit_bytes=64 * 1024 * 1024 - 65536
            ),
        )(*[i[1] for i in ins])
        o = dict(zip([a for a, *_ in outs], res))
        if cfg.sums:
            o = finish(o)
            loss = o["o_loss"]
        else:
            loss = o["o_loss"][0, 0]
        if not cfg.loss_here:
            loss = lax.psum(loss, "dp")
        head = (
            o["o_pe"].reshape(rows, length, E),
            o["o_qe"].reshape(qn, ql, E),
            loss,
            o["o_gp"].reshape(rows, length, D),
            o["o_gq"].reshape(qn, ql, D),
        )
        if cfg.sums:
            vec = [o["o_v%d" % k] for k in range(8)]
            g_qkv, g_out, g_up, g_bup, g_dn, g_proj = [
                o["o_" + k] for k in ("qkv", "out", "up", "bup", "dn", "proj")
            ]
        else:
            q3 = o["o_q"].reshape(3, D, 3, 256)
            q3 = jnp.transpose(q3, (1, 2, 0, 3)).reshape(D, 3 * D)

            def scat(v):
                return lax.psum_scatter(v, ("dp", "psg"), scatter_dimension=0, tiled=True)

            vec = scat(o["o_vr"].T)
            vec = [vec[:, k] for k in range(8)]
            g_bup = scat(o["o_bup"].reshape(-1))
            g_qkv, g_out, g_up, g_dn, g_proj = [
                scat(v.astype(F32)) for v in (q3, o["o_out"], o["o_up"], o["o_dn"], o["o_misc"][:, 0:128])
            ]
        return head + (
            g_qkv, vec[0], vec[1], g_out, vec[2], vec[3], vec[4],
            g_up, g_bup, g_dn, vec[5], vec[6], vec[7], g_proj,
        )

    return body


def solution(mesh):
    rowspec = P(("dp", "psg"))
    three = P(("dp", "psg"), None, None)
    two = P(("dp", "psg"), None)
    in_specs = (three, two, three, P("dp", "psg")) + (P(),) * 14
    out_specs = (
        three, three, P(), three, three,
        two, rowspec, rowspec, two, rowspec, rowspec, rowspec,
        two, rowspec, two, rowspec, rowspec, rowspec, two,
    )
    body = make_body(mesh.shape["dp"], mesh.shape["psg"])
    return jax.shard_map(body, mesh=mesh, in_specs=in_specs, out_specs=out_specs, check_vma=False)
```

```python
import functools

import jax
import jax.numpy as jnp
from jax import lax
from jax.experimental import pallas as pl
from jax.experimental.pallas import tpu as pltpu
from jax.sharding import PartitionSpec as P

F32 = jnp.float32
BF = jnp.bfloat16
MESH = pl.DeviceIdType.MESH
H = 12
HD = 64
SEGS = 3
LOG2E = 1.4426950408889634
SHARP = 0.1
TILES = ((0, 0, 256, 0), (128, 0, 384, 256), (256, 128, 384, 640), (384, 256, 256, 1024))
PW = 1280
LEN = 512


def nn(a, b):
    return lax.dot_general(a, b, (((1,), (0,)), ((), ())), preferred_element_type=F32)


def nt(a, b):
    return lax.dot_general(a, b, (((1,), (1,)), ((), ())), preferred_element_type=F32)


def tn(a, b):
    return lax.dot_general(a, b, (((0,), (0,)), ((), ())), preferred_element_type=F32)


def at(i, n):
    return pl.ds(pl.multiple_of(i * n, n), n)


def rows_at(start, n, unit):
    return pl.ds(pl.multiple_of(start, unit), n)


class Space:
    pass


def norm_stats(v):
    mean = jnp.mean(v, -1, keepdims=True)
    c = v - mean
    inv = lax.rsqrt(jnp.mean(c * c, -1, keepdims=True) + 1e-12)
    return c * inv, inv


class Ring:
    def __init__(self, s, u, g, b, half, places, f, rd, where):
        self.s, self.u, self.g, self.b, self.half = s, u, g, b, half
        self.c_at, self.a_at, self.b_at, self.z_at = places
        self.f, self.rd = f, rd
        dp, psg = where
        self.z, self.x, self.y, self.c = dp // 2, lax.rem(dp, 2), psg // 2, lax.rem(psg, 2)
        self.core = {"psg": self.y * 2 + 1 - self.c}
        self.xn = {"dp": self.z * 2 + 1 - self.x}
        self.yn = {"psg": (1 - self.y) * 2 + self.c}
        self.zn = [{"dp": lax.rem(self.z + k, 4) * 2 + self.x} for k in range(1, 4)]

    def cols(self, c):
        return pl.ds(pl.multiple_of(c * self.half, 128), self.half)

    def part(self, row, n, c):
        return self.g.at[pl.ds(pl.multiple_of(row * self.b, 16), n * self.b), self.cols(c)]

    def remote(self, i, src, dst, dev):
        return pltpu.make_async_remote_copy(
            src_ref=src, dst_ref=dst, send_sem=self.s.gss.at[self.u, i], recv_sem=self.s.grs.at[self.u, i],
            device_id=dev, device_id_type=MESH,
        )

    def copy_c(self, z):
        return self.remote(z, self.part(4 * z, 4, 1 - self.c), self.c_at(z), self.core)

    def copy_a(self, z):
        if z % 2 == 0:
            return [self.remote(4 + z // 2, self.part(4 * z + 2 * (1 - self.x), 2, self.c), self.a_at(z, 0, 2), self.xn)]
        return [
            self.remote(
                6 + z - 1 + x, self.part(4 * z + 2 * x + 1 - self.y, 1, self.c), self.a_at(z, x, 1), self.yn
            )
            for x in range(2)
        ]

    def copy_b(self, z):
        if z % 2 == 0:
            return self.remote(10 + z, self.part(4 * z + 2 * self.x + 1 - self.y, 1, self.c), self.b_at(z), self.yn)
        return self.remote(10 + z, self.part(4 * z + 2 * (1 - self.x) + self.y, 1, self.c), self.b_at(z), self.xn)

    def copy_z(self, k):
        z = lax.rem(self.z + k + 1, 4)
        return self.remote(14 + k, self.part(4 * z + 2 * self.x + self.y, 1, self.c), self.z_at(k), self.zn[k])

    def send_z(self, z):
        k = lax.rem(z - self.z + 3, 4)

        @pl.when(z != self.z)
        def _():
            self.s_z(z, k).start()

    def s_z(self, z, k):
        return pltpu.make_async_remote_copy(
            src_ref=self.part(4 * z + 2 * self.x + self.y, 1, self.c), dst_ref=self.z_at(k),
            send_sem=self.s.gss.at[self.u, 14 + k], recv_sem=self.s.grs.at[self.u, 14 + k],
            device_id={"dp": z * 2 + self.x}, device_id_type=MESH,
        )

    def copy_d(self):
        h = self.b // 2
        src = self.f.at[pl.ds(pl.multiple_of((1 - self.c) * h, 8), h), :]
        return self.remote(17, src, self.rd, self.core)

    def add(self, part, got):
        part[...] = part[...] + got[...]

    def start(self, *zs):
        for z in zs:
            self.copy_c(z).start()

    def to_a(self, *zs):
        for z in zs:
            self.copy_c(z).wait_recv()
            self.add(self.part(4 * z, 4, self.c), self.c_at(z))
            for c in self.copy_a(z):
                c.start()

    def to_b(self, *zs):
        for z in zs:
            for c in self.copy_a(z):
                c.wait_recv()
            if z % 2 == 0:
                self.add(self.part(4 * z + 2 * self.x, 2, self.c), self.a_at(z, 0, 2))
            else:
                for x in range(2):
                    self.add(self.part(4 * z + 2 * x + self.y, 1, self.c), self.a_at(z, x, 1))
            self.copy_b(z).start()

    def to_z(self, *zs):
        for z in zs:
            self.copy_b(z).wait_recv()
            self.add(self.part(4 * z + 2 * self.x + self.y, 1, self.c), self.b_at(z))
            self.send_z(z)

    def to_core(self):
        v = self.part(4 * self.z + 2 * self.x + self.y, 1, self.c)[...].astype(F32)
        for k in range(3):
            self.copy_z(k).wait_recv()
            v = v + self.z_at(k)[...].astype(F32)
        self.f[...] = v
        self.copy_d().start()

    def out(self, put):
        self.copy_d().wait_recv()
        h = self.b // 2
        put(self.c, self.f[pl.ds(pl.multiple_of(self.c * h, 8), h), :])
        put(1 - self.c, self.rd[...])

    def finish(self):
        for z in range(4):
            self.copy_c(z).wait_send()
            for c in self.copy_a(z):
                c.wait_send()
            self.copy_b(z).wait_send()
        for k in range(3):
            self.copy_z(k).wait_send()
        self.copy_d().wait_send()


def place(ref, f, n, width):
    def ref_at(i, x=0, m=1):
        row, col = f(i)
        if not isinstance(row, int):
            return ref.at[pl.ds(pl.multiple_of(row, 16), n), col : col + width]
        return ref.at[row + x * n : row + x * n + m * n, col : col + width]

    return ref_at


def make_rings(s, cfg, where):
    D, FF = cfg.D, cfg.FF
    h, w, b, e = D // 2, FF // 2, D // 16, FF // 16
    low = D
    spots = lambda r, k: (
        place(r, lambda z: (low + 4 * b * (z % 2), (k + z // 2) * h), 4 * b, h),
        place(r, lambda z: (low + 2 * b * z, (k + 2) * h), b, h),
        place(r, lambda z: (low + b * z, (k + 3) * h), b, h),
        place(r, lambda z: (low + b * (4 + z), (k + 3) * h), b, h),
    )
    down = (
        place(s.hid, lambda z: (0, z * h), 4 * e, h),
        place(s.arecv, lambda z: (2 * e * z, 0), e, h),
        place(s.hid, lambda z: (e * z, 6 * h), e, h),
        place(s.hid, lambda z: (e * z, 7 * h), e, h),
    )
    up = (
        place(s.hid, lambda z: (4 * b * z, 0), 4 * b, w),
        place(s.slo, lambda z: (2 * b * z, w), b, w),
        place(s.slo, lambda z: (b * (8 + z), w), b, w),
        place(s.slo, lambda z: (b * (12 + z), w), b, w),
    )
    second = (
        place(s.y1, lambda z: (4 * b * z, 0), 4 * b, h),
        place(s.y1, lambda z: (low + 2 * b * z, 0), b, h),
        place(s.y1, lambda z: (b * z, h), b, h),
        place(s.y1, lambda z: (b * (4 + z), h), b, h),
    )
    third = (
        place(s.y1, lambda z: (b * (7 + 4 * z), h), 4 * b, h),
        place(s.hid, lambda z: (low + 2 * b * z, 4 * h), b, h),
        place(s.hid, lambda z: (low + b * z, 5 * h), b, h),
        place(s.hid, lambda z: (low + b * (4 + z), 5 * h), b, h),
    )
    small = (
        place(s.mrecv, lambda z: (4 * b * z, 0), 4 * b, 128),
        place(s.mrecv, lambda z: (b * (16 + 2 * z), 0), b, 128),
        place(s.mrecv, lambda z: (b * (24 + z), 0), b, 128),
        place(s.mrecv, lambda z: (b * (28 + z), 0), b, 128),
    )
    mk = lambda u, g, bb, half, places, f, rd: Ring(s, u, g, bb, half, places, f, rd, where)
    return (
        mk(0, s.wdn, e, h, down, s.fd, s.rd),
        mk(1, s.wup, b, w, up, s.fu, s.ru),
        mk(2, s.wout, b, h, spots(s.hid, 0), s.fq.at[0], s.rq.at[0]),
        mk(3, s.fb, b, h, spots(s.slo, 0), s.fq.at[1], s.rq.at[1]),
        mk(4, s.gb, b, h, second, s.fq.at[2], s.rq.at[2]),
        mk(5, s.ctx, b, h, third, s.fq.at[3], s.rq.at[3]),
        mk(6, s.misc, b, 128, small, s.fm, s.rm),
    )


def kernel(cfg, *refs):
    s = Space()
    for name, ref in zip(cfg.names, refs):
        setattr(s, name, ref)
    T, NP, NQ, TT = cfg.T, cfg.NP, cfg.NQ, cfg.TT
    D, FF = cfg.D, cfg.FF
    nrow = NP // LEN
    me_dp = lax.axis_index("dp")
    me_psg = lax.axis_index("psg")
    n_psg, n_dp = cfg.n_psg, cfg.n_dp

    def load(k, src, dst):
        c = pltpu.make_async_copy(src, dst, s.lsem.at[k])
        if k < 3:
            c.start()
        return c

    l_x = load(0, s.i_pass, s.x.at[0:NP])
    l_q = load(1, s.i_query, s.x.at[NP:T])
    l_wqkv = load(2, s.i_wqkv, s.wqkv)
    l_wout = load(3, s.i_wout, s.wout)
    l_wup = load(4, s.i_wup, s.wup)
    l_wdn = load(5, s.i_wdn, s.wdn)
    l_wpj = load(6, s.i_wproj, s.wproj)

    for k, v in enumerate((s.i_bout, s.i_g1, s.i_b1, s.i_bdn, s.i_g2, s.i_b2)):
        s.vin[k : k + 1, :] = v[...][None, :]
    v_bout, v_g1, v_b1, v_bdn, v_g2, v_b2 = [s.vin.at[k : k + 1] for k in range(6)]
    bar = pltpu.get_barrier_semaphore()
    peers = []
    for k in range(1, n_psg):
        peers.append({"psg": lax.rem(me_psg + k, n_psg)})
    if cfg.loss_here:
        for k in range(1, n_dp):
            peers.append({"dp": lax.rem(me_dp + k, n_dp)})
    for p in peers:
        pl.semaphore_signal(bar, inc=1, device_id=p, device_id_type=MESH)

    sums = cfg.sums
    if sums:
        ring_d, ring_u, ring_o, ring_1, ring_2, ring_3, ring_m = rings = make_rings(s, cfg, (me_dp, me_psg))

        def epoch_signal(k):
            for dev in [ring_d.core, ring_d.xn, ring_d.yn] + ring_d.zn:
                pl.semaphore_signal(s.epoch.at[k], inc=1, device_id=dev, device_id_type=MESH)

        def give_credit(z):
            pl.semaphore_signal(s.credit.at[z], inc=1, device_id=ring_d.core, device_id_type=MESH)

        def take_credit(z):
            pl.semaphore_wait(s.credit.at[z], 1)
            ring_d.start(z)

        def start_up():
            pl.semaphore_wait(s.credit.at[4], 1)
            ring_u.start(0, 1, 2, 3)

        def epoch_wait(k):
            pl.semaphore_wait(s.epoch.at[k], 6)

    plan = {}

    def loop(name, n, body):
        todo = plan.get(name, {})

        def with_plan(i, carry):
            body(i, carry)
            for k in sorted(todo):

                @pl.when(i == k)
                def _(k=k):
                    for act in todo[k]:
                        act()

            return 0

        lax.fori_loop(0, n, with_plan, 0)

    def put_in(ref):
        def put(c, v):
            ref[:, pl.ds(pl.multiple_of(c * v.shape[1], 128), v.shape[1])] = v

        return put

    def put_group(g):
        def put(c, v):
            for i in range(v.shape[1] // 128):
                k = c * (v.shape[1] // 128) + i
                col = (k // 2) * D + g * 256 + lax.rem(k, 2) * 128
                s.o_qkv[:, pl.ds(pl.multiple_of(col, 128), 128)] = v[:, i * 128 : i * 128 + 128]

        return put

    bounds = []
    for r in range(nrow):
        seg = s.i_seg[r : r + 1, :]
        bounds.append(
            (
                jnp.sum(jnp.where(seg < 1, 1.0, 0.0), axis=1, keepdims=True),
                jnp.sum(jnp.where(seg < 2, 1.0, 0.0), axis=1, keepdims=True),
            )
        )

    s.bqkv[...] = jnp.zeros_like(s.bqkv)
    s.bqkv[0:1, 0:D] = s.i_bq[...][None, :]
    s.bqkv[0:1, 2 * D : 3 * D] = s.i_bv[...][None, :]
    s.bup[0:1, :] = s.i_bup[...][None, :]
    l_x.wait()
    l_q.wait()
    l_wqkv.wait()
    for c in (l_wout, l_wup, l_wdn, l_wpj):
        c.start()

    def qkv_body(n, _):
        c = at(n, 256)
        s.mixed[:, c] = (nn(s.x[...], s.wqkv[:, c]) + s.bqkv[0:1, c]).astype(BF)
        return 0

    lax.fori_loop(0, 3 * D // 256, qkv_body, 0)

    scale = 0.125 * LOG2E
    li = lax.broadcasted_iota(jnp.int32, (LEN, 128), 1).astype(F32)
    si = lax.broadcasted_iota(jnp.int32, (128, LEN), 0).astype(F32)
    for r in range(nrow):
        b0, b1 = bounds[r]
        rr = slice(r * LEN, (r + 1) * LEN)
        ti = lax.broadcasted_iota(jnp.int32, (LEN, 128), 0).astype(F32)
        seg = jnp.where(ti >= b0, 1.0, 0.0) + jnp.where(ti >= b1, 1.0, 0.0)
        s.koh[rr, :] = jnp.where(seg == li, 1.0, 0.0).astype(BF)
        ti = lax.broadcasted_iota(jnp.int32, (128, LEN), 1).astype(F32)
        seg = jnp.where(ti >= b0, 1.0, 0.0) + jnp.where(ti >= b1, 1.0, 0.0)
        s.qoh[:, rr] = jnp.where(jnp.logical_or(seg == si, si >= SEGS), 0.0, -1e30).astype(BF)
    ql = cfg.qlen
    ti = lax.broadcasted_iota(jnp.int32, (NQ, 128), 0)
    li = lax.broadcasted_iota(jnp.int32, (NQ, 128), 1)
    s.koh[NP:T, :] = jnp.where(jnp.logical_and(ti >= li * ql, ti < li * ql + ql), 1.0, 0.0).astype(BF)
    si = lax.broadcasted_iota(jnp.int32, (128, NQ), 0)
    ti = lax.broadcasted_iota(jnp.int32, (128, NQ), 1)
    mine = jnp.logical_and(ti >= si * ql, ti < si * ql + ql)
    s.qoh[:, NP:T] = jnp.where(jnp.logical_or(mine, si * ql >= NQ), 0.0, -1e30).astype(BF)
    one_b, zero_b = jnp.ones((), BF), jnp.zeros((), BF)

    def two(v, axis):
        keep = lax.broadcasted_iota(jnp.int32, v.shape, axis) < 64
        return jnp.concatenate([jnp.where(keep, v, zero_b), jnp.where(keep, zero_b, v)], 1 - axis)

    def diagonal(v):
        return jnp.concatenate([v[0:64, 0:128], v[64:128, 128:256]], 0)

    def att_tile(qr, kr, qa, ka, kw, cq, ck, cv, keep_e):
        keys = jnp.concatenate([s.mixed[kr, ck], s.koh[kr, :]], 1)
        far = s.qoh[:, qr]
        queries = jnp.concatenate([two(s.qt[:, qa], 0), jnp.concatenate([far, far], 1)], 0)
        sc = nn(keys, queries)
        e = jnp.exp2(sc * scale - jnp.max(sc, axis=0, keepdims=True) * scale).astype(BF)
        keep_e(e)
        o = nn(jnp.concatenate([s.vt[:, ka], jnp.ones((16, kw), BF)], 0), e)
        inv = 1.0 / o[128:129, :]
        s.ctx[qr, cq] = diagonal(o[0:128, :] * inv).T.astype(BF)
        s.dctx[qr, cq] = diagonal(jnp.broadcast_to(inv, (128, 256))).T.astype(BF)

    def pair_cols(hp):
        return at(hp, 128), at(hp + D // 128, 128), at(hp + 2 * D // 128, 128)

    def p_copy_out(i, slot):
        return pltpu.make_async_copy(s.pbuf.at[slot], s.o_p.at[i], s.psem.at[slot])

    def att_body(i, _):
        r, hp = i // (H // 2), lax.rem(i, H // 2)
        slot = lax.rem(i, 2)

        @pl.when(i >= 2)
        def _():
            p_copy_out(i - 2, slot).wait()

        cq, ck, cv = pair_cols(hp)
        whole = rows_at(r * LEN, LEN, LEN)
        s.qt[...] = s.mixed[whole, cq].T
        s.vt[...] = s.mixed[whole, cv].T
        for qs, ks, kw, off in TILES:

            def keep_e(e):
                s.pbuf[slot, off : off + kw, :] = e

            qr, kr = rows_at(r * LEN + qs, 128, 128), rows_at(r * LEN + ks, kw, 128)
            att_tile(qr, kr, slice(qs, qs + 128), slice(ks, ks + kw), kw, cq, ck, cv, keep_e)
        p_copy_out(i, slot).start()
        return 0

    lax.fori_loop(0, nrow * (H // 2), att_body, 0)

    def att_q_body(hp, _):
        cq, ck, cv = pair_cols(hp)
        s.qt[:, 0:NQ] = s.mixed[NP:T, cq].T
        s.vt[:, 0:NQ] = s.mixed[NP:T, cv].T

        def keep_e(e):
            s.pq[hp] = e

        att_tile(slice(NP, T), slice(NP, T), slice(0, NQ), slice(0, NQ), NQ, cq, ck, cv, keep_e)
        return 0

    lax.fori_loop(0, H // 2, att_q_body, 0)
    last = nrow * (H // 2)
    p_copy_out(last - 2, (last - 2) % 2).wait()
    p_copy_out(last - 1, (last - 1) % 2).wait()

    l_wout.wait()

    def out_body(t, _):
        rr = at(t, TT)
        v = nn(s.ctx[rr, :], s.wout[...]) + v_bout[...] + s.x[rr, :].astype(F32)
        y, inv = norm_stats(v)
        s.y1[rr, :] = y.astype(BF)
        s.st[rr, 0:1] = inv
        s.fb[rr, :] = (y * v_g1[...] + v_b1[...]).astype(BF)
        return 0

    lax.fori_loop(0, T // TT, out_body, 0)

    l_wup.wait()

    def up_body(n, _):
        c = at(n, 256)
        for m in range(T // TT):
            rr = slice(m * TT, m * TT + TT)
            h = nn(s.fb[rr, :], s.wup[:, c]) + s.bup[0:1, c]
            cdf = 0.5 * (1.0 + lax.erf(h * 0.7071067811865476))
            s.hid[rr, c] = (h * cdf).astype(BF)
            s.slo[rr, c] = (cdf + h * jnp.exp2(h * h * (-0.5 * LOG2E)) * 0.3989422804014327).astype(BF)
        return 0

    lax.fori_loop(0, FF // 256, up_body, 0)

    def remote(src, dst, ssem, rsem, dev):
        return pltpu.make_async_remote_copy(
            src_ref=src, dst_ref=dst, send_sem=ssem, recv_sem=rsem, device_id=dev, device_id_type=MESH
        )

    l_wdn.wait()
    l_wpj.wait()

    q_copies = [
        remote(s.unitb.at[NP:T], s.aq.at[k], s.ss.at[0, k], s.rs.at[0, k], {"psg": lax.rem(me_psg + k, n_psg)})
        for k in range(1, n_psg)
    ]

    def down_body(t, _):
        rr = at(T // TT - 1 - t, TT)
        first = s.y1[rr, :].astype(F32) * v_g1[...] + v_b1[...]
        v = first + (nn(s.hid[rr, :], s.wdn[...]) + v_bdn[...])
        y, inv = norm_stats(v)
        s.gs[rr, :] = y
        s.st[rr, 1:2] = inv
        sec = (y * v_g2[...] + v_b2[...]).astype(BF)
        s.gb[rr, :] = sec
        pj = nn(sec, s.wproj[...])
        il = lax.rsqrt(jnp.sum(pj * pj, -1, keepdims=True) + 1e-06)
        s.st[rr, 2:3] = il
        u = pj * il
        s.unit[rr, :] = u
        s.unitb[rr, :] = u.astype(BF)

        @pl.when(t == 0)
        def _():
            pl.semaphore_wait(bar, len(peers))
            for c in q_copies:
                c.start()

        return 0

    lax.fori_loop(0, T // TT, down_body, 0)

    o_pe = pltpu.make_async_copy(s.unitb.at[0:NP], s.o_pe, s.osem.at[0])
    o_pe.start()
    o_qe = pltpu.make_async_copy(s.unitb.at[NP:T], s.o_qe, s.osem.at[1])
    o_qe.start()

    s.aq[0] = s.unitb[NP:T, :]

    for r in range(nrow):
        b0, b1 = bounds[r]
        ti = lax.broadcasted_iota(jnp.int32, (LEN, 128), 0).astype(F32)
        li = lax.broadcasted_iota(jnp.int32, (LEN, 128), 1).astype(F32)
        pid = SEGS * r + jnp.where(ti >= b0, 1.0, 0.0) + jnp.where(ti >= b1, 1.0, 0.0)
        s.ind[r * LEN : (r + 1) * LEN, :] = jnp.where(pid == li, 1.0, 0.0).astype(BF)
    count = jnp.sum(s.ind[...].astype(F32), axis=0, keepdims=True)
    slots = nrow * SEGS
    valid = lax.broadcasted_iota(jnp.int32, (1, 128), 1) < slots
    count = jnp.where(valid, count, 1.0)
    nqg = NQ // ql
    s.lg[0] = jnp.zeros(s.lg.shape[1:], F32)

    def powers(k):
        sim = nt(s.aq[k], s.unitb[0:NP, :])
        return jnp.exp2((sim - 1.0) * (LOG2E / SHARP))

    for k in range(n_psg):
        if k:
            q_copies[k - 1].wait_recv()
        pw = powers(k)
        hi = pw.astype(BF)
        lo = (pw - hi.astype(F32)).astype(BF)
        tot = nn(hi, s.ind[...]) + nn(lo, s.ind[...])
        tot = jnp.where(valid, tot, 1.0)
        s.tot[k] = tot
        line = jnp.log(tot / count) + 1.0 / SHARP
        line = jnp.where(valid, line, 0.0)
        src = lax.rem(me_psg + n_psg - k, n_psg)
        s.line[rows_at(src * NQ, NQ, NQ), :] = line

    nq_all = n_psg * nqg
    qrow = lax.broadcasted_iota(jnp.int32, (nq_all, n_psg * NQ), 0) * ql
    qcol = lax.broadcasted_iota(jnp.int32, (nq_all, n_psg * NQ), 1)
    sel = jnp.where(jnp.logical_and(qcol >= qrow, qcol < qrow + ql), 1.0, 0.0).astype(BF)
    line = s.line[...]
    hi = line.astype(BF)
    line = line - hi.astype(F32)
    mid = line.astype(BF)
    lo = (line - mid.astype(F32)).astype(BF)
    s.lg[0, 0:nq_all, :] = nn(sel, hi) + (nn(sel, mid) + nn(sel, lo))
    s.tsq[...] = jnp.zeros_like(s.tsq)
    s.tsq[0:slots, 0:nq_all] = s.i_teach[...]
    s.lg[0, nq_all : 2 * nq_all, :] = s.tsq[...].T[0:nq_all, :]
    l_copies = []
    for k in range(1, n_psg):
        c = remote(
            s.lg.at[0], s.lg.at[k], s.ss.at[1, k], s.rs.at[1, k], {"psg": lax.rem(me_psg + k, n_psg)}
        )
        c.start()
        l_copies.append(c)
    for c in l_copies:
        c.wait_recv()
    ok = valid[None]
    lg = s.lg[...]
    half = nq_all

    def log_norm(v):
        vm = jnp.where(valid[None], v, -1e30)
        top = jnp.max(jnp.max(vm, axis=-1, keepdims=True), axis=0, keepdims=True)
        sh = v - top
        ex = jnp.where(valid[None], jnp.exp(sh), 0.0)
        tot = jnp.sum(jnp.sum(ex, axis=-1, keepdims=True), axis=0, keepdims=True)
        return sh - jnp.log(tot)

    stu = log_norm(lg[:, 0:half, :])
    tea = log_norm(lg[:, half : 2 * half, :])
    pt = jnp.exp(tea)
    kl = jnp.where(ok, pt * (tea - stu), 0.0)
    group_sum = jnp.sum(jnp.sum(jnp.sum(kl, axis=0), axis=-1, keepdims=True), axis=0, keepdims=True)
    s.ls[0] = jnp.broadcast_to(group_sum / n_dp, (8, 128))
    loss_copies = []
    if cfg.loss_here:
        for k in range(1, n_dp):
            c = remote(
                s.ls.at[0], s.ls.at[k], s.lss.at[k], s.lrs.at[k], {"dp": lax.rem(me_dp + k, n_dp)}
            )
            c.start()
            loss_copies.append(c)
    s.gl[...] = jnp.where(valid, (jnp.exp(stu[0]) - pt[0]) / n_dp, 0.0)
    for q in range(nq_all):
        s.line[q * ql : q * ql + ql, :] = jnp.broadcast_to(s.gl[q : q + 1, :], (ql, 128))

    g_copies = []
    for k in list(range(1, n_psg)) + [0]:
        pw = powers(k)
        src = lax.rem(me_psg + n_psg - k, n_psg)
        ratio = s.line[rows_at(src * NQ, NQ, NQ), :] / s.tot[k]
        ratio = ratio * (1.0 / SHARP)
        hi = ratio.astype(BF)
        lo = (ratio - hi.astype(F32)).astype(BF)
        g = ((nt(hi, s.ind[...]) + nt(lo, s.ind[...])) * pw).astype(BF)
        s.gsim[k * NQ : (k + 1) * NQ, :] = g
        qp = nn(g, s.unitb[0:NP, :])
        if k:
            s.qs[k] = qp.astype(BF)
            c = remote(s.qs.at[k], s.qr.at[k], s.ss.at[2, k], s.rs.at[2, k], {"psg": src})
            c.start()
            g_copies.append(c)
        else:
            s.own[...] = qp

    def unit_back(gu, rr):
        u = s.unit[rr, :]
        return (s.st[rr, 2:3] * (gu - u * jnp.sum(gu * u, -1, keepdims=True))).astype(BF)

    aq = s.aq[...].reshape(n_psg * NQ, 128)
    for m in range(NP // 256):
        rr = slice(m * 256, m * 256 + 256)
        gu = tn(s.gsim[:, rr], aq)
        s.gp[rr, :] = unit_back(gu, rr)
    s.vcol[...] = tn(s.gb[0:NP, :], s.gp[0:NP, :])

    if sums:
        al = (0, 1, 2, 3)

        def at_step(name, k, f, *args):
            plan.setdefault(name, {}).setdefault(k, []).append(lambda: f(*args))

        for z in range(4):
            at_step("ff", 3 * z + 2, give_credit, z)
        for z in range(3):
            at_step("ff", 3 * z + 3, take_credit, z)
            at_step("ff", 3 * z + 5, ring_d.to_a, z)
        at_step("norm1", 0, epoch_wait, 0)
        at_step("norm1", 0, ring_d.to_b, 0)
        at_step("norm1", 0, ring_d.to_a, 3)
        at_step("norm1", 0, give_credit, 4)
        at_step("norm1", 1, ring_d.to_b, 1)
        at_step("norm1", 3, ring_d.to_b, 2)
        at_step("gup", 1, ring_d.to_z, 0, 1)
        at_step("gup", 3, ring_d.to_b, 3)
        at_step("gup", 5, start_up)
        at_step("gup", 7, ring_d.to_z, 2)
        at_step("dctx", 0, epoch_wait, 1)
        at_step("dctx", 0, ring_u.to_a, *al)
        at_step("dctx", 2, ring_d.to_z, 3)
        at_step("att0", 0, ring_o.to_a, *al)
        at_step("att0", 2, ring_u.to_b, 0, 1)
        at_step("att1", 0, ring_1.to_a, *al)
        at_step("att1", 0, ring_d.to_core)
        at_step("att1", 1, ring_u.to_b, 2, 3)
        at_step("att1", 2, ring_u.to_z, 0, 1)
        at_step("att1", 3, ring_o.to_b, *al)
        at_step("att1", 3, ring_d.out, put_in(s.o_dn))
        at_step("att2", 0, ring_2.to_a, *al)
        at_step("att2", 1, ring_1.to_b, *al)
        at_step("att2", 1, ring_u.to_z, 2, 3)
        at_step("att2", 2, ring_o.to_z, *al)
        at_step("dx", 0, ring_3.to_a, *al)
        at_step("dx", 0, ring_m.to_a, *al)
        at_step("dx", 0, ring_2.to_b, *al)
        at_step("dx", 1, ring_1.to_z, *al)
        at_step("dx", 2, ring_2.to_z, *al)
        at_step("dx", 3, ring_u.to_core)

    s.vr[...] = jnp.zeros_like(s.vr)

    def addrow(k, v):
        s.vr[k : k + 1, :] = s.vr[k : k + 1, :] + jnp.sum(v, axis=0, keepdims=True)

    def norm2_rows(rr):
        g = nt(s.gp[rr, :], s.wproj[...])
        y = s.gs[rr, :]
        addrow(6, g * y)
        addrow(7, g)
        d = g * v_g2[...]
        gs = s.st[rr, 1:2] * (d - jnp.mean(d, -1, keepdims=True) - y * jnp.mean(d * y, -1, keepdims=True))
        s.gs[rr, :] = gs
        b = gs.astype(BF)
        s.gb[rr, :] = b
        addrow(5, b.astype(F32))

    def norm2_body(t, _):
        norm2_rows(at(t, 256))
        return 0

    loop('norm2', NP // 256, norm2_body)
    for c in g_copies:
        c.wait_recv()
    gu = s.own[...]
    for k in range(1, n_psg):
        gu = gu + s.qr[k].astype(F32)
    s.gp[NP:T, :] = unit_back(gu, slice(NP, T))
    s.misc[:, 0:128] = (s.vcol[...] + tn(s.gb[NP:T, :], s.gp[NP:T, :])).astype(BF)
    norm2_rows(slice(NP, T))

    def ff_body(n, _):
        c = at(n, 256)
        w = s.wdn[c, :]
        tot = jnp.zeros((1, 256), F32)
        for m in range(T // TT):
            rr = slice(m * TT, m * TT + TT)
            g = (nt(s.gb[rr, :], w) * s.slo[rr, c].astype(F32)).astype(BF)
            s.slo[rr, c] = g
            tot = tot + jnp.sum(g.astype(F32), axis=0, keepdims=True)
        s.bup[0:1, c] = tot
        s.wdn[c, :] = tn(s.hid[:, c], s.gb[...]).astype(BF)
        return 0

    loop('ff', FF // 256, ff_body)
    if sums:
        epoch_signal(0)
        take_credit(3)

    def norm1_body(t, _):
        rr = at(t, TT)
        g = s.gs[rr, :] + nt(s.slo[rr, :], s.wup[...])
        y = s.y1[rr, :].astype(F32)
        addrow(3, g * y)
        addrow(4, g)
        d = g * v_g1[...]
        gs = s.st[rr, 0:1] * (d - jnp.mean(d, -1, keepdims=True) - y * jnp.mean(d * y, -1, keepdims=True))
        s.gs[rr, :] = gs
        b = gs.astype(BF)
        s.gb[rr, :] = b
        addrow(2, b.astype(F32))
        return 0

    loop('norm1', T // TT, norm1_body)

    def gup_body(n, _):
        if sums:
            n = lax.rem(n + (1 - ring_d.c) * (FF // 512), FF // 256)
        c = at(n, 256)
        s.wup[:, c] = tn(s.fb[...], s.slo[:, c]).astype(BF)
        return 0

    loop('gup', FF // 256, gup_body)
    if sums:
        epoch_signal(1)

    def dctx_body(t, _):
        rr = at(t, TT)
        s.dctx[rr, :] = (nt(s.gb[rr, :], s.wout[...]) * s.dctx[rr, :].astype(F32)).astype(BF)
        return 0

    loop('dctx', T // TT, dctx_body)

    def gout_body(n, _):
        c = at(n, 256)
        s.wout[:, c] = tn(s.ctx[...], s.gb[:, c]).astype(BF)
        return 0

    loop('gout', D // 256, gout_body)
    if sums:
        q = D // 32
        lane = lax.broadcasted_iota(jnp.int32, (q, 128), 1)
        for i in range(FF // 384):
            for k in range(3):
                v = s.bup[0:1, i * 384 + k * 128 : i * 384 + k * 128 + 128]
                s.tcol[k * 128 : k * 128 + 128, :] = jnp.broadcast_to(v, (128, 128)).T
            for d in range(4):
                v = jnp.zeros((q, 128), F32)
                for k in range(4):
                    v = jnp.where(lane == 8 + k, s.tcol[(4 * d + k) * q : (4 * d + k) * q + q, :], v)
                s.vcol[(4 * i + d) * q : (4 * i + d) * q + q, :] = v
    if sums:
        ring_o.start(*al)

    def p_copy_in(j):
        g, rest = j // (2 * nrow), lax.rem(j, 2 * nrow)
        i = (rest // 2) * (H // 2) + 2 * g + lax.rem(rest, 2)
        slot = lax.rem(j, 2)
        return pltpu.make_async_copy(s.o_p.at[i], s.pbuf.at[slot], s.psem.at[slot])

    steps = nrow * (H // 2)
    p_copy_in(0).start()

    def turn(rr, n, cq, ck):
        do = s.dctx[rr, cq]
        s.qt[:, 0:n] = do.T
        s.vt[:, 0:n] = (-do.astype(F32) * s.ctx[rr, cq].astype(F32)).astype(BF).T
        s.kt[:, 0:n] = s.mixed[rr, ck].T

    def back_tile(qr, kr, qa, ka, kw, cq, ck, cv, e):
        values = jnp.concatenate([s.mixed[kr, cv], jnp.ones((kw, 128), BF)], 1)
        grads = jnp.concatenate([two(s.qt[:, qa], 0), two(s.vt[:, qa], 0)], 0)
        ds = (e.astype(F32) * nn(values, grads)).astype(BF)
        dk = nn(ds, two(s.mixed[qr, cq], 1))
        dv = nn(e, two(s.dctx[qr, cq], 1))
        dq = (diagonal(nn(s.kt[:, ka], ds)).T * 0.125).astype(BF)
        return dq, dk, dv

    def att_back(j, _):
        g, rest = j // (2 * nrow), lax.rem(j, 2 * nrow)
        r = rest // 2
        hp = 2 * g + lax.rem(rest, 2)
        slot = lax.rem(j, 2)

        @pl.when(j + 1 < steps)
        def _():
            p_copy_in(j + 1).start()

        p_copy_in(j).wait()
        cq, ck, cv = pair_cols(hp)
        base = r * LEN

        def rws(a, n):
            return rows_at(base + a, n, 128)

        turn(rws(0, LEN), LEN, cq, ck)
        s.dka[...] = jnp.zeros_like(s.dka)
        s.dva[...] = jnp.zeros_like(s.dva)
        for qs, ks, kw, off in TILES:
            dq, dk, dv = back_tile(
                rws(qs, 128), rws(ks, kw), slice(qs, qs + 128), slice(ks, ks + kw), kw, cq, ck, cv,
                s.pbuf[slot, off : off + kw, :],
            )
            s.dq[qs : qs + 128, :] = dq
            s.dka[ks : ks + kw, :] += dk
            s.dva[ks : ks + kw, :] += dv
        s.mixed[rws(0, LEN), cq] = s.dq[...]
        s.mixed[rws(0, LEN), ck] = (s.dka[...] * 0.125).astype(BF)
        s.mixed[rws(0, LEN), cv] = s.dva[...].astype(BF)
        return 0

    def att_back_q(hp, _):
        cq, ck, cv = pair_cols(hp)
        rr = slice(NP, T)
        turn(rr, NQ, cq, ck)
        dq, dk, dv = back_tile(rr, rr, slice(0, NQ), slice(0, NQ), NQ, cq, ck, cv, s.pq[hp])
        s.mixed[rr, cq] = dq
        s.mixed[rr, ck] = (dk * 0.125).astype(BF)
        s.mixed[rr, cv] = dv.astype(BF)
        return 0

    lax.fori_loop(0, H // 2, att_back_q, 0)

    groups = (s.fb, s.gb, s.ctx)

    def group_grad(g):
        for w in range(3):
            c = w * D + g * 256
            groups[g][0:D, w * 256 : w * 256 + 256] = tn(s.x[...], s.mixed[:, c : c + 256]).astype(BF)

    for g in range(3):

        @functools.partial(loop, 'att%d' % g, 2 * nrow)
        def _(j, _, g=g):
            att_back(2 * nrow * g + j, 0)

        group_grad(g)
        if sums:
            (ring_1, ring_2, ring_3)[g].start(*al)
    for w, k in ((0, 0), (2, 1)):
        s.vr[k : k + 1, :] = jnp.sum(s.mixed[:, w * D : w * D + D].astype(F32), axis=0, keepdims=True)

    if sums:
        pad = jnp.zeros((120, 128), F32)
        few = lax.broadcasted_iota(jnp.int32, (128, 128), 1) < 8
        for i in range(D // 128):
            rr = slice(i * 128, i * 128 + 128)
            s.vcol[rr, :] = jnp.where(few, jnp.concatenate([s.vr[:, rr], pad], 0).T, s.vcol[rr, :])
        s.misc[:, 128:256] = s.vcol[...].astype(BF)
        ring_m.start(*al)

    def dx_body(t, _):
        rr = at(t, TT)
        s.gs[rr, :] = s.gs[rr, :] + nt(s.mixed[rr, :], s.wqkv[...])
        return 0

    loop('dx', T // TT, dx_body)
    outs = [
        pltpu.make_async_copy(s.gs.at[0:NP], s.o_gp, s.osem.at[2]),
        pltpu.make_async_copy(s.gs.at[NP:T], s.o_gq, s.osem.at[3]),
    ]
    if not sums:
        outs += [
            pltpu.make_async_copy(s.wdn, s.o_dn, s.osem.at[4]),
            pltpu.make_async_copy(s.wup, s.o_up, s.osem.at[5]),
            pltpu.make_async_copy(s.wout, s.o_out, s.osem.at[6]),
            pltpu.make_async_copy(s.ctx.at[0:D], s.o_q.at[0], s.osem.at[7]),
            pltpu.make_async_copy(s.fb.at[0:D], s.o_q.at[1], s.osem.at[8]),
            pltpu.make_async_copy(s.gb.at[0:D], s.o_q.at[2], s.osem.at[9]),
            pltpu.make_async_copy(s.misc, s.o_misc, s.osem.at[10]),
        ]
        s.o_bup[...] = s.bup[0:1, :]
        s.o_vr[...] = s.vr[...]
    for c in outs:
        c.start()
    if sums:
        ring_3.to_b(*al)
        ring_m.to_b(*al)
        ring_o.to_core()
        ring_u.out(put_in(s.o_up))
        ring_1.to_core()
        ring_o.out(put_in(s.o_out))
        ring_3.to_z(*al)
        ring_m.to_z(*al)
        ring_2.to_core()
        ring_1.out(put_group(0))
        ring_2.out(put_group(1))
        ring_3.to_core()
        ring_m.to_core()
        ring_3.out(put_group(2))
        ring_m.out(put_in(s.o_misc))
        for r in rings:
            r.finish()
    for c in q_copies + l_copies + g_copies + loss_copies:
        c.wait_send()
    for c in loss_copies:
        c.wait_recv()
    if cfg.loss_here:
        s.o_loss[...] = jnp.sum(s.ls[...], axis=0)
    else:
        s.o_loss[...] = s.ls[0]
    for c in [o_pe, o_qe] + outs:
        c.wait()


def finish_kernel(names, *refs):
    s = Space()
    for name, ref in zip(names, refs):
        setattr(s, name, ref)
    pairs = ((s.pe, s.o_pe), (s.qe, s.o_qe), (s.gp, s.o_gp), (s.gq, s.o_gq))
    pairs += ((s.dn, s.o_dn), (s.up, s.o_up), (s.out, s.o_out), (s.qkv, s.o_qkv))
    ways = []
    for (src, dst), buf in zip(pairs, (s.bpe, s.bqe, s.bgp, s.bgq, s.bdn, s.bup, s.bout, s.bqkv)):
        n = src.shape[0] // 4 if src.shape[0] > 512 else src.shape[0]
        for i in range(src.shape[0] // n):
            k = len(ways)
            rr = slice(i * n, i * n + n)
            ways.append(
                (
                    pltpu.make_async_copy(src.at[rr], buf.at[rr], s.sem.at[0, k]),
                    pltpu.make_async_copy(buf.at[rr], dst.at[rr], s.sem.at[1, k]),
                )
            )
    for c, _ in ways:
        c.start()
    s.o_loss[...] = s.loss[0, 0]
    s.o_proj[...] = s.misc[:, 0:128]
    q = s.misc.shape[0]
    s.sq[...] = jnp.zeros_like(s.sq)
    s.sq[0:q, :] = s.misc[:, 128:256]
    s.sq[...] = s.sq[...].T
    for k in range(8):
        getattr(s, "o_v%d" % k)[...] = s.sq[k, 0:q]
    s.o_bup[...] = jnp.concatenate([s.sq[8 + k : 9 + k, 0:q] for k in range(4)], 1)[0]
    for c, d in ways:
        c.wait()
        d.start()
    for _, d in ways:
        d.wait()


def finish(o):
    sd = jax.ShapeDtypeStruct
    any_spec = pl.BlockSpec(memory_space=pl.ANY)
    vm = pl.BlockSpec(memory_space=pltpu.VMEM)
    names = ["pe", "qe", "gp", "gq", "dn", "up", "out", "qkv"]
    ins = [(n, o["o_" + n], any_spec) for n in names] + [("loss", o["o_loss"], vm), ("misc", o["o_misc"], vm)]
    outs = [("o_" + n, sd(o["o_" + n].shape, o["o_" + n].dtype), any_spec) for n in names]
    q = o["o_misc"].shape[0]
    outs += [("o_loss", sd((), F32), pl.BlockSpec(memory_space=pltpu.SMEM)), ("o_proj", sd((q, 128), F32), vm)]
    outs += [("o_v%d" % k, sd((q,), F32), vm) for k in range(8)] + [("o_bup", sd((4 * q,), F32), vm)]
    scratch = [("sq", pltpu.VMEM((128, 128), F32)), ("sem", pltpu.SemaphoreType.DMA((2, 14)))]
    scratch += [("b" + n, pltpu.VMEM(o["o_" + n].shape, o["o_" + n].dtype)) for n in names]
    all_names = [n for n, *_ in ins] + [n for n, *_ in outs] + [n for n, _ in scratch]
    res = pl.pallas_call(
        functools.partial(finish_kernel, all_names),
        out_shape=[v[1] for v in outs],
        in_specs=[v[2] for v in ins],
        out_specs=[v[2] for v in outs],
        scratch_shapes=[v for _, v in scratch],
    )(*[v[1] for v in ins])
    return dict(zip([n for n, *_ in outs], res))


def make_body(n_dp, n_psg):
    def body(
        passage_states, segment_ids, query_states, teacher_scores,
        w_qkv, bias_q, bias_v, w_out, bias_out, ln1_gain, ln1_bias,
        w_up, bias_up, w_down, bias_down, ln2_gain, ln2_bias, w_proj,
    ):
        D, FF = w_up.shape
        E = w_proj.shape[1]
        rows, length, _ = passage_states.shape
        qn, ql, _ = query_states.shape
        NP, NQ = rows * length, qn * ql
        T = NP + NQ
        cfg = Space()
        cfg.T, cfg.NP, cfg.NQ, cfg.TT = T, NP, NQ, T // 4
        cfg.D, cfg.FF, cfg.qlen = D, FF, ql
        cfg.n_dp, cfg.n_psg = n_dp, n_psg
        cfg.loss_here = n_dp <= 16
        cfg.sums = n_dp == 8 and n_psg == 4
        npair = rows * (H // 2)
        any_spec = pl.BlockSpec(memory_space=pl.ANY)
        vm = pl.BlockSpec(memory_space=pltpu.VMEM)
        ins = [
            ("i_pass", passage_states.reshape(NP, D), any_spec),
            ("i_query", query_states.reshape(NQ, D), any_spec),
            ("i_seg", segment_ids, vm),
            ("i_teach", teacher_scores.T, vm),
            ("i_wqkv", w_qkv, any_spec),
            ("i_bq", bias_q, vm),
            ("i_bv", bias_v, vm),
            ("i_wout", w_out, any_spec),
            ("i_bout", bias_out, vm),
            ("i_g1", ln1_gain, vm),
            ("i_b1", ln1_bias, vm),
            ("i_wup", w_up, any_spec),
            ("i_bup", bias_up, vm),
            ("i_wdn", w_down, any_spec),
            ("i_bdn", bias_down, vm),
            ("i_g2", ln2_gain, vm),
            ("i_b2", ln2_bias, vm),
            ("i_wproj", w_proj, any_spec),
        ]
        sd = jax.ShapeDtypeStruct
        outs = [
            ("o_pe", sd((NP, E), BF), any_spec),
            ("o_qe", sd((NQ, E), BF), any_spec),
            ("o_loss", sd((8, 128), F32), vm),
            ("o_gp", sd((NP, D), F32), any_spec),
            ("o_gq", sd((NQ, D), F32), any_spec),
            ("o_p", sd((npair, PW, 256), BF), any_spec),
        ]
        n_dev = n_dp * n_psg
        if cfg.sums:
            outs += [
                ("o_dn", sd((FF // n_dev, D), F32), vm),
                ("o_up", sd((D // n_dev, FF), F32), vm),
                ("o_out", sd((D // n_dev, D), F32), vm),
                ("o_qkv", sd((D // n_dev, 3 * D), F32), vm),
                ("o_misc", sd((D // n_dev, 256), F32), vm),
            ]
        else:
            outs += [
                ("o_dn", sd((FF, D), BF), any_spec),
                ("o_up", sd((D, FF), BF), any_spec),
                ("o_out", sd((D, D), BF), any_spec),
                ("o_q", sd((3, D, D), BF), any_spec),
                ("o_misc", sd((D, 256), BF), any_spec),
                ("o_bup", sd((1, FF), F32), vm),
                ("o_vr", sd((8, D), F32), vm),
            ]
        V = pltpu.VMEM
        DMA = pltpu.SemaphoreType.DMA
        scratch = [
            ("x", V((T, D), BF)),
            ("wqkv", V((D, 3 * D), BF)),
            ("wout", V((D, D), BF)),
            ("wup", V((D, FF), BF)),
            ("wdn", V((FF, D), BF)),
            ("wproj", V((D, E), BF)),
            ("bqkv", V((8, 3 * D), F32)),
            ("vin", V((8, D), F32)),
            ("tsq", V((128, 128), F32)),
            ("mixed", V((T, 3 * D), BF)),
            ("pbuf", V((2, PW, 256), BF)),
            ("pq", V((H // 2, NQ, 256), BF)),
            ("koh", V((T, 128), BF)),
            ("qoh", V((128, T), BF)),
            ("qt", V((128, LEN), BF)),
            ("vt", V((128, LEN), BF)),
            ("kt", V((128, LEN), BF)),
            ("ctx", V((T, D), BF)),
            ("y1", V((T, D), BF)),
            ("fb", V((T, D), BF)),
            ("hid", V((T, FF), BF)),
            ("slo", V((T, FF), BF)),
            ("gs", V((T, D), F32)),
            ("gb", V((T, D), BF)),
            ("st", V((T, 128), F32)),
            ("unit", V((T, E), F32)),
            ("unitb", V((T, E), BF)),
            ("aq", V((n_psg, NQ, E), BF)),
            ("ind", V((NP, 128), BF)),
            ("tot", V((n_psg, NQ, 128), F32)),
            ("lg", V((n_psg, 2 * n_psg * qn, 128), F32)),
            ("line", V((n_psg * NQ, 128), F32)),
            ("gl", V((n_psg * qn, 128), F32)),
            ("ls", V((n_dp if cfg.loss_here else 1, 8, 128), F32)),
            ("gsim", V((n_psg * NQ, NP), BF)),
            ("qs", V((n_psg, NQ, E), BF)),
            ("qr", V((n_psg, NQ, E), BF)),
            ("own", V((NQ, E), F32)),
            ("gp", V((T, E), BF)),
            ("misc", V((D, 256), BF)),
            ("vr", V((8, D), F32)),
            ("vcol", V((D, 128), F32)),
            ("bup", V((8, FF), F32)),
            ("dctx", V((T, D), BF)),
            ("dq", V((LEN, 128), BF)),
            ("dka", V((LEN, 128), F32)),
            ("dva", V((LEN, 128), F32)),
            ("lsem", DMA((7,))),
            ("psem", DMA((2,))),
            ("osem", DMA((11,))),
            ("ss", DMA((3, n_psg))),
            ("rs", DMA((3, n_psg))),
            ("lss", DMA((n_dp,))),
            ("lrs", DMA((n_dp,))),
        ]
        if cfg.sums:
            b, e = D // 16, FF // 16
            scratch += [
                ("tcol", V((384, 128), F32)),
                ("mrecv", V((31 * b, 128), BF)),
                ("fd", V((e, D // 2), F32)),
                ("rd", V((e // 2, D // 2), F32)),
                ("fu", V((b, FF // 2), F32)),
                ("ru", V((b // 2, FF // 2), F32)),
                ("fq", V((4, b, D // 2), F32)),
                ("rq", V((4, b // 2, D // 2), F32)),
                ("fm", V((b, 128), F32)),
                ("rm", V((b // 2, 128), F32)),
                ("gss", DMA((7, 18))),
                ("grs", DMA((7, 18))),
                ("arecv", V((8 * e, D // 2), BF)),
                ("credit", pltpu.SemaphoreType.REGULAR((5,))),
                ("epoch", pltpu.SemaphoreType.REGULAR((2,))),
            ]
        cfg.names = [a for a, *_ in ins] + [a for a, *_ in outs] + [a for a, _ in scratch]
        res = pl.pallas_call(
            functools.partial(kernel, cfg),
            out_shape=[o[1] for o in outs],
            in_specs=[i[2] for i in ins],
            out_specs=[o[2] for o in outs],
            scratch_shapes=[v for _, v in scratch],
            compiler_params=pltpu.CompilerParams(
                collective_id=0, has_side_effects=True, vmem_limit_bytes=64 * 1024 * 1024 - 65536
            ),
        )(*[i[1] for i in ins])
        o = dict(zip([a for a, *_ in outs], res))
        if cfg.sums:
            o = finish(o)
            loss = o["o_loss"]
        else:
            loss = o["o_loss"][0, 0]
        if not cfg.loss_here:
            loss = lax.psum(loss, "dp")
        head = (
            o["o_pe"].reshape(rows, length, E),
            o["o_qe"].reshape(qn, ql, E),
            loss,
            o["o_gp"].reshape(rows, length, D),
            o["o_gq"].reshape(qn, ql, D),
        )
        if cfg.sums:
            vec = [o["o_v%d" % k] for k in range(8)]
            g_qkv, g_out, g_up, g_bup, g_dn, g_proj = [
                o["o_" + k] for k in ("qkv", "out", "up", "bup", "dn", "proj")
            ]
        else:
            q3 = o["o_q"].reshape(3, D, 3, 256)
            q3 = jnp.transpose(q3, (1, 2, 0, 3)).reshape(D, 3 * D)

            def scat(v):
                return lax.psum_scatter(v, ("dp", "psg"), scatter_dimension=0, tiled=True)

            vec = scat(o["o_vr"].T)
            vec = [vec[:, k] for k in range(8)]
            g_bup = scat(o["o_bup"].reshape(-1))
            g_qkv, g_out, g_up, g_dn, g_proj = [
                scat(v.astype(F32)) for v in (q3, o["o_out"], o["o_up"], o["o_dn"], o["o_misc"][:, 0:128])
            ]
        return head + (
            g_qkv, vec[0], vec[1], g_out, vec[2], vec[3], vec[4],
            g_up, g_bup, g_dn, vec[5], vec[6], vec[7], g_proj,
        )

    return body


def solution(mesh):
    rowspec = P(("dp", "psg"))
    three = P(("dp", "psg"), None, None)
    two = P(("dp", "psg"), None)
    in_specs = (three, two, three, P("dp", "psg")) + (P(),) * 14
    out_specs = (
        three, three, P(), three, three,
        two, rowspec, rowspec, two, rowspec, rowspec, rowspec,
        two, rowspec, two, rowspec, rowspec, rowspec, two,
    )
    body = make_body(mesh.shape["dp"], mesh.shape["psg"])
    return jax.shard_map(body, mesh=mesh, in_specs=in_specs, out_specs=out_specs, check_vma=False)
```

```python
import functools

import jax
import jax.numpy as jnp
from jax import lax
from jax.experimental import pallas as pl
from jax.experimental.pallas import tpu as pltpu
from jax.sharding import PartitionSpec as P

F32 = jnp.float32
BF = jnp.bfloat16
MESH = pl.DeviceIdType.MESH
H = 12
HD = 64
SEGS = 3
LOG2E = 1.4426950408889634
SHARP = 0.1
TILES = ((0, 0, 256, 0), (128, 0, 384, 256), (256, 128, 384, 640), (384, 256, 256, 1024))
PW = 1280
LEN = 512


def nn(a, b):
    return lax.dot_general(a, b, (((1,), (0,)), ((), ())), preferred_element_type=F32)


def nt(a, b):
    return lax.dot_general(a, b, (((1,), (1,)), ((), ())), preferred_element_type=F32)


def tn(a, b):
    return lax.dot_general(a, b, (((0,), (0,)), ((), ())), preferred_element_type=F32)


def at(i, n):
    return pl.ds(pl.multiple_of(i * n, n), n)


def rows_at(start, n, unit):
    return pl.ds(pl.multiple_of(start, unit), n)


class Space:
    pass


def norm_stats(v):
    mean = jnp.mean(v, -1, keepdims=True)
    c = v - mean
    inv = lax.rsqrt(jnp.mean(c * c, -1, keepdims=True) + 1e-12)
    return c * inv, inv


class Ring:
    def __init__(self, s, u, g, b, half, places, f, rd, where, stride=None, off=0):
        self.s, self.u, self.g, self.b, self.half = s, u, g, b, half
        self.stride, self.off = stride or half, off
        self.c_at, self.a_at, self.b_at, self.z_at = places
        self.f, self.rd = f, rd
        dp, psg = where
        self.z, self.x, self.y, self.c = dp // 2, lax.rem(dp, 2), psg // 2, lax.rem(psg, 2)
        self.core = {"psg": self.y * 2 + 1 - self.c}
        self.xn = {"dp": self.z * 2 + 1 - self.x}
        self.yn = {"psg": (1 - self.y) * 2 + self.c}
        self.zn = [{"dp": lax.rem(self.z + k, 4) * 2 + self.x} for k in range(1, 4)]

    def cols(self, c):
        return pl.ds(pl.multiple_of(c * self.stride + self.off, 128), self.half)

    def part(self, row, n, c):
        return self.g.at[pl.ds(pl.multiple_of(row * self.b, 16), n * self.b), self.cols(c)]

    def remote(self, i, src, dst, dev):
        return pltpu.make_async_remote_copy(
            src_ref=src, dst_ref=dst, send_sem=self.s.gss.at[self.u, i], recv_sem=self.s.grs.at[self.u, i],
            device_id=dev, device_id_type=MESH,
        )

    def copy_c(self, z):
        return self.remote(z, self.part(4 * z, 4, 1 - self.c), self.c_at(z), self.core)

    def copy_a(self, z):
        if z % 2 == 0:
            return [self.remote(4 + z // 2, self.part(4 * z + 2 * (1 - self.x), 2, self.c), self.a_at(z, 0, 2), self.xn)]
        return [
            self.remote(
                6 + z - 1 + x, self.part(4 * z + 2 * x + 1 - self.y, 1, self.c), self.a_at(z, x, 1), self.yn
            )
            for x in range(2)
        ]

    def copy_b(self, z):
        if z % 2 == 0:
            return self.remote(10 + z, self.part(4 * z + 2 * self.x + 1 - self.y, 1, self.c), self.b_at(z), self.yn)
        return self.remote(10 + z, self.part(4 * z + 2 * (1 - self.x) + self.y, 1, self.c), self.b_at(z), self.xn)

    def copy_z(self, k):
        z = lax.rem(self.z + k + 1, 4)
        return self.remote(14 + k, self.part(4 * z + 2 * self.x + self.y, 1, self.c), self.z_at(k), self.zn[k])

    def send_z(self, z):
        k = lax.rem(z - self.z + 3, 4)

        @pl.when(z != self.z)
        def _():
            self.s_z(z, k).start()

    def s_z(self, z, k):
        return pltpu.make_async_remote_copy(
            src_ref=self.part(4 * z + 2 * self.x + self.y, 1, self.c), dst_ref=self.z_at(k),
            send_sem=self.s.gss.at[self.u, 14 + k], recv_sem=self.s.grs.at[self.u, 14 + k],
            device_id={"dp": z * 2 + self.x}, device_id_type=MESH,
        )

    def copy_d(self):
        h = self.b // 2
        src = self.f.at[pl.ds(pl.multiple_of((1 - self.c) * h, 8), h), :]
        return self.remote(17, src, self.rd, self.core)

    def add(self, part, got):
        part[...] = part[...] + got[...]

    def start(self, *zs):
        for z in zs:
            self.copy_c(z).start()

    def to_a(self, *zs):
        for z in zs:
            self.copy_c(z).wait_recv()
            self.add(self.part(4 * z, 4, self.c), self.c_at(z))
            for c in self.copy_a(z):
                c.start()

    def to_b(self, *zs):
        for z in zs:
            for c in self.copy_a(z):
                c.wait_recv()
            if z % 2 == 0:
                self.add(self.part(4 * z + 2 * self.x, 2, self.c), self.a_at(z, 0, 2))
            else:
                for x in range(2):
                    self.add(self.part(4 * z + 2 * x + self.y, 1, self.c), self.a_at(z, x, 1))
            self.copy_b(z).start()

    def to_z(self, *zs):
        for z in zs:
            self.copy_b(z).wait_recv()
            self.add(self.part(4 * z + 2 * self.x + self.y, 1, self.c), self.b_at(z))
            self.send_z(z)

    def to_core(self):
        v = self.part(4 * self.z + 2 * self.x + self.y, 1, self.c)[...].astype(F32)
        for k in range(3):
            self.copy_z(k).wait_recv()
            v = v + self.z_at(k)[...].astype(F32)
        self.f[...] = v
        self.copy_d().start()

    def out(self, put):
        self.copy_d().wait_recv()
        h = self.b // 2
        put(self.c, self.f[pl.ds(pl.multiple_of(self.c * h, 8), h), :])
        put(1 - self.c, self.rd[...])

    def finish(self):
        for z in range(4):
            self.copy_c(z).wait_send()
            for c in self.copy_a(z):
                c.wait_send()
            self.copy_b(z).wait_send()
        for k in range(3):
            self.copy_z(k).wait_send()
        self.copy_d().wait_send()


def place(ref, f, n, width):
    def ref_at(i, x=0, m=1):
        row, col = f(i)
        if not isinstance(row, int):
            return ref.at[pl.ds(pl.multiple_of(row, 16), n), col : col + width]
        return ref.at[row + x * n : row + x * n + m * n, col : col + width]

    return ref_at


def make_rings(s, cfg, where):
    D, FF = cfg.D, cfg.FF
    h, w, b, e = D // 2, FF // 2, D // 16, FF // 16
    low = D
    spots = lambda r, k: (
        place(r, lambda z: (low + 4 * b * (z % 2), (k + z // 2) * h), 4 * b, h),
        place(r, lambda z: (low + 2 * b * z, (k + 2) * h), b, h),
        place(r, lambda z: (low + b * z, (k + 3) * h), b, h),
        place(r, lambda z: (low + b * (4 + z), (k + 3) * h), b, h),
    )
    down = (
        place(s.hid, lambda z: (0, z * h), 4 * e, h),
        place(s.arecv, lambda z: (2 * e * z, 0), e, h),
        place(s.hid, lambda z: (e * z, 6 * h), e, h),
        place(s.hid, lambda z: (e * z, 7 * h), e, h),
    )
    v = w // 2
    ups = lambda k: (
        place(s.hid, lambda z: (4 * b * z, k * v), 4 * b, v),
        place(s.hid, lambda z: (b * (8 * k + 2 * z), 2 * v), b, v),
        place(s.slo, lambda z: (b * z, k * v), b, v),
        place(s.slo, lambda z: (b * (4 + z), k * v), b, v),
    )
    second = (
        place(s.y1, lambda z: (4 * b * z, 0), 4 * b, h),
        place(s.y1, lambda z: (low + 2 * b * z, 0), b, h),
        place(s.y1, lambda z: (b * z, h), b, h),
        place(s.y1, lambda z: (b * (4 + z), h), b, h),
    )
    third = (
        place(s.y1, lambda z: (b * (7 + 4 * z), h), 4 * b, h),
        place(s.hid, lambda z: (low + 2 * b * z, 4 * h), b, h),
        place(s.hid, lambda z: (low + b * z, 5 * h), b, h),
        place(s.hid, lambda z: (low + b * (4 + z), 5 * h), b, h),
    )
    small = (
        place(s.mrecv, lambda z: (4 * b * z, 0), 4 * b, 128),
        place(s.mrecv, lambda z: (b * (16 + 2 * z), 0), b, 128),
        place(s.mrecv, lambda z: (b * (24 + z), 0), b, 128),
        place(s.mrecv, lambda z: (b * (28 + z), 0), b, 128),
    )
    mk = lambda u, g, bb, half, places, f, rd: Ring(s, u, g, bb, half, places, f, rd, where)
    return (
        mk(0, s.wdn, e, h, down, s.fd, s.rd),
        (
            Ring(s, 1, s.wup, b, v, ups(0), s.fu.at[0], s.ru.at[0], where, w, 0),
            Ring(s, 7, s.wup, b, v, ups(1), s.fu.at[1], s.ru.at[1], where, w, v),
        ),
        mk(2, s.wout, b, h, spots(s.hid, 0), s.fq.at[0], s.rq.at[0]),
        mk(3, s.fb, b, h, spots(s.slo, 0), s.fq.at[1], s.rq.at[1]),
        mk(4, s.gb, b, h, second, s.fq.at[2], s.rq.at[2]),
        mk(5, s.ctx, b, h, third, s.fq.at[3], s.rq.at[3]),
        mk(6, s.misc, b, 128, small, s.fm, s.rm),
    )


def kernel(cfg, *refs):
    s = Space()
    for name, ref in zip(cfg.names, refs):
        setattr(s, name, ref)
    T, NP, NQ, TT = cfg.T, cfg.NP, cfg.NQ, cfg.TT
    D, FF = cfg.D, cfg.FF
    nrow = NP // LEN
    me_dp = lax.axis_index("dp")
    me_psg = lax.axis_index("psg")
    n_psg, n_dp = cfg.n_psg, cfg.n_dp

    def load(k, src, dst):
        c = pltpu.make_async_copy(src, dst, s.lsem.at[k])
        if k < 3:
            c.start()
        return c

    l_x = load(0, s.i_pass, s.x.at[0:NP])
    l_q = load(1, s.i_query, s.x.at[NP:T])
    l_wqkv = load(2, s.i_wqkv, s.wqkv)
    l_wout = load(3, s.i_wout, s.wout)
    l_wup = load(4, s.i_wup, s.wup)
    l_wdn = load(5, s.i_wdn, s.wdn)
    l_wpj = load(6, s.i_wproj, s.wproj)

    for k, v in enumerate((s.i_bout, s.i_g1, s.i_b1, s.i_bdn, s.i_g2, s.i_b2)):
        s.vin[k : k + 1, :] = v[...][None, :]
    v_bout, v_g1, v_b1, v_bdn, v_g2, v_b2 = [s.vin.at[k : k + 1] for k in range(6)]
    bar = pltpu.get_barrier_semaphore()
    peers = []
    for k in range(1, n_psg):
        peers.append({"psg": lax.rem(me_psg + k, n_psg)})
    if cfg.loss_here:
        for k in range(1, n_dp):
            peers.append({"dp": lax.rem(me_dp + k, n_dp)})
    for p in peers:
        pl.semaphore_signal(bar, inc=1, device_id=p, device_id_type=MESH)

    sums = cfg.sums
    if sums:
        ring_d, (ring_u, ring_v), ring_o, ring_1, ring_2, ring_3, ring_m = make_rings(s, cfg, (me_dp, me_psg))
        rings = (ring_d, ring_u, ring_v, ring_o, ring_1, ring_2, ring_3, ring_m)

        def epoch_signal(k):
            for dev in [ring_d.core, ring_d.xn, ring_d.yn] + ring_d.zn:
                pl.semaphore_signal(s.epoch.at[k], inc=1, device_id=dev, device_id_type=MESH)

        def give_credit(z):
            pl.semaphore_signal(s.credit.at[z], inc=1, device_id=ring_d.core, device_id_type=MESH)

        def take_credit(z):
            pl.semaphore_wait(s.credit.at[z], 1)
            ring_d.start(z)

        def start_up():
            pl.semaphore_wait(s.credit.at[4], 1)
            ring_u.start(0, 1, 2, 3)

        def epoch_wait(k):
            pl.semaphore_wait(s.epoch.at[k], 6)

    plan = {}

    def loop(name, n, body):
        todo = plan.get(name, {})

        def with_plan(i, carry):
            body(i, carry)
            for k in sorted(todo):

                @pl.when(i == k)
                def _(k=k):
                    for act in todo[k]:
                        act()

            return 0

        lax.fori_loop(0, n, with_plan, 0)

    def put_in(ref):
        def put(c, v):
            ref[:, pl.ds(pl.multiple_of(c * v.shape[1], 128), v.shape[1])] = v

        return put

    def put_up(k):
        def put(c, v):
            n = v.shape[1]
            s.o_up[:, pl.ds(pl.multiple_of((2 * c + k) * n, 128), n)] = v

        return put

    def put_group(g):
        def put(c, v):
            for i in range(v.shape[1] // 128):
                k = c * (v.shape[1] // 128) + i
                col = (k // 2) * D + g * 256 + lax.rem(k, 2) * 128
                s.o_qkv[:, pl.ds(pl.multiple_of(col, 128), 128)] = v[:, i * 128 : i * 128 + 128]

        return put

    bounds = []
    for r in range(nrow):
        seg = s.i_seg[r : r + 1, :]
        bounds.append(
            (
                jnp.sum(jnp.where(seg < 1, 1.0, 0.0), axis=1, keepdims=True),
                jnp.sum(jnp.where(seg < 2, 1.0, 0.0), axis=1, keepdims=True),
            )
        )

    s.bqkv[...] = jnp.zeros_like(s.bqkv)
    s.bqkv[0:1, 0:D] = s.i_bq[...][None, :]
    s.bqkv[0:1, 2 * D : 3 * D] = s.i_bv[...][None, :]
    s.bup[0:1, :] = s.i_bup[...][None, :]
    l_x.wait()
    l_q.wait()
    l_wqkv.wait()
    for c in (l_wout, l_wup, l_wdn, l_wpj):
        c.start()

    def qkv_body(n, _):
        c = at(n, 256)
        s.mixed[:, c] = (nn(s.x[...], s.wqkv[:, c]) + s.bqkv[0:1, c]).astype(BF)
        return 0

    lax.fori_loop(0, 3 * D // 256, qkv_body, 0)

    scale = 0.125 * LOG2E
    li = lax.broadcasted_iota(jnp.int32, (LEN, 128), 1).astype(F32)
    si = lax.broadcasted_iota(jnp.int32, (128, LEN), 0).astype(F32)
    for r in range(nrow):
        b0, b1 = bounds[r]
        rr = slice(r * LEN, (r + 1) * LEN)
        ti = lax.broadcasted_iota(jnp.int32, (LEN, 128), 0).astype(F32)
        seg = jnp.where(ti >= b0, 1.0, 0.0) + jnp.where(ti >= b1, 1.0, 0.0)
        s.koh[rr, :] = jnp.where(seg == li, 1.0, 0.0).astype(BF)
        ti = lax.broadcasted_iota(jnp.int32, (128, LEN), 1).astype(F32)
        seg = jnp.where(ti >= b0, 1.0, 0.0) + jnp.where(ti >= b1, 1.0, 0.0)
        s.qoh[:, rr] = jnp.where(jnp.logical_or(seg == si, si >= SEGS), 0.0, -1e30).astype(BF)
    ql = cfg.qlen
    ti = lax.broadcasted_iota(jnp.int32, (NQ, 128), 0)
    li = lax.broadcasted_iota(jnp.int32, (NQ, 128), 1)
    s.koh[NP:T, :] = jnp.where(jnp.logical_and(ti >= li * ql, ti < li * ql + ql), 1.0, 0.0).astype(BF)
    si = lax.broadcasted_iota(jnp.int32, (128, NQ), 0)
    ti = lax.broadcasted_iota(jnp.int32, (128, NQ), 1)
    mine = jnp.logical_and(ti >= si * ql, ti < si * ql + ql)
    s.qoh[:, NP:T] = jnp.where(jnp.logical_or(mine, si * ql >= NQ), 0.0, -1e30).astype(BF)
    one_b, zero_b = jnp.ones((), BF), jnp.zeros((), BF)

    def two(v, axis):
        keep = lax.broadcasted_iota(jnp.int32, v.shape, axis) < 64
        return jnp.concatenate([jnp.where(keep, v, zero_b), jnp.where(keep, zero_b, v)], 1 - axis)

    def diagonal(v):
        return jnp.concatenate([v[0:64, 0:128], v[64:128, 128:256]], 0)

    def att_tile(qr, kr, qa, ka, kw, cq, ck, cv, keep_e):
        keys = jnp.concatenate([s.mixed[kr, ck], s.koh[kr, :]], 1)
        far = s.qoh[:, qr]
        queries = jnp.concatenate([two(s.qt[:, qa], 0), jnp.concatenate([far, far], 1)], 0)
        sc = nn(keys, queries)
        e = jnp.exp2(sc * scale - jnp.max(sc, axis=0, keepdims=True) * scale).astype(BF)
        keep_e(e)
        o = nn(jnp.concatenate([s.vt[:, ka], jnp.ones((16, kw), BF)], 0), e)
        inv = 1.0 / o[128:129, :]
        s.ctx[qr, cq] = diagonal(o[0:128, :] * inv).T.astype(BF)
        s.dctx[qr, cq] = diagonal(jnp.broadcast_to(inv, (128, 256))).T.astype(BF)

    def pair_cols(hp):
        return at(hp, 128), at(hp + D // 128, 128), at(hp + 2 * D // 128, 128)

    def p_copy_out(i, slot):
        return pltpu.make_async_copy(s.pbuf.at[slot], s.o_p.at[i], s.psem.at[slot])

    def att_body(i, _):
        r, hp = i // (H // 2), lax.rem(i, H // 2)
        slot = lax.rem(i, 2)

        @pl.when(i >= 2)
        def _():
            p_copy_out(i - 2, slot).wait()

        cq, ck, cv = pair_cols(hp)
        whole = rows_at(r * LEN, LEN, LEN)
        s.qt[...] = s.mixed[whole, cq].T
        s.vt[...] = s.mixed[whole, cv].T
        for qs, ks, kw, off in TILES:

            def keep_e(e):
                s.pbuf[slot, off : off + kw, :] = e

            qr, kr = rows_at(r * LEN + qs, 128, 128), rows_at(r * LEN + ks, kw, 128)
            att_tile(qr, kr, slice(qs, qs + 128), slice(ks, ks + kw), kw, cq, ck, cv, keep_e)
        p_copy_out(i, slot).start()
        return 0

    lax.fori_loop(0, nrow * (H // 2), att_body, 0)

    def att_q_body(hp, _):
        cq, ck, cv = pair_cols(hp)
        s.qt[:, 0:NQ] = s.mixed[NP:T, cq].T
        s.vt[:, 0:NQ] = s.mixed[NP:T, cv].T

        def keep_e(e):
            s.pq[hp] = e

        att_tile(slice(NP, T), slice(NP, T), slice(0, NQ), slice(0, NQ), NQ, cq, ck, cv, keep_e)
        return 0

    lax.fori_loop(0, H // 2, att_q_body, 0)
    last = nrow * (H // 2)
    p_copy_out(last - 2, (last - 2) % 2).wait()
    p_copy_out(last - 1, (last - 1) % 2).wait()

    l_wout.wait()

    def out_body(t, _):
        rr = at(t, T // 2)
        v = nn(s.ctx[rr, :], s.wout[...]) + v_bout[...] + s.x[rr, :].astype(F32)
        y, inv = norm_stats(v)
        s.y1[rr, :] = y.astype(BF)
        s.st[rr, 0:1] = inv
        s.fb[rr, :] = (y * v_g1[...] + v_b1[...]).astype(BF)
        return 0

    lax.fori_loop(0, 2, out_body, 0)

    l_wup.wait()

    def up_body(n, _):
        c = at(n, 256)
        for rr in (slice(0, T),):
            h = nn(s.fb[rr, :], s.wup[:, c]) + s.bup[0:1, c]
            cdf = 0.5 * (1.0 + lax.erf(h * 0.7071067811865476))
            s.hid[rr, c] = (h * cdf).astype(BF)
            s.slo[rr, c] = (cdf + h * jnp.exp2(h * h * (-0.5 * LOG2E)) * 0.3989422804014327).astype(BF)
        return 0

    lax.fori_loop(0, FF // 256, up_body, 0)

    def remote(src, dst, ssem, rsem, dev):
        return pltpu.make_async_remote_copy(
            src_ref=src, dst_ref=dst, send_sem=ssem, recv_sem=rsem, device_id=dev, device_id_type=MESH
        )

    l_wdn.wait()
    l_wpj.wait()

    q_copies = [
        remote(s.unitb.at[NP:T], s.aq.at[k], s.ss.at[0, k], s.rs.at[0, k], {"psg": lax.rem(me_psg + k, n_psg)})
        for k in range(1, n_psg)
    ]

    def down_body(t, _):
        rr = at(1 - t, T // 2)
        first = s.y1[rr, :].astype(F32) * v_g1[...] + v_b1[...]
        v = first + (nn(s.hid[rr, :], s.wdn[...]) + v_bdn[...])
        y, inv = norm_stats(v)
        s.gs[rr, :] = y
        s.st[rr, 1:2] = inv
        sec = (y * v_g2[...] + v_b2[...]).astype(BF)
        s.gb[rr, :] = sec
        pj = nn(sec, s.wproj[...])
        il = lax.rsqrt(jnp.sum(pj * pj, -1, keepdims=True) + 1e-06)
        s.st[rr, 2:3] = il
        u = pj * il
        s.unit[rr, :] = u
        s.unitb[rr, :] = u.astype(BF)

        @pl.when(t == 0)
        def _():
            pl.semaphore_wait(bar, len(peers))
            for c in q_copies:
                c.start()

        return 0

    lax.fori_loop(0, 2, down_body, 0)

    o_pe = pltpu.make_async_copy(s.unitb.at[0:NP], s.o_pe, s.osem.at[0])
    o_pe.start()
    o_qe = pltpu.make_async_copy(s.unitb.at[NP:T], s.o_qe, s.osem.at[1])
    o_qe.start()

    s.aq[0] = s.unitb[NP:T, :]

    for r in range(nrow):
        b0, b1 = bounds[r]
        ti = lax.broadcasted_iota(jnp.int32, (LEN, 128), 0).astype(F32)
        li = lax.broadcasted_iota(jnp.int32, (LEN, 128), 1).astype(F32)
        pid = SEGS * r + jnp.where(ti >= b0, 1.0, 0.0) + jnp.where(ti >= b1, 1.0, 0.0)
        s.ind[r * LEN : (r + 1) * LEN, :] = jnp.where(pid == li, 1.0, 0.0).astype(BF)
    count = jnp.sum(s.ind[...].astype(F32), axis=0, keepdims=True)
    slots = nrow * SEGS
    valid = lax.broadcasted_iota(jnp.int32, (1, 128), 1) < slots
    count = jnp.where(valid, count, 1.0)
    nqg = NQ // ql
    s.lg[0] = jnp.zeros(s.lg.shape[1:], F32)

    def powers(k):
        sim = nt(s.aq[k], s.unitb[0:NP, :])
        return jnp.exp2((sim - 1.0) * (LOG2E / SHARP))

    for k in range(n_psg):
        if k:
            q_copies[k - 1].wait_recv()
        pw = powers(k)
        hi = pw.astype(BF)
        lo = (pw - hi.astype(F32)).astype(BF)
        tot = nn(hi, s.ind[...]) + nn(lo, s.ind[...])
        tot = jnp.where(valid, tot, 1.0)
        s.tot[k] = tot
        line = jnp.log(tot / count) + 1.0 / SHARP
        line = jnp.where(valid, line, 0.0)
        src = lax.rem(me_psg + n_psg - k, n_psg)
        s.line[rows_at(src * NQ, NQ, NQ), :] = line

    nq_all = n_psg * nqg
    qrow = lax.broadcasted_iota(jnp.int32, (nq_all, n_psg * NQ), 0) * ql
    qcol = lax.broadcasted_iota(jnp.int32, (nq_all, n_psg * NQ), 1)
    sel = jnp.where(jnp.logical_and(qcol >= qrow, qcol < qrow + ql), 1.0, 0.0).astype(BF)
    line = s.line[...]
    hi = line.astype(BF)
    line = line - hi.astype(F32)
    mid = line.astype(BF)
    lo = (line - mid.astype(F32)).astype(BF)
    s.lg[0, 0:nq_all, :] = nn(sel, hi) + (nn(sel, mid) + nn(sel, lo))
    s.tsq[...] = jnp.zeros_like(s.tsq)
    s.tsq[0:slots, 0:nq_all] = s.i_teach[...]
    s.lg[0, nq_all : 2 * nq_all, :] = s.tsq[...].T[0:nq_all, :]
    l_copies = []
    for k in range(1, n_psg):
        c = remote(
            s.lg.at[0], s.lg.at[k], s.ss.at[1, k], s.rs.at[1, k], {"psg": lax.rem(me_psg + k, n_psg)}
        )
        c.start()
        l_copies.append(c)
    for c in l_copies:
        c.wait_recv()
    ok = valid[None]
    lg = s.lg[...]
    half = nq_all

    def log_norm(v):
        vm = jnp.where(valid[None], v, -1e30)
        top = jnp.max(jnp.max(vm, axis=-1, keepdims=True), axis=0, keepdims=True)
        sh = v - top
        ex = jnp.where(valid[None], jnp.exp(sh), 0.0)
        tot = jnp.sum(jnp.sum(ex, axis=-1, keepdims=True), axis=0, keepdims=True)
        return sh - jnp.log(tot)

    stu = log_norm(lg[:, 0:half, :])
    tea = log_norm(lg[:, half : 2 * half, :])
    pt = jnp.exp(tea)
    kl = jnp.where(ok, pt * (tea - stu), 0.0)
    group_sum = jnp.sum(jnp.sum(jnp.sum(kl, axis=0), axis=-1, keepdims=True), axis=0, keepdims=True)
    s.ls[0] = jnp.broadcast_to(group_sum / n_dp, (8, 128))
    loss_copies = []
    if cfg.loss_here:
        for k in range(1, n_dp):
            c = remote(
                s.ls.at[0], s.ls.at[k], s.lss.at[k], s.lrs.at[k], {"dp": lax.rem(me_dp + k, n_dp)}
            )
            c.start()
            loss_copies.append(c)
    s.gl[...] = jnp.where(valid, (jnp.exp(stu[0]) - pt[0]) / n_dp, 0.0)
    for q in range(nq_all):
        s.line[q * ql : q * ql + ql, :] = jnp.broadcast_to(s.gl[q : q + 1, :], (ql, 128))

    g_copies = []
    for k in list(range(1, n_psg)) + [0]:
        pw = powers(k)
        src = lax.rem(me_psg + n_psg - k, n_psg)
        ratio = s.line[rows_at(src * NQ, NQ, NQ), :] / s.tot[k]
        ratio = ratio * (1.0 / SHARP)
        hi = ratio.astype(BF)
        lo = (ratio - hi.astype(F32)).astype(BF)
        g = ((nt(hi, s.ind[...]) + nt(lo, s.ind[...])) * pw).astype(BF)
        s.gsim[k * NQ : (k + 1) * NQ, :] = g
        qp = nn(g, s.unitb[0:NP, :])
        if k:
            s.qs[k] = qp.astype(BF)
            c = remote(s.qs.at[k], s.qr.at[k], s.ss.at[2, k], s.rs.at[2, k], {"psg": src})
            c.start()
            g_copies.append(c)
        else:
            s.own[...] = qp

    def unit_back(gu, rr):
        u = s.unit[rr, :]
        return (s.st[rr, 2:3] * (gu - u * jnp.sum(gu * u, -1, keepdims=True))).astype(BF)

    aq = s.aq[...].reshape(n_psg * NQ, 128)
    for m in range(NP // 256):
        rr = slice(m * 256, m * 256 + 256)
        gu = tn(s.gsim[:, rr], aq)
        s.gp[rr, :] = unit_back(gu, rr)
    s.vcol[...] = tn(s.gb[0:NP, :], s.gp[0:NP, :])

    if sums:
        al = (0, 1, 2, 3)

        def at_step(name, k, f, *args):
            plan.setdefault(name, {}).setdefault(k, []).append(lambda: f(*args))

        for z in range(4):
            at_step("ff", 3 * z + 2, give_credit, z)
        for z in range(3):
            at_step("ff", 3 * z + 3, take_credit, z)
            at_step("ff", 3 * z + 5, ring_d.to_a, z)
        at_step("norm1", 0, epoch_wait, 0)
        at_step("norm1", 0, ring_d.to_b, 0)
        at_step("norm1", 0, ring_d.to_a, 3)
        at_step("norm1", 0, give_credit, 4)
        at_step("norm1", 1, ring_d.to_b, 1)
        at_step("gup", 1, ring_d.to_b, 2)
        at_step("gup", 2, start_up)
        at_step("gup", 4, ring_d.to_z, 1)
        at_step("gup", 6, ring_u.to_a, *al)
        at_step("gup", 8, ring_v.start, *al)
        at_step("gup", 11, ring_d.to_b, 3)
        at_step("dctx", 0, epoch_wait, 1)
        at_step("dctx", 0, ring_d.to_z, 0)
        at_step("dctx", 2, ring_d.to_z, 2)
        at_step("gout", 0, ring_v.to_a, *al)
        at_step("att0", 0, ring_d.to_z, 3)
        at_step("att0", 0, ring_u.to_b, *al)
        at_step("att0", 1, ring_o.to_a, *al)
        at_step("att1", 0, ring_v.to_b, *al)
        at_step("att1", 0, ring_1.to_a, *al)
        at_step("att1", 0, ring_u.to_z, *al)
        at_step("att1", 1, ring_d.to_core)
        at_step("att1", 2, ring_o.to_b, *al)
        at_step("att2", 0, ring_2.to_a, *al)
        at_step("att2", 0, ring_v.to_z, *al)
        at_step("att2", 0, ring_d.out, put_in(s.o_dn))
        at_step("att2", 1, ring_1.to_b, *al)
        at_step("att2", 2, ring_o.to_z, *al)
        at_step("att2", 3, ring_u.to_core)
        at_step("dx", 0, ring_3.to_a, *al)
        at_step("dx", 0, ring_m.to_a, *al)
        at_step("dx", 0, ring_2.to_b, *al)
        at_step("dx", 0, ring_1.to_z, *al)
        at_step("dx", 1, ring_u.out, put_up(0))
        at_step("dx", 2, ring_v.to_core)
        at_step("dx", 2, ring_2.to_z, *al)
        at_step("dx", 3, ring_o.to_core)

    s.vr[...] = jnp.zeros_like(s.vr)

    def addrow(k, v):
        s.vr[k : k + 1, :] = s.vr[k : k + 1, :] + jnp.sum(v, axis=0, keepdims=True)

    def norm2_rows(rr):
        g = nt(s.gp[rr, :], s.wproj[...])
        y = s.gs[rr, :]
        addrow(6, g * y)
        addrow(7, g)
        d = g * v_g2[...]
        gs = s.st[rr, 1:2] * (d - jnp.mean(d, -1, keepdims=True) - y * jnp.mean(d * y, -1, keepdims=True))
        s.gs[rr, :] = gs
        b = gs.astype(BF)
        s.gb[rr, :] = b
        addrow(5, b.astype(F32))

    def norm2_body(t, _):
        norm2_rows(at(t, 256))
        return 0

    loop('norm2', NP // 256, norm2_body)
    for c in g_copies:
        c.wait_recv()
    gu = s.own[...]
    for k in range(1, n_psg):
        gu = gu + s.qr[k].astype(F32)
    s.gp[NP:T, :] = unit_back(gu, slice(NP, T))
    s.misc[:, 0:128] = (s.vcol[...] + tn(s.gb[NP:T, :], s.gp[NP:T, :])).astype(BF)
    norm2_rows(slice(NP, T))

    def ff_body(n, _):
        c = at(n, 256)
        w = s.wdn[c, :]
        tot = jnp.zeros((1, 256), F32)
        for m in range(T // TT):
            rr = slice(m * TT, m * TT + TT)
            g = (nt(s.gb[rr, :], w) * s.slo[rr, c].astype(F32)).astype(BF)
            s.slo[rr, c] = g
            tot = tot + jnp.sum(g.astype(F32), axis=0, keepdims=True)
        s.bup[0:1, c] = tot
        s.wdn[c, :] = tn(s.hid[:, c], s.gb[...]).astype(BF)
        return 0

    loop('ff', FF // 256, ff_body)
    if sums:
        epoch_signal(0)
        take_credit(3)

    def norm1_body(t, _):
        rr = at(t, TT)
        g = s.gs[rr, :] + nt(s.slo[rr, :], s.wup[...])
        y = s.y1[rr, :].astype(F32)
        addrow(3, g * y)
        addrow(4, g)
        d = g * v_g1[...]
        gs = s.st[rr, 0:1] * (d - jnp.mean(d, -1, keepdims=True) - y * jnp.mean(d * y, -1, keepdims=True))
        s.gs[rr, :] = gs
        b = gs.astype(BF)
        s.gb[rr, :] = b
        addrow(2, b.astype(F32))
        return 0

    loop('norm1', T // TT, norm1_body)

    def gup_body(n, _):
        if sums:
            q = FF // 1024
            turn, k = n // q, lax.rem(n, q)
            n = lax.rem(1 - ring_d.c + turn, 2) * 2 * q + (turn // 2) * q + k
        c = at(n, 256)
        s.wup[:, c] = tn(s.fb[...], s.slo[:, c]).astype(BF)
        return 0

    loop('gup', FF // 256, gup_body)
    if sums:
        epoch_signal(1)

    def dctx_body(t, _):
        rr = at(t, TT)
        s.dctx[rr, :] = (nt(s.gb[rr, :], s.wout[...]) * s.dctx[rr, :].astype(F32)).astype(BF)
        return 0

    loop('dctx', T // TT, dctx_body)

    def gout_body(n, _):
        c = at(n, 256)
        s.wout[:, c] = tn(s.ctx[...], s.gb[:, c]).astype(BF)
        return 0

    loop('gout', D // 256, gout_body)
    if sums:
        q = D // 32
        lane = lax.broadcasted_iota(jnp.int32, (q, 128), 1)
        for i in range(FF // 384):
            for k in range(3):
                v = s.bup[0:1, i * 384 + k * 128 : i * 384 + k * 128 + 128]
                s.tcol[k * 128 : k * 128 + 128, :] = jnp.broadcast_to(v, (128, 128)).T
            for d in range(4):
                v = jnp.zeros((q, 128), F32)
                for k in range(4):
                    v = jnp.where(lane == 8 + k, s.tcol[(4 * d + k) * q : (4 * d + k) * q + q, :], v)
                s.vcol[(4 * i + d) * q : (4 * i + d) * q + q, :] = v
    if sums:
        ring_o.start(*al)

    def p_copy_in(j):
        g, rest = j // (2 * nrow), lax.rem(j, 2 * nrow)
        i = (rest // 2) * (H // 2) + 2 * g + lax.rem(rest, 2)
        slot = lax.rem(j, 2)
        return pltpu.make_async_copy(s.o_p.at[i], s.pbuf.at[slot], s.psem.at[slot])

    steps = nrow * (H // 2)
    p_copy_in(0).start()

    def turn(rr, n, cq, ck):
        do = s.dctx[rr, cq]
        s.qt[:, 0:n] = do.T
        s.vt[:, 0:n] = (-do.astype(F32) * s.ctx[rr, cq].astype(F32)).astype(BF).T
        s.kt[:, 0:n] = s.mixed[rr, ck].T

    def back_tile(qr, kr, qa, ka, kw, cq, ck, cv, e):
        values = jnp.concatenate([s.mixed[kr, cv], jnp.ones((kw, 128), BF)], 1)
        grads = jnp.concatenate([two(s.qt[:, qa], 0), two(s.vt[:, qa], 0)], 0)
        ds = (e.astype(F32) * nn(values, grads)).astype(BF)
        dk = nn(ds, two(s.mixed[qr, cq], 1))
        dv = nn(e, two(s.dctx[qr, cq], 1))
        dq = (diagonal(nn(s.kt[:, ka], ds)).T * 0.125).astype(BF)
        return dq, dk, dv

    def att_back(j, _):
        g, rest = j // (2 * nrow), lax.rem(j, 2 * nrow)
        r = rest // 2
        hp = 2 * g + lax.rem(rest, 2)
        slot = lax.rem(j, 2)

        @pl.when(j + 1 < steps)
        def _():
            p_copy_in(j + 1).start()

        p_copy_in(j).wait()
        cq, ck, cv = pair_cols(hp)
        base = r * LEN

        def rws(a, n):
            return rows_at(base + a, n, 128)

        turn(rws(0, LEN), LEN, cq, ck)
        s.dka[...] = jnp.zeros_like(s.dka)
        s.dva[...] = jnp.zeros_like(s.dva)
        for qs, ks, kw, off in TILES:
            dq, dk, dv = back_tile(
                rws(qs, 128), rws(ks, kw), slice(qs, qs + 128), slice(ks, ks + kw), kw, cq, ck, cv,
                s.pbuf[slot, off : off + kw, :],
            )
            s.dq[qs : qs + 128, :] = dq
            s.dka[ks : ks + kw, :] += dk
            s.dva[ks : ks + kw, :] += dv
        s.mixed[rws(0, LEN), cq] = s.dq[...]
        s.mixed[rws(0, LEN), ck] = (s.dka[...] * 0.125).astype(BF)
        s.mixed[rws(0, LEN), cv] = s.dva[...].astype(BF)
        return 0

    def att_back_q(hp, _):
        cq, ck, cv = pair_cols(hp)
        rr = slice(NP, T)
        turn(rr, NQ, cq, ck)
        dq, dk, dv = back_tile(rr, rr, slice(0, NQ), slice(0, NQ), NQ, cq, ck, cv, s.pq[hp])
        s.mixed[rr, cq] = dq
        s.mixed[rr, ck] = (dk * 0.125).astype(BF)
        s.mixed[rr, cv] = dv.astype(BF)
        return 0

    lax.fori_loop(0, H // 2, att_back_q, 0)

    groups = (s.fb, s.gb, s.ctx)

    def group_grad(g):
        for w in range(3):
            c = w * D + g * 256
            groups[g][0:D, w * 256 : w * 256 + 256] = tn(s.x[...], s.mixed[:, c : c + 256]).astype(BF)

    for g in range(3):

        @functools.partial(loop, 'att%d' % g, 2 * nrow)
        def _(j, _, g=g):
            att_back(2 * nrow * g + j, 0)

        group_grad(g)
        if sums:
            (ring_1, ring_2, ring_3)[g].start(*al)
    for w, k in ((0, 0), (2, 1)):
        s.vr[k : k + 1, :] = jnp.sum(s.mixed[:, w * D : w * D + D].astype(F32), axis=0, keepdims=True)

    if sums:
        pad = jnp.zeros((120, 128), F32)
        few = lax.broadcasted_iota(jnp.int32, (128, 128), 1) < 8
        for i in range(D // 128):
            rr = slice(i * 128, i * 128 + 128)
            s.vcol[rr, :] = jnp.where(few, jnp.concatenate([s.vr[:, rr], pad], 0).T, s.vcol[rr, :])
        s.misc[:, 128:256] = s.vcol[...].astype(BF)
        ring_m.start(*al)

    def dx_body(t, _):
        rr = at(t, TT)
        s.gs[rr, :] = s.gs[rr, :] + nt(s.mixed[rr, :], s.wqkv[...])
        return 0

    loop('dx', T // TT, dx_body)
    outs = [
        pltpu.make_async_copy(s.gs.at[0:NP], s.o_gp, s.osem.at[2]),
        pltpu.make_async_copy(s.gs.at[NP:T], s.o_gq, s.osem.at[3]),
    ]
    if not sums:
        outs += [
            pltpu.make_async_copy(s.wdn, s.o_dn, s.osem.at[4]),
            pltpu.make_async_copy(s.wup, s.o_up, s.osem.at[5]),
            pltpu.make_async_copy(s.wout, s.o_out, s.osem.at[6]),
            pltpu.make_async_copy(s.ctx.at[0:D], s.o_q.at[0], s.osem.at[7]),
            pltpu.make_async_copy(s.fb.at[0:D], s.o_q.at[1], s.osem.at[8]),
            pltpu.make_async_copy(s.gb.at[0:D], s.o_q.at[2], s.osem.at[9]),
            pltpu.make_async_copy(s.misc, s.o_misc, s.osem.at[10]),
        ]
        s.o_bup[...] = s.bup[0:1, :]
        s.o_vr[...] = s.vr[...]
    for c in outs:
        c.start()
    if sums:
        ring_3.to_b(*al)
        ring_m.to_b(*al)
        ring_v.out(put_up(1))
        ring_1.to_core()
        ring_o.out(put_in(s.o_out))
        ring_3.to_z(*al)
        ring_m.to_z(*al)
        ring_2.to_core()
        ring_1.out(put_group(0))
        ring_2.out(put_group(1))
        ring_3.to_core()
        ring_m.to_core()
        ring_3.out(put_group(2))
        ring_m.out(put_in(s.o_misc))
        for r in rings:
            r.finish()
    for c in q_copies + l_copies + g_copies + loss_copies:
        c.wait_send()
    for c in loss_copies:
        c.wait_recv()
    if cfg.loss_here:
        s.o_loss[...] = jnp.sum(s.ls[...], axis=0)
    else:
        s.o_loss[...] = s.ls[0]
    for c in [o_pe, o_qe] + outs:
        c.wait()


def finish_kernel(names, *refs):
    s = Space()
    for name, ref in zip(names, refs):
        setattr(s, name, ref)
    pairs = ((s.pe, s.o_pe), (s.qe, s.o_qe), (s.gp, s.o_gp), (s.gq, s.o_gq))
    pairs += ((s.dn, s.o_dn), (s.up, s.o_up), (s.out, s.o_out), (s.qkv, s.o_qkv))
    ways = []
    for (src, dst), buf in zip(pairs, (s.bpe, s.bqe, s.bgp, s.bgq, s.bdn, s.bup, s.bout, s.bqkv)):
        n = src.shape[0] // 4 if src.shape[0] > 512 else src.shape[0]
        for i in range(src.shape[0] // n):
            k = len(ways)
            rr = slice(i * n, i * n + n)
            ways.append(
                (
                    pltpu.make_async_copy(src.at[rr], buf.at[rr], s.sem.at[0, k]),
                    pltpu.make_async_copy(buf.at[rr], dst.at[rr], s.sem.at[1, k]),
                )
            )
    for c, _ in ways:
        c.start()
    s.o_loss[...] = s.loss[0, 0]
    s.o_proj[...] = s.misc[:, 0:128]
    q = s.misc.shape[0]
    s.sq[...] = jnp.zeros_like(s.sq)
    s.sq[0:q, :] = s.misc[:, 128:256]
    s.sq[...] = s.sq[...].T
    for k in range(8):
        getattr(s, "o_v%d" % k)[...] = s.sq[k, 0:q]
    s.o_bup[...] = jnp.concatenate([s.sq[8 + k : 9 + k, 0:q] for k in range(4)], 1)[0]
    for c, d in ways:
        c.wait()
        d.start()
    for _, d in ways:
        d.wait()


def finish(o):
    sd = jax.ShapeDtypeStruct
    any_spec = pl.BlockSpec(memory_space=pl.ANY)
    vm = pl.BlockSpec(memory_space=pltpu.VMEM)
    names = ["pe", "qe", "gp", "gq", "dn", "up", "out", "qkv"]
    ins = [(n, o["o_" + n], any_spec) for n in names] + [("loss", o["o_loss"], vm), ("misc", o["o_misc"], vm)]
    outs = [("o_" + n, sd(o["o_" + n].shape, o["o_" + n].dtype), any_spec) for n in names]
    q = o["o_misc"].shape[0]
    outs += [("o_loss", sd((), F32), pl.BlockSpec(memory_space=pltpu.SMEM)), ("o_proj", sd((q, 128), F32), vm)]
    outs += [("o_v%d" % k, sd((q,), F32), vm) for k in range(8)] + [("o_bup", sd((4 * q,), F32), vm)]
    scratch = [("sq", pltpu.VMEM((128, 128), F32)), ("sem", pltpu.SemaphoreType.DMA((2, 14)))]
    scratch += [("b" + n, pltpu.VMEM(o["o_" + n].shape, o["o_" + n].dtype)) for n in names]
    all_names = [n for n, *_ in ins] + [n for n, *_ in outs] + [n for n, _ in scratch]
    res = pl.pallas_call(
        functools.partial(finish_kernel, all_names),
        out_shape=[v[1] for v in outs],
        in_specs=[v[2] for v in ins],
        out_specs=[v[2] for v in outs],
        scratch_shapes=[v for _, v in scratch],
    )(*[v[1] for v in ins])
    return dict(zip([n for n, *_ in outs], res))


def make_body(n_dp, n_psg):
    def body(
        passage_states, segment_ids, query_states, teacher_scores,
        w_qkv, bias_q, bias_v, w_out, bias_out, ln1_gain, ln1_bias,
        w_up, bias_up, w_down, bias_down, ln2_gain, ln2_bias, w_proj,
    ):
        D, FF = w_up.shape
        E = w_proj.shape[1]
        rows, length, _ = passage_states.shape
        qn, ql, _ = query_states.shape
        NP, NQ = rows * length, qn * ql
        T = NP + NQ
        cfg = Space()
        cfg.T, cfg.NP, cfg.NQ, cfg.TT = T, NP, NQ, T // 4
        cfg.D, cfg.FF, cfg.qlen = D, FF, ql
        cfg.n_dp, cfg.n_psg = n_dp, n_psg
        cfg.loss_here = n_dp <= 16
        cfg.sums = n_dp == 8 and n_psg == 4
        npair = rows * (H // 2)
        any_spec = pl.BlockSpec(memory_space=pl.ANY)
        vm = pl.BlockSpec(memory_space=pltpu.VMEM)
        ins = [
            ("i_pass", passage_states.reshape(NP, D), any_spec),
            ("i_query", query_states.reshape(NQ, D), any_spec),
            ("i_seg", segment_ids, vm),
            ("i_teach", teacher_scores.T, vm),
            ("i_wqkv", w_qkv, any_spec),
            ("i_bq", bias_q, vm),
            ("i_bv", bias_v, vm),
            ("i_wout", w_out, any_spec),
            ("i_bout", bias_out, vm),
            ("i_g1", ln1_gain, vm),
            ("i_b1", ln1_bias, vm),
            ("i_wup", w_up, any_spec),
            ("i_bup", bias_up, vm),
            ("i_wdn", w_down, any_spec),
            ("i_bdn", bias_down, vm),
            ("i_g2", ln2_gain, vm),
            ("i_b2", ln2_bias, vm),
            ("i_wproj", w_proj, any_spec),
        ]
        sd = jax.ShapeDtypeStruct
        outs = [
            ("o_pe", sd((NP, E), BF), any_spec),
            ("o_qe", sd((NQ, E), BF), any_spec),
            ("o_loss", sd((8, 128), F32), vm),
            ("o_gp", sd((NP, D), F32), any_spec),
            ("o_gq", sd((NQ, D), F32), any_spec),
            ("o_p", sd((npair, PW, 256), BF), any_spec),
        ]
        n_dev = n_dp * n_psg
        if cfg.sums:
            outs += [
                ("o_dn", sd((FF // n_dev, D), F32), vm),
                ("o_up", sd((D // n_dev, FF), F32), vm),
                ("o_out", sd((D // n_dev, D), F32), vm),
                ("o_qkv", sd((D // n_dev, 3 * D), F32), vm),
                ("o_misc", sd((D // n_dev, 256), F32), vm),
            ]
        else:
            outs += [
                ("o_dn", sd((FF, D), BF), any_spec),
                ("o_up", sd((D, FF), BF), any_spec),
                ("o_out", sd((D, D), BF), any_spec),
                ("o_q", sd((3, D, D), BF), any_spec),
                ("o_misc", sd((D, 256), BF), any_spec),
                ("o_bup", sd((1, FF), F32), vm),
                ("o_vr", sd((8, D), F32), vm),
            ]
        V = pltpu.VMEM
        DMA = pltpu.SemaphoreType.DMA
        scratch = [
            ("x", V((T, D), BF)),
            ("wqkv", V((D, 3 * D), BF)),
            ("wout", V((D, D), BF)),
            ("wup", V((D, FF), BF)),
            ("wdn", V((FF, D), BF)),
            ("wproj", V((D, E), BF)),
            ("bqkv", V((8, 3 * D), F32)),
            ("vin", V((8, D), F32)),
            ("tsq", V((128, 128), F32)),
            ("mixed", V((T, 3 * D), BF)),
            ("pbuf", V((2, PW, 256), BF)),
            ("pq", V((H // 2, NQ, 256), BF)),
            ("koh", V((T, 128), BF)),
            ("qoh", V((128, T), BF)),
            ("qt", V((128, LEN), BF)),
            ("vt", V((128, LEN), BF)),
            ("kt", V((128, LEN), BF)),
            ("ctx", V((T, D), BF)),
            ("y1", V((T, D), BF)),
            ("fb", V((T, D), BF)),
            ("hid", V((T, FF), BF)),
            ("slo", V((T, FF), BF)),
            ("gs", V((T, D), F32)),
            ("gb", V((T, D), BF)),
            ("st", V((T, 128), F32)),
            ("unit", V((T, E), F32)),
            ("unitb", V((T, E), BF)),
            ("aq", V((n_psg, NQ, E), BF)),
            ("ind", V((NP, 128), BF)),
            ("tot", V((n_psg, NQ, 128), F32)),
            ("lg", V((n_psg, 2 * n_psg * qn, 128), F32)),
            ("line", V((n_psg * NQ, 128), F32)),
            ("gl", V((n_psg * qn, 128), F32)),
            ("ls", V((n_dp if cfg.loss_here else 1, 8, 128), F32)),
            ("gsim", V((n_psg * NQ, NP), BF)),
            ("qs", V((n_psg, NQ, E), BF)),
            ("qr", V((n_psg, NQ, E), BF)),
            ("own", V((NQ, E), F32)),
            ("gp", V((T, E), BF)),
            ("misc", V((D, 256), BF)),
            ("vr", V((8, D), F32)),
            ("vcol", V((D, 128), F32)),
            ("bup", V((8, FF), F32)),
            ("dctx", V((T, D), BF)),
            ("dq", V((LEN, 128), BF)),
            ("dka", V((LEN, 128), F32)),
            ("dva", V((LEN, 128), F32)),
            ("lsem", DMA((7,))),
            ("psem", DMA((2,))),
            ("osem", DMA((11,))),
            ("ss", DMA((3, n_psg))),
            ("rs", DMA((3, n_psg))),
            ("lss", DMA((n_dp,))),
            ("lrs", DMA((n_dp,))),
        ]
        if cfg.sums:
            b, e = D // 16, FF // 16
            scratch += [
                ("tcol", V((384, 128), F32)),
                ("mrecv", V((31 * b, 128), BF)),
                ("fd", V((e, D // 2), F32)),
                ("rd", V((e // 2, D // 2), F32)),
                ("fu", V((2, b, FF // 4), F32)),
                ("ru", V((2, b // 2, FF // 4), F32)),
                ("fq", V((4, b, D // 2), F32)),
                ("rq", V((4, b // 2, D // 2), F32)),
                ("fm", V((b, 128), F32)),
                ("rm", V((b // 2, 128), F32)),
                ("gss", DMA((8, 18))),
                ("grs", DMA((8, 18))),
                ("arecv", V((8 * e, D // 2), BF)),
                ("credit", pltpu.SemaphoreType.REGULAR((5,))),
                ("epoch", pltpu.SemaphoreType.REGULAR((2,))),
            ]
        cfg.names = [a for a, *_ in ins] + [a for a, *_ in outs] + [a for a, _ in scratch]
        res = pl.pallas_call(
            functools.partial(kernel, cfg),
            out_shape=[o[1] for o in outs],
            in_specs=[i[2] for i in ins],
            out_specs=[o[2] for o in outs],
            scratch_shapes=[v for _, v in scratch],
            compiler_params=pltpu.CompilerParams(
                collective_id=0, has_side_effects=True, vmem_limit_bytes=64 * 1024 * 1024 - 65536
            ),
        )(*[i[1] for i in ins])
        o = dict(zip([a for a, *_ in outs], res))
        if cfg.sums:
            o = finish(o)
            loss = o["o_loss"]
        else:
            loss = o["o_loss"][0, 0]
        if not cfg.loss_here:
            loss = lax.psum(loss, "dp")
        head = (
            o["o_pe"].reshape(rows, length, E),
            o["o_qe"].reshape(qn, ql, E),
            loss,
            o["o_gp"].reshape(rows, length, D),
            o["o_gq"].reshape(qn, ql, D),
        )
        if cfg.sums:
            vec = [o["o_v%d" % k] for k in range(8)]
            g_qkv, g_out, g_up, g_bup, g_dn, g_proj = [
                o["o_" + k] for k in ("qkv", "out", "up", "bup", "dn", "proj")
            ]
        else:
            q3 = o["o_q"].reshape(3, D, 3, 256)
            q3 = jnp.transpose(q3, (1, 2, 0, 3)).reshape(D, 3 * D)

            def scat(v):
                return lax.psum_scatter(v, ("dp", "psg"), scatter_dimension=0, tiled=True)

            vec = scat(o["o_vr"].T)
            vec = [vec[:, k] for k in range(8)]
            g_bup = scat(o["o_bup"].reshape(-1))
            g_qkv, g_out, g_up, g_dn, g_proj = [
                scat(v.astype(F32)) for v in (q3, o["o_out"], o["o_up"], o["o_dn"], o["o_misc"][:, 0:128])
            ]
        return head + (
            g_qkv, vec[0], vec[1], g_out, vec[2], vec[3], vec[4],
            g_up, g_bup, g_dn, vec[5], vec[6], vec[7], g_proj,
        )

    return body


def solution(mesh):
    rowspec = P(("dp", "psg"))
    three = P(("dp", "psg"), None, None)
    two = P(("dp", "psg"), None)
    in_specs = (three, two, three, P("dp", "psg")) + (P(),) * 14
    out_specs = (
        three, three, P(), three, three,
        two, rowspec, rowspec, two, rowspec, rowspec, rowspec,
        two, rowspec, two, rowspec, rowspec, rowspec, two,
    )
    body = make_body(mesh.shape["dp"], mesh.shape["psg"])
    return jax.shard_map(body, mesh=mesh, in_specs=in_specs, out_specs=out_specs, check_vma=False)
```

```python
import functools

import jax
import jax.numpy as jnp
from jax import lax
from jax.experimental import pallas as pl
from jax.experimental.pallas import tpu as pltpu
from jax.sharding import PartitionSpec as P

F32 = jnp.float32
BF = jnp.bfloat16
MESH = pl.DeviceIdType.MESH
H = 12
HD = 64
SEGS = 3
LOG2E = 1.4426950408889634
SHARP = 0.1
TILES = ((0, 0, 256, 0), (128, 0, 384, 256), (256, 128, 384, 640), (384, 256, 256, 1024))
PW = 1280
LEN = 512


def nn(a, b):
    return lax.dot_general(a, b, (((1,), (0,)), ((), ())), preferred_element_type=F32)


def nt(a, b):
    return lax.dot_general(a, b, (((1,), (1,)), ((), ())), preferred_element_type=F32)


def tn(a, b):
    return lax.dot_general(a, b, (((0,), (0,)), ((), ())), preferred_element_type=F32)


def at(i, n):
    return pl.ds(pl.multiple_of(i * n, n), n)


def rows_at(start, n, unit):
    return pl.ds(pl.multiple_of(start, unit), n)


class Space:
    pass


def norm_stats(v):
    mean = jnp.mean(v, -1, keepdims=True)
    c = v - mean
    inv = lax.rsqrt(jnp.mean(c * c, -1, keepdims=True) + 1e-12)
    return c * inv, inv


class Ring:
    def __init__(self, s, u, g, b, half, places, f, rd, where, stride=None, off=0):
        self.s, self.u, self.g, self.b, self.half = s, u, g, b, half
        self.stride, self.off = stride or half, off
        self.c_at, self.a_at, self.b_at, self.z_at = places
        self.f, self.rd = f, rd
        dp, psg = where
        self.z, self.x, self.y, self.c = dp // 2, lax.rem(dp, 2), psg // 2, lax.rem(psg, 2)
        self.core = {"psg": self.y * 2 + 1 - self.c}
        self.xn = {"dp": self.z * 2 + 1 - self.x}
        self.yn = {"psg": (1 - self.y) * 2 + self.c}
        self.zn = [{"dp": lax.rem(self.z + k, 4) * 2 + self.x} for k in range(1, 4)]

    def cols(self, c):
        return pl.ds(pl.multiple_of(c * self.stride + self.off, 128), self.half)

    def part(self, row, n, c):
        return self.g.at[pl.ds(pl.multiple_of(row * self.b, 16), n * self.b), self.cols(c)]

    def remote(self, i, src, dst, dev):
        return pltpu.make_async_remote_copy(
            src_ref=src, dst_ref=dst, send_sem=self.s.gss.at[self.u, i], recv_sem=self.s.grs.at[self.u, i],
            device_id=dev, device_id_type=MESH,
        )

    def copy_c(self, z):
        return self.remote(z, self.part(4 * z, 4, 1 - self.c), self.c_at(z), self.core)

    def copy_a(self, z):
        if z % 2 == 0:
            return [self.remote(4 + z // 2, self.part(4 * z + 2 * (1 - self.x), 2, self.c), self.a_at(z, 0, 2), self.xn)]
        return [
            self.remote(
                6 + z - 1 + x, self.part(4 * z + 2 * x + 1 - self.y, 1, self.c), self.a_at(z, x, 1), self.yn
            )
            for x in range(2)
        ]

    def copy_b(self, z):
        if z % 2 == 0:
            return self.remote(10 + z, self.part(4 * z + 2 * self.x + 1 - self.y, 1, self.c), self.b_at(z), self.yn)
        return self.remote(10 + z, self.part(4 * z + 2 * (1 - self.x) + self.y, 1, self.c), self.b_at(z), self.xn)

    def copy_z(self, k):
        z = lax.rem(self.z + k + 1, 4)
        return self.remote(14 + k, self.part(4 * z + 2 * self.x + self.y, 1, self.c), self.z_at(k), self.zn[k])

    def send_z(self, z):
        k = lax.rem(z - self.z + 3, 4)

        @pl.when(z != self.z)
        def _():
            self.s_z(z, k).start()

    def s_z(self, z, k):
        return pltpu.make_async_remote_copy(
            src_ref=self.part(4 * z + 2 * self.x + self.y, 1, self.c), dst_ref=self.z_at(k),
            send_sem=self.s.gss.at[self.u, 14 + k], recv_sem=self.s.grs.at[self.u, 14 + k],
            device_id={"dp": z * 2 + self.x}, device_id_type=MESH,
        )

    def copy_d(self):
        h = self.b // 2
        src = self.f.at[pl.ds(pl.multiple_of((1 - self.c) * h, 8), h), :]
        return self.remote(17, src, self.rd, self.core)

    def add(self, part, got):
        part[...] = part[...] + got[...]

    def start(self, *zs):
        for z in zs:
            self.copy_c(z).start()

    def to_a(self, *zs):
        for z in zs:
            self.copy_c(z).wait_recv()
            self.add(self.part(4 * z, 4, self.c), self.c_at(z))
            for c in self.copy_a(z):
                c.start()

    def to_b(self, *zs):
        for z in zs:
            for c in self.copy_a(z):
                c.wait_recv()
            if z % 2 == 0:
                self.add(self.part(4 * z + 2 * self.x, 2, self.c), self.a_at(z, 0, 2))
            else:
                for x in range(2):
                    self.add(self.part(4 * z + 2 * x + self.y, 1, self.c), self.a_at(z, x, 1))
            self.copy_b(z).start()

    def to_z(self, *zs):
        for z in zs:
            self.copy_b(z).wait_recv()
            self.add(self.part(4 * z + 2 * self.x + self.y, 1, self.c), self.b_at(z))
            self.send_z(z)

    def to_core(self):
        v = self.part(4 * self.z + 2 * self.x + self.y, 1, self.c)[...].astype(F32)
        for k in range(3):
            self.copy_z(k).wait_recv()
            v = v + self.z_at(k)[...].astype(F32)
        self.f[...] = v
        self.copy_d().start()

    def out(self, put):
        self.copy_d().wait_recv()
        h = self.b // 2
        put(self.c, self.f[pl.ds(pl.multiple_of(self.c * h, 8), h), :])
        put(1 - self.c, self.rd[...])

    def finish(self):
        for z in range(4):
            self.copy_c(z).wait_send()
            for c in self.copy_a(z):
                c.wait_send()
            self.copy_b(z).wait_send()
        for k in range(3):
            self.copy_z(k).wait_send()
        self.copy_d().wait_send()


def place(ref, f, n, width):
    def ref_at(i, x=0, m=1):
        row, col = f(i)
        if not isinstance(row, int):
            return ref.at[pl.ds(pl.multiple_of(row, 16), n), col : col + width]
        return ref.at[row + x * n : row + x * n + m * n, col : col + width]

    return ref_at


def make_rings(s, cfg, where):
    D, FF = cfg.D, cfg.FF
    h, w, b, e = D // 2, FF // 2, D // 16, FF // 16
    low = D
    spots = lambda r, k: (
        place(r, lambda z: (low + 4 * b * (z % 2), (k + z // 2) * h), 4 * b, h),
        place(r, lambda z: (low + 2 * b * z, (k + 2) * h), b, h),
        place(r, lambda z: (low + b * z, (k + 3) * h), b, h),
        place(r, lambda z: (low + b * (4 + z), (k + 3) * h), b, h),
    )
    down = (
        place(s.hid, lambda z: (0, z * h), 4 * e, h),
        place(s.arecv, lambda z: (2 * e * z, 0), e, h),
        place(s.hid, lambda z: (e * z, 6 * h), e, h),
        place(s.hid, lambda z: (e * z, 7 * h), e, h),
    )
    v = w // 2
    ups = lambda k: (
        place(s.hid, lambda z: (4 * b * z, k * v), 4 * b, v),
        place(s.hid, lambda z: (b * (8 * k + 2 * z), 2 * v), b, v),
        place(s.slo, lambda z: (b * z, k * v), b, v),
        place(s.slo, lambda z: (b * (4 + z), k * v), b, v),
    )
    second = (
        place(s.y1, lambda z: (4 * b * z, 0), 4 * b, h),
        place(s.y1, lambda z: (low + 2 * b * z, 0), b, h),
        place(s.y1, lambda z: (b * z, h), b, h),
        place(s.y1, lambda z: (b * (4 + z), h), b, h),
    )
    third = (
        place(s.y1, lambda z: (b * (7 + 4 * z), h), 4 * b, h),
        place(s.hid, lambda z: (low + 2 * b * z, 4 * h), b, h),
        place(s.hid, lambda z: (low + b * z, 5 * h), b, h),
        place(s.hid, lambda z: (low + b * (4 + z), 5 * h), b, h),
    )
    small = (
        place(s.mrecv, lambda z: (4 * b * z, 0), 4 * b, 128),
        place(s.mrecv, lambda z: (b * (16 + 2 * z), 0), b, 128),
        place(s.mrecv, lambda z: (b * (24 + z), 0), b, 128),
        place(s.mrecv, lambda z: (b * (28 + z), 0), b, 128),
    )
    mk = lambda u, g, bb, half, places, f, rd: Ring(s, u, g, bb, half, places, f, rd, where)
    return (
        mk(0, s.wdn, e, h, down, s.fd, s.rd),
        (
            Ring(s, 1, s.wup, b, v, ups(0), s.fu.at[0], s.ru.at[0], where, w, 0),
            Ring(s, 7, s.wup, b, v, ups(1), s.fu.at[1], s.ru.at[1], where, w, v),
        ),
        mk(2, s.wout, b, h, spots(s.hid, 0), s.fq.at[0], s.rq.at[0]),
        mk(3, s.fb, b, h, spots(s.slo, 0), s.fq.at[1], s.rq.at[1]),
        mk(4, s.gb, b, h, second, s.fq.at[2], s.rq.at[2]),
        mk(5, s.ctx, b, h, third, s.fq.at[3], s.rq.at[3]),
        mk(6, s.misc, b, 128, small, s.fm, s.rm),
    )


def kernel(cfg, *refs):
    s = Space()
    for name, ref in zip(cfg.names, refs):
        setattr(s, name, ref)
    T, NP, NQ, TT = cfg.T, cfg.NP, cfg.NQ, cfg.TT
    D, FF = cfg.D, cfg.FF
    nrow = NP // LEN
    me_dp = lax.axis_index("dp")
    me_psg = lax.axis_index("psg")
    n_psg, n_dp = cfg.n_psg, cfg.n_dp

    def load(k, src, dst):
        c = pltpu.make_async_copy(src, dst, s.lsem.at[k])
        if k < 3:
            c.start()
        return c

    l_x = load(0, s.i_pass, s.x.at[0:NP])
    l_q = load(1, s.i_query, s.x.at[NP:T])
    l_wqkv = load(2, s.i_wqkv, s.wqkv)
    l_wout = load(3, s.i_wout, s.wout)
    l_wup = load(4, s.i_wup, s.wup)
    l_wdn = load(5, s.i_wdn, s.wdn)
    l_wpj = load(6, s.i_wproj, s.wproj)

    for k, v in enumerate((s.i_bout, s.i_g1, s.i_b1, s.i_bdn, s.i_g2, s.i_b2)):
        s.vin[k : k + 1, :] = v[...][None, :]
    v_bout, v_g1, v_b1, v_bdn, v_g2, v_b2 = [s.vin.at[k : k + 1] for k in range(6)]
    bar = pltpu.get_barrier_semaphore()
    peers = []
    for k in range(1, n_psg):
        peers.append({"psg": lax.rem(me_psg + k, n_psg)})
    if cfg.loss_here:
        for k in range(1, n_dp):
            peers.append({"dp": lax.rem(me_dp + k, n_dp)})
    for p in peers:
        pl.semaphore_signal(bar, inc=1, device_id=p, device_id_type=MESH)

    sums = cfg.sums
    if sums:
        ring_d, (ring_u, ring_v), ring_o, ring_1, ring_2, ring_3, ring_m = make_rings(s, cfg, (me_dp, me_psg))
        rings = (ring_d, ring_u, ring_v, ring_o, ring_1, ring_2, ring_3, ring_m)

        def epoch_signal(k):
            for dev in [ring_d.core, ring_d.xn, ring_d.yn] + ring_d.zn:
                pl.semaphore_signal(s.epoch.at[k], inc=1, device_id=dev, device_id_type=MESH)

        def give_credit(z):
            pl.semaphore_signal(s.credit.at[z], inc=1, device_id=ring_d.core, device_id_type=MESH)

        def take_credit(z):
            pl.semaphore_wait(s.credit.at[z], 1)
            ring_d.start(z)

        def start_up():
            pl.semaphore_wait(s.credit.at[4], 1)
            ring_u.start(0, 1, 2, 3)

        def epoch_wait(k):
            pl.semaphore_wait(s.epoch.at[k], 6)

    plan = {}

    def loop(name, n, body):
        todo = plan.get(name, {})

        def with_plan(i, carry):
            body(i, carry)
            for k in sorted(todo):

                @pl.when(i == k)
                def _(k=k):
                    for act in todo[k]:
                        act()

            return 0

        lax.fori_loop(0, n, with_plan, 0)

    def put_in(ref):
        def put(c, v):
            ref[:, pl.ds(pl.multiple_of(c * v.shape[1], 128), v.shape[1])] = v

        return put

    def put_up(k):
        def put(c, v):
            n = v.shape[1]
            s.o_up[:, pl.ds(pl.multiple_of((2 * c + k) * n, 128), n)] = v

        return put

    def put_group(g):
        def put(c, v):
            for i in range(v.shape[1] // 128):
                k = c * (v.shape[1] // 128) + i
                col = (k // 2) * D + g * 256 + lax.rem(k, 2) * 128
                s.o_qkv[:, pl.ds(pl.multiple_of(col, 128), 128)] = v[:, i * 128 : i * 128 + 128]

        return put

    bounds = []
    for r in range(nrow):
        seg = s.i_seg[r : r + 1, :]
        bounds.append(
            (
                jnp.sum(jnp.where(seg < 1, 1.0, 0.0), axis=1, keepdims=True),
                jnp.sum(jnp.where(seg < 2, 1.0, 0.0), axis=1, keepdims=True),
            )
        )

    s.bqkv[...] = jnp.zeros_like(s.bqkv)
    s.bqkv[0:1, 0:D] = s.i_bq[...][None, :]
    s.bqkv[0:1, 2 * D : 3 * D] = s.i_bv[...][None, :]
    s.bup[0:1, :] = s.i_bup[...][None, :]
    l_x.wait()
    l_q.wait()
    l_wqkv.wait()
    for c in (l_wout, l_wup, l_wdn, l_wpj):
        c.start()

    def qkv_body(n, _):
        c = at(n, 256)
        s.mixed[:, c] = (nn(s.x[...], s.wqkv[:, c]) + s.bqkv[0:1, c]).astype(BF)
        return 0

    lax.fori_loop(0, 3 * D // 256, qkv_body, 0)

    scale = 0.125 * LOG2E
    li = lax.broadcasted_iota(jnp.int32, (LEN, 128), 1).astype(F32)
    si = lax.broadcasted_iota(jnp.int32, (128, LEN), 0).astype(F32)
    for r in range(nrow):
        b0, b1 = bounds[r]
        rr = slice(r * LEN, (r + 1) * LEN)
        ti = lax.broadcasted_iota(jnp.int32, (LEN, 128), 0).astype(F32)
        seg = jnp.where(ti >= b0, 1.0, 0.0) + jnp.where(ti >= b1, 1.0, 0.0)
        s.koh[rr, :] = jnp.where(seg == li, 1.0, 0.0).astype(BF)
        ti = lax.broadcasted_iota(jnp.int32, (128, LEN), 1).astype(F32)
        seg = jnp.where(ti >= b0, 1.0, 0.0) + jnp.where(ti >= b1, 1.0, 0.0)
        s.qoh[:, rr] = jnp.where(jnp.logical_or(seg == si, si >= SEGS), 0.0, -1e30).astype(BF)
    ql = cfg.qlen
    ti = lax.broadcasted_iota(jnp.int32, (NQ, 128), 0)
    li = lax.broadcasted_iota(jnp.int32, (NQ, 128), 1)
    s.koh[NP:T, :] = jnp.where(jnp.logical_and(ti >= li * ql, ti < li * ql + ql), 1.0, 0.0).astype(BF)
    si = lax.broadcasted_iota(jnp.int32, (128, NQ), 0)
    ti = lax.broadcasted_iota(jnp.int32, (128, NQ), 1)
    mine = jnp.logical_and(ti >= si * ql, ti < si * ql + ql)
    s.qoh[:, NP:T] = jnp.where(jnp.logical_or(mine, si * ql >= NQ), 0.0, -1e30).astype(BF)
    one_b, zero_b = jnp.ones((), BF), jnp.zeros((), BF)

    def two(v, axis):
        keep = lax.broadcasted_iota(jnp.int32, v.shape, axis) < 64
        return jnp.concatenate([jnp.where(keep, v, zero_b), jnp.where(keep, zero_b, v)], 1 - axis)

    def diagonal(v):
        return jnp.concatenate([v[0:64, 0:128], v[64:128, 128:256]], 0)

    def att_tile(qr, kr, qa, ka, kw, cq, ck, cv, keep_e):
        keys = jnp.concatenate([s.mixed[kr, ck], s.koh[kr, :]], 1)
        far = s.qoh[:, qr]
        queries = jnp.concatenate([two(s.qt[:, qa], 0), jnp.concatenate([far, far], 1)], 0)
        sc = nn(keys, queries)
        e = jnp.exp2(sc * scale - jnp.max(sc, axis=0, keepdims=True) * scale).astype(BF)
        keep_e(e)
        o = nn(jnp.concatenate([s.vt[:, ka], jnp.ones((16, kw), BF)], 0), e)
        inv = 1.0 / o[128:129, :]
        s.ctx[qr, cq] = diagonal(o[0:128, :] * inv).T.astype(BF)
        s.dctx[qr, cq] = diagonal(jnp.broadcast_to(inv, (128, 256))).T.astype(BF)

    def pair_cols(hp):
        return at(hp, 128), at(hp + D // 128, 128), at(hp + 2 * D // 128, 128)

    def p_copy_out(i, slot):
        return pltpu.make_async_copy(s.pbuf.at[slot], s.o_p.at[i], s.psem.at[slot])

    def att_body(i, _):
        r, hp = i // (H // 2), lax.rem(i, H // 2)
        slot = lax.rem(i, 2)

        @pl.when(i >= 2)
        def _():
            p_copy_out(i - 2, slot).wait()

        cq, ck, cv = pair_cols(hp)
        whole = rows_at(r * LEN, LEN, LEN)
        s.qt[...] = s.mixed[whole, cq].T
        s.vt[...] = s.mixed[whole, cv].T
        for qs, ks, kw, off in TILES:

            def keep_e(e):
                s.pbuf[slot, off : off + kw, :] = e

            qr, kr = rows_at(r * LEN + qs, 128, 128), rows_at(r * LEN + ks, kw, 128)
            att_tile(qr, kr, slice(qs, qs + 128), slice(ks, ks + kw), kw, cq, ck, cv, keep_e)
        p_copy_out(i, slot).start()
        return 0

    lax.fori_loop(0, nrow * (H // 2), att_body, 0)

    def att_q_body(hp, _):
        cq, ck, cv = pair_cols(hp)
        s.qt[:, 0:NQ] = s.mixed[NP:T, cq].T
        s.vt[:, 0:NQ] = s.mixed[NP:T, cv].T

        def keep_e(e):
            s.pq[hp] = e

        att_tile(slice(NP, T), slice(NP, T), slice(0, NQ), slice(0, NQ), NQ, cq, ck, cv, keep_e)
        return 0

    lax.fori_loop(0, H // 2, att_q_body, 0)
    last = nrow * (H // 2)
    p_copy_out(last - 2, (last - 2) % 2).wait()
    p_copy_out(last - 1, (last - 1) % 2).wait()

    l_wout.wait()

    def out_body(t, _):
        rr = at(t, T // 2)
        v = nn(s.ctx[rr, :], s.wout[...]) + v_bout[...] + s.x[rr, :].astype(F32)
        y, inv = norm_stats(v)
        s.y1[rr, :] = y.astype(BF)
        s.st[rr, 0:1] = inv
        s.fb[rr, :] = (y * v_g1[...] + v_b1[...]).astype(BF)
        return 0

    lax.fori_loop(0, 2, out_body, 0)

    l_wup.wait()

    def up_body(n, _):
        c = at(n, 256)
        for rr in (slice(0, T),):
            h = nn(s.fb[rr, :], s.wup[:, c]) + s.bup[0:1, c]
            cdf = 0.5 * (1.0 + lax.erf(h * 0.7071067811865476))
            s.hid[rr, c] = (h * cdf).astype(BF)
            s.slo[rr, c] = (cdf + h * jnp.exp2(h * h * (-0.5 * LOG2E)) * 0.3989422804014327).astype(BF)
        return 0

    lax.fori_loop(0, FF // 256, up_body, 0)

    def remote(src, dst, ssem, rsem, dev):
        return pltpu.make_async_remote_copy(
            src_ref=src, dst_ref=dst, send_sem=ssem, recv_sem=rsem, device_id=dev, device_id_type=MESH
        )

    l_wdn.wait()
    l_wpj.wait()

    q_copies = [
        remote(s.unitb.at[NP:T], s.aq.at[k], s.ss.at[0, k], s.rs.at[0, k], {"psg": lax.rem(me_psg + k, n_psg)})
        for k in range(1, n_psg)
    ]

    def down_body(t, _):
        rr = at(1 - t, T // 2)
        first = s.y1[rr, :].astype(F32) * v_g1[...] + v_b1[...]
        v = first + (nn(s.hid[rr, :], s.wdn[...]) + v_bdn[...])
        y, inv = norm_stats(v)
        s.gs[rr, :] = y
        s.st[rr, 1:2] = inv
        sec = (y * v_g2[...] + v_b2[...]).astype(BF)
        s.gb[rr, :] = sec
        pj = nn(sec, s.wproj[...])
        il = lax.rsqrt(jnp.sum(pj * pj, -1, keepdims=True) + 1e-06)
        s.st[rr, 2:3] = il
        u = pj * il
        s.unit[rr, :] = u
        s.unitb[rr, :] = u.astype(BF)

        @pl.when(t == 0)
        def _():
            pl.semaphore_wait(bar, len(peers))
            for c in q_copies:
                c.start()

        return 0

    lax.fori_loop(0, 2, down_body, 0)

    o_pe = pltpu.make_async_copy(s.unitb.at[0:NP], s.o_pe, s.osem.at[0])
    o_pe.start()
    o_qe = pltpu.make_async_copy(s.unitb.at[NP:T], s.o_qe, s.osem.at[1])
    o_qe.start()

    s.aq[0] = s.unitb[NP:T, :]

    for r in range(nrow):
        b0, b1 = bounds[r]
        ti = lax.broadcasted_iota(jnp.int32, (LEN, 128), 0).astype(F32)
        li = lax.broadcasted_iota(jnp.int32, (LEN, 128), 1).astype(F32)
        pid = SEGS * r + jnp.where(ti >= b0, 1.0, 0.0) + jnp.where(ti >= b1, 1.0, 0.0)
        s.ind[r * LEN : (r + 1) * LEN, :] = jnp.where(pid == li, 1.0, 0.0).astype(BF)
    count = jnp.sum(s.ind[...].astype(F32), axis=0, keepdims=True)
    slots = nrow * SEGS
    valid = lax.broadcasted_iota(jnp.int32, (1, 128), 1) < slots
    count = jnp.where(valid, count, 1.0)
    nqg = NQ // ql
    s.lg[0] = jnp.zeros(s.lg.shape[1:], F32)

    def powers(k):
        sim = nt(s.aq[k], s.unitb[0:NP, :])
        return jnp.exp2((sim - 1.0) * (LOG2E / SHARP))

    for k in range(n_psg):
        if k:
            q_copies[k - 1].wait_recv()
        pw = powers(k)
        hi = pw.astype(BF)
        lo = (pw - hi.astype(F32)).astype(BF)
        tot = nn(hi, s.ind[...]) + nn(lo, s.ind[...])
        tot = jnp.where(valid, tot, 1.0)
        s.tot[k] = tot
        line = jnp.log(tot / count) + 1.0 / SHARP
        line = jnp.where(valid, line, 0.0)
        src = lax.rem(me_psg + n_psg - k, n_psg)
        s.line[rows_at(src * NQ, NQ, NQ), :] = line

    nq_all = n_psg * nqg
    qrow = lax.broadcasted_iota(jnp.int32, (nq_all, n_psg * NQ), 0) * ql
    qcol = lax.broadcasted_iota(jnp.int32, (nq_all, n_psg * NQ), 1)
    sel = jnp.where(jnp.logical_and(qcol >= qrow, qcol < qrow + ql), 1.0, 0.0).astype(BF)
    line = s.line[...]
    hi = line.astype(BF)
    line = line - hi.astype(F32)
    mid = line.astype(BF)
    lo = (line - mid.astype(F32)).astype(BF)
    s.lg[0, 0:nq_all, :] = nn(sel, hi) + (nn(sel, mid) + nn(sel, lo))
    s.tsq[...] = jnp.zeros_like(s.tsq)
    s.tsq[0:slots, 0:nq_all] = s.i_teach[...]
    s.lg[0, nq_all : 2 * nq_all, :] = s.tsq[...].T[0:nq_all, :]
    l_copies = []
    for k in range(1, n_psg):
        c = remote(
            s.lg.at[0], s.lg.at[k], s.ss.at[1, k], s.rs.at[1, k], {"psg": lax.rem(me_psg + k, n_psg)}
        )
        c.start()
        l_copies.append(c)
    for c in l_copies:
        c.wait_recv()
    ok = valid[None]
    lg = s.lg[...]
    half = nq_all

    def log_norm(v):
        vm = jnp.where(valid[None], v, -1e30)
        top = jnp.max(jnp.max(vm, axis=-1, keepdims=True), axis=0, keepdims=True)
        sh = v - top
        ex = jnp.where(valid[None], jnp.exp(sh), 0.0)
        tot = jnp.sum(jnp.sum(ex, axis=-1, keepdims=True), axis=0, keepdims=True)
        return sh - jnp.log(tot)

    stu = log_norm(lg[:, 0:half, :])
    tea = log_norm(lg[:, half : 2 * half, :])
    pt = jnp.exp(tea)
    kl = jnp.where(ok, pt * (tea - stu), 0.0)
    group_sum = jnp.sum(jnp.sum(jnp.sum(kl, axis=0), axis=-1, keepdims=True), axis=0, keepdims=True)
    s.ls[0] = jnp.broadcast_to(group_sum / n_dp, (8, 128))
    loss_copies = []
    if cfg.loss_here:
        for k in range(1, n_dp):
            c = remote(
                s.ls.at[0], s.ls.at[k], s.lss.at[k], s.lrs.at[k], {"dp": lax.rem(me_dp + k, n_dp)}
            )
            c.start()
            loss_copies.append(c)
    s.gl[...] = jnp.where(valid, (jnp.exp(stu[0]) - pt[0]) / n_dp, 0.0)
    for q in range(nq_all):
        s.line[q * ql : q * ql + ql, :] = jnp.broadcast_to(s.gl[q : q + 1, :], (ql, 128))

    g_copies = []
    for k in list(range(1, n_psg)) + [0]:
        pw = powers(k)
        src = lax.rem(me_psg + n_psg - k, n_psg)
        ratio = s.line[rows_at(src * NQ, NQ, NQ), :] / s.tot[k]
        ratio = ratio * (1.0 / SHARP)
        hi = ratio.astype(BF)
        lo = (ratio - hi.astype(F32)).astype(BF)
        g = ((nt(hi, s.ind[...]) + nt(lo, s.ind[...])) * pw).astype(BF)
        s.gsim[k * NQ : (k + 1) * NQ, :] = g
        qp = nn(g, s.unitb[0:NP, :])
        if k:
            s.qs[k] = qp.astype(BF)
            c = remote(s.qs.at[k], s.qr.at[k], s.ss.at[2, k], s.rs.at[2, k], {"psg": src})
            c.start()
            g_copies.append(c)
        else:
            s.own[...] = qp

    def unit_back(gu, rr):
        u = s.unit[rr, :]
        return (s.st[rr, 2:3] * (gu - u * jnp.sum(gu * u, -1, keepdims=True))).astype(BF)

    aq = s.aq[...].reshape(n_psg * NQ, 128)
    for m in range(NP // 256):
        rr = slice(m * 256, m * 256 + 256)
        gu = tn(s.gsim[:, rr], aq)
        s.gp[rr, :] = unit_back(gu, rr)
    s.vcol[...] = tn(s.gb[0:NP, :], s.gp[0:NP, :])

    if sums:
        al = (0, 1, 2, 3)

        def at_step(name, k, f, *args):
            plan.setdefault(name, {}).setdefault(k, []).append(lambda: f(*args))

        for z in range(4):
            at_step("ff", 3 * z + 2, give_credit, z)
        for z in range(3):
            at_step("ff", 3 * z + 3, take_credit, z)
            at_step("ff", 3 * z + 5, ring_d.to_a, z)
        at_step("norm1", 0, epoch_wait, 0)
        at_step("norm1", 0, ring_d.to_b, 0)
        at_step("norm1", 0, ring_d.to_a, 3)
        at_step("norm1", 0, give_credit, 4)
        at_step("norm1", 1, ring_d.to_b, 1)
        at_step("gup", 1, ring_d.to_b, 2)
        at_step("gup", 2, start_up)
        at_step("gup", 4, ring_d.to_z, 1)
        at_step("gup", 6, ring_u.to_a, *al)
        at_step("gup", 8, ring_v.start, *al)
        at_step("gup", 11, ring_d.to_b, 3)
        at_step("dctx", 0, epoch_wait, 1)
        at_step("dctx", 0, ring_d.to_z, 0)
        at_step("dctx", 2, ring_d.to_z, 2)
        at_step("gout", 0, ring_v.to_a, *al)
        at_step("att0", 0, ring_d.to_z, 3)
        at_step("att0", 0, ring_u.to_b, *al)
        at_step("att0", 1, ring_o.to_a, *al)
        at_step("att1", 0, ring_v.to_b, *al)
        at_step("att1", 0, ring_1.to_a, *al)
        at_step("att1", 0, ring_u.to_z, *al)
        at_step("att1", 1, ring_d.to_core)
        at_step("att1", 2, ring_o.to_b, *al)
        at_step("att2", 0, ring_2.to_a, *al)
        at_step("att2", 0, ring_v.to_z, *al)
        at_step("att2", 0, ring_d.out, put_in(s.o_dn))
        at_step("att2", 1, ring_1.to_b, *al)
        at_step("att2", 2, ring_o.to_z, *al)
        at_step("att2", 3, ring_u.to_core)
        at_step("dx", 0, ring_2.to_b, *al)
        at_step("dx", 0, ring_1.to_z, *al)
        at_step("dx", 1, ring_u.out, put_up(0))
        at_step("dx", 2, ring_v.to_core)
        at_step("dx", 2, ring_2.to_z, *al)
        at_step("dx", 3, ring_o.to_core)

    s.vr[...] = jnp.zeros_like(s.vr)

    def addrow(k, v):
        s.vr[k : k + 1, :] = s.vr[k : k + 1, :] + jnp.sum(v, axis=0, keepdims=True)

    def norm2_rows(rr):
        g = nt(s.gp[rr, :], s.wproj[...])
        y = s.gs[rr, :]
        addrow(6, g * y)
        addrow(7, g)
        d = g * v_g2[...]
        gs = s.st[rr, 1:2] * (d - jnp.mean(d, -1, keepdims=True) - y * jnp.mean(d * y, -1, keepdims=True))
        s.gs[rr, :] = gs
        b = gs.astype(BF)
        s.gb[rr, :] = b
        addrow(5, b.astype(F32))

    def norm2_body(t, _):
        norm2_rows(at(t, 256))
        return 0

    loop('norm2', NP // 256, norm2_body)
    for c in g_copies:
        c.wait_recv()
    gu = s.own[...]
    for k in range(1, n_psg):
        gu = gu + s.qr[k].astype(F32)
    s.gp[NP:T, :] = unit_back(gu, slice(NP, T))
    s.misc[:, 0:128] = (s.vcol[...] + tn(s.gb[NP:T, :], s.gp[NP:T, :])).astype(BF)
    norm2_rows(slice(NP, T))

    def ff_body(n, _):
        c = at(n, 256)
        w = s.wdn[c, :]
        tot = jnp.zeros((1, 256), F32)
        for m in range(T // TT):
            rr = slice(m * TT, m * TT + TT)
            g = (nt(s.gb[rr, :], w) * s.slo[rr, c].astype(F32)).astype(BF)
            s.slo[rr, c] = g
            tot = tot + jnp.sum(g.astype(F32), axis=0, keepdims=True)
        s.bup[0:1, c] = tot
        s.wdn[c, :] = tn(s.hid[:, c], s.gb[...]).astype(BF)
        return 0

    loop('ff', FF // 256, ff_body)
    if sums:
        epoch_signal(0)
        take_credit(3)

    def norm1_body(t, _):
        rr = at(t, TT)
        g = s.gs[rr, :] + nt(s.slo[rr, :], s.wup[...])
        y = s.y1[rr, :].astype(F32)
        addrow(3, g * y)
        addrow(4, g)
        d = g * v_g1[...]
        gs = s.st[rr, 0:1] * (d - jnp.mean(d, -1, keepdims=True) - y * jnp.mean(d * y, -1, keepdims=True))
        s.gs[rr, :] = gs
        b = gs.astype(BF)
        s.gb[rr, :] = b
        addrow(2, b.astype(F32))
        return 0

    loop('norm1', T // TT, norm1_body)

    def gup_body(n, _):
        if sums:
            q = FF // 1024
            turn, k = n // q, lax.rem(n, q)
            n = lax.rem(1 - ring_d.c + turn, 2) * 2 * q + (turn // 2) * q + k
        c = at(n, 256)
        s.wup[:, c] = tn(s.fb[...], s.slo[:, c]).astype(BF)
        return 0

    loop('gup', FF // 256, gup_body)
    if sums:
        epoch_signal(1)

    def dctx_body(t, _):
        rr = at(t, TT)
        s.dctx[rr, :] = (nt(s.gb[rr, :], s.wout[...]) * s.dctx[rr, :].astype(F32)).astype(BF)
        return 0

    loop('dctx', T // TT, dctx_body)

    def gout_body(n, _):
        c = at(n, 256)
        s.wout[:, c] = tn(s.ctx[...], s.gb[:, c]).astype(BF)
        return 0

    loop('gout', D // 256, gout_body)
    if sums:
        q = D // 32
        lane = lax.broadcasted_iota(jnp.int32, (q, 128), 1)
        for i in range(FF // 384):
            for k in range(3):
                v = s.bup[0:1, i * 384 + k * 128 : i * 384 + k * 128 + 128]
                s.tcol[k * 128 : k * 128 + 128, :] = jnp.broadcast_to(v, (128, 128)).T
            for d in range(4):
                v = jnp.zeros((q, 128), F32)
                for k in range(4):
                    v = jnp.where(lane == 8 + k, s.tcol[(4 * d + k) * q : (4 * d + k) * q + q, :], v)
                s.vcol[(4 * i + d) * q : (4 * i + d) * q + q, :] = v
    if sums:
        ring_o.start(*al)

    def p_copy_in(j):
        g, rest = j // (2 * nrow), lax.rem(j, 2 * nrow)
        i = (rest // 2) * (H // 2) + 2 * g + lax.rem(rest, 2)
        slot = lax.rem(j, 2)
        return pltpu.make_async_copy(s.o_p.at[i], s.pbuf.at[slot], s.psem.at[slot])

    steps = nrow * (H // 2)
    p_copy_in(0).start()

    def turn(rr, n, cq, ck):
        do = s.dctx[rr, cq]
        s.qt[:, 0:n] = do.T
        s.vt[:, 0:n] = (-do.astype(F32) * s.ctx[rr, cq].astype(F32)).astype(BF).T
        s.kt[:, 0:n] = s.mixed[rr, ck].T

    def back_tile(qr, kr, qa, ka, kw, cq, ck, cv, e):
        values = jnp.concatenate([s.mixed[kr, cv], jnp.ones((kw, 128), BF)], 1)
        grads = jnp.concatenate([two(s.qt[:, qa], 0), two(s.vt[:, qa], 0)], 0)
        ds = (e.astype(F32) * nn(values, grads)).astype(BF)
        dk = nn(ds, two(s.mixed[qr, cq], 1))
        dv = nn(e, two(s.dctx[qr, cq], 1))
        dq = (diagonal(nn(s.kt[:, ka], ds)).T * 0.125).astype(BF)
        return dq, dk, dv

    def att_back(j, _):
        g, rest = j // (2 * nrow), lax.rem(j, 2 * nrow)
        r = rest // 2
        hp = 2 * g + lax.rem(rest, 2)
        slot = lax.rem(j, 2)

        @pl.when(j + 1 < steps)
        def _():
            p_copy_in(j + 1).start()

        p_copy_in(j).wait()
        cq, ck, cv = pair_cols(hp)
        base = r * LEN

        def rws(a, n):
            return rows_at(base + a, n, 128)

        turn(rws(0, LEN), LEN, cq, ck)
        s.dka[...] = jnp.zeros_like(s.dka)
        s.dva[...] = jnp.zeros_like(s.dva)
        for qs, ks, kw, off in TILES:
            dq, dk, dv = back_tile(
                rws(qs, 128), rws(ks, kw), slice(qs, qs + 128), slice(ks, ks + kw), kw, cq, ck, cv,
                s.pbuf[slot, off : off + kw, :],
            )
            s.dq[qs : qs + 128, :] = dq
            s.dka[ks : ks + kw, :] += dk
            s.dva[ks : ks + kw, :] += dv
        s.mixed[rws(0, LEN), cq] = s.dq[...]
        s.mixed[rws(0, LEN), ck] = (s.dka[...] * 0.125).astype(BF)
        s.mixed[rws(0, LEN), cv] = s.dva[...].astype(BF)
        return 0

    def att_back_q(hp, _):
        cq, ck, cv = pair_cols(hp)
        rr = slice(NP, T)
        turn(rr, NQ, cq, ck)
        dq, dk, dv = back_tile(rr, rr, slice(0, NQ), slice(0, NQ), NQ, cq, ck, cv, s.pq[hp])
        s.mixed[rr, cq] = dq
        s.mixed[rr, ck] = (dk * 0.125).astype(BF)
        s.mixed[rr, cv] = dv.astype(BF)
        return 0

    lax.fori_loop(0, H // 2, att_back_q, 0)

    groups = (s.fb, s.gb, s.ctx)

    def group_grad(g):
        for w in range(3):
            c = w * D + g * 256
            groups[g][0:D, w * 256 : w * 256 + 256] = tn(s.x[...], s.mixed[:, c : c + 256]).astype(BF)

    for g in range(3):

        @functools.partial(loop, 'att%d' % g, 2 * nrow)
        def _(j, _, g=g):
            att_back(2 * nrow * g + j, 0)

        group_grad(g)
        if sums:
            (ring_1, ring_2, ring_3)[g].start(*al)
    for w, k in ((0, 0), (2, 1)):
        s.vr[k : k + 1, :] = jnp.sum(s.mixed[:, w * D : w * D + D].astype(F32), axis=0, keepdims=True)

    if sums:
        pad = jnp.zeros((120, 128), F32)
        few = lax.broadcasted_iota(jnp.int32, (128, 128), 1) < 8
        for i in range(D // 128):
            rr = slice(i * 128, i * 128 + 128)
            s.vcol[rr, :] = jnp.where(few, jnp.concatenate([s.vr[:, rr], pad], 0).T, s.vcol[rr, :])
        s.misc[:, 128:256] = s.vcol[...].astype(BF)
        ring_m.start(*al)
        ring_3.to_a(*al)
        ring_m.to_a(*al)

    def dx_body(t, _):
        rr = at(t, TT)
        s.gs[rr, :] = s.gs[rr, :] + nt(s.mixed[rr, :], s.wqkv[...])
        return 0

    loop('dx', T // TT, dx_body)
    outs = [
        pltpu.make_async_copy(s.gs.at[0:NP], s.o_gp, s.osem.at[2]),
        pltpu.make_async_copy(s.gs.at[NP:T], s.o_gq, s.osem.at[3]),
    ]
    if not sums:
        outs += [
            pltpu.make_async_copy(s.wdn, s.o_dn, s.osem.at[4]),
            pltpu.make_async_copy(s.wup, s.o_up, s.osem.at[5]),
            pltpu.make_async_copy(s.wout, s.o_out, s.osem.at[6]),
            pltpu.make_async_copy(s.ctx.at[0:D], s.o_q.at[0], s.osem.at[7]),
            pltpu.make_async_copy(s.fb.at[0:D], s.o_q.at[1], s.osem.at[8]),
            pltpu.make_async_copy(s.gb.at[0:D], s.o_q.at[2], s.osem.at[9]),
            pltpu.make_async_copy(s.misc, s.o_misc, s.osem.at[10]),
        ]
        s.o_bup[...] = s.bup[0:1, :]
        s.o_vr[...] = s.vr[...]
    for c in outs:
        c.start()
    if sums:
        ring_3.to_b(*al)
        ring_m.to_b(*al)
        ring_v.out(put_up(1))
        ring_1.to_core()
        ring_o.out(put_in(s.o_out))
        ring_3.to_z(*al)
        ring_m.to_z(*al)
        ring_2.to_core()
        ring_1.out(put_group(0))
        ring_2.out(put_group(1))
        ring_3.to_core()
        ring_m.to_core()
        ring_3.out(put_group(2))
        ring_m.out(put_in(s.o_misc))
        for r in rings:
            r.finish()
    for c in q_copies + l_copies + g_copies + loss_copies:
        c.wait_send()
    for c in loss_copies:
        c.wait_recv()
    if cfg.loss_here:
        s.o_loss[...] = jnp.sum(s.ls[...], axis=0)
    else:
        s.o_loss[...] = s.ls[0]
    for c in [o_pe, o_qe] + outs:
        c.wait()


def finish_kernel(names, *refs):
    s = Space()
    for name, ref in zip(names, refs):
        setattr(s, name, ref)
    pairs = ((s.pe, s.o_pe), (s.qe, s.o_qe), (s.gp, s.o_gp), (s.gq, s.o_gq))
    pairs += ((s.dn, s.o_dn), (s.up, s.o_up), (s.out, s.o_out), (s.qkv, s.o_qkv))
    ways = []
    for (src, dst), buf in zip(pairs, (s.bpe, s.bqe, s.bgp, s.bgq, s.bdn, s.bup, s.bout, s.bqkv)):
        n = src.shape[0] // 4 if src.shape[0] > 512 else src.shape[0]
        for i in range(src.shape[0] // n):
            k = len(ways)
            rr = slice(i * n, i * n + n)
            ways.append(
                (
                    pltpu.make_async_copy(src.at[rr], buf.at[rr], s.sem.at[0, k]),
                    pltpu.make_async_copy(buf.at[rr], dst.at[rr], s.sem.at[1, k]),
                )
            )
    for c, _ in ways:
        c.start()
    s.o_loss[...] = s.loss[0, 0]
    s.o_proj[...] = s.misc[:, 0:128]
    q = s.misc.shape[0]
    s.sq[...] = jnp.zeros_like(s.sq)
    s.sq[0:q, :] = s.misc[:, 128:256]
    s.sq[...] = s.sq[...].T
    for k in range(8):
        getattr(s, "o_v%d" % k)[...] = s.sq[k, 0:q]
    s.o_bup[...] = jnp.concatenate([s.sq[8 + k : 9 + k, 0:q] for k in range(4)], 1)[0]
    for c, d in ways:
        c.wait()
        d.start()
    for _, d in ways:
        d.wait()


def finish(o):
    sd = jax.ShapeDtypeStruct
    any_spec = pl.BlockSpec(memory_space=pl.ANY)
    vm = pl.BlockSpec(memory_space=pltpu.VMEM)
    names = ["pe", "qe", "gp", "gq", "dn", "up", "out", "qkv"]
    ins = [(n, o["o_" + n], any_spec) for n in names] + [("loss", o["o_loss"], vm), ("misc", o["o_misc"], vm)]
    outs = [("o_" + n, sd(o["o_" + n].shape, o["o_" + n].dtype), any_spec) for n in names]
    q = o["o_misc"].shape[0]
    outs += [("o_loss", sd((), F32), pl.BlockSpec(memory_space=pltpu.SMEM)), ("o_proj", sd((q, 128), F32), vm)]
    outs += [("o_v%d" % k, sd((q,), F32), vm) for k in range(8)] + [("o_bup", sd((4 * q,), F32), vm)]
    scratch = [("sq", pltpu.VMEM((128, 128), F32)), ("sem", pltpu.SemaphoreType.DMA((2, 14)))]
    scratch += [("b" + n, pltpu.VMEM(o["o_" + n].shape, o["o_" + n].dtype)) for n in names]
    all_names = [n for n, *_ in ins] + [n for n, *_ in outs] + [n for n, _ in scratch]
    res = pl.pallas_call(
        functools.partial(finish_kernel, all_names),
        out_shape=[v[1] for v in outs],
        in_specs=[v[2] for v in ins],
        out_specs=[v[2] for v in outs],
        scratch_shapes=[v for _, v in scratch],
    )(*[v[1] for v in ins])
    return dict(zip([n for n, *_ in outs], res))


def make_body(n_dp, n_psg):
    def body(
        passage_states, segment_ids, query_states, teacher_scores,
        w_qkv, bias_q, bias_v, w_out, bias_out, ln1_gain, ln1_bias,
        w_up, bias_up, w_down, bias_down, ln2_gain, ln2_bias, w_proj,
    ):
        D, FF = w_up.shape
        E = w_proj.shape[1]
        rows, length, _ = passage_states.shape
        qn, ql, _ = query_states.shape
        NP, NQ = rows * length, qn * ql
        T = NP + NQ
        cfg = Space()
        cfg.T, cfg.NP, cfg.NQ, cfg.TT = T, NP, NQ, T // 4
        cfg.D, cfg.FF, cfg.qlen = D, FF, ql
        cfg.n_dp, cfg.n_psg = n_dp, n_psg
        cfg.loss_here = n_dp <= 16
        cfg.sums = n_dp == 8 and n_psg == 4
        npair = rows * (H // 2)
        any_spec = pl.BlockSpec(memory_space=pl.ANY)
        vm = pl.BlockSpec(memory_space=pltpu.VMEM)
        ins = [
            ("i_pass", passage_states.reshape(NP, D), any_spec),
            ("i_query", query_states.reshape(NQ, D), any_spec),
            ("i_seg", segment_ids, vm),
            ("i_teach", teacher_scores.T, vm),
            ("i_wqkv", w_qkv, any_spec),
            ("i_bq", bias_q, vm),
            ("i_bv", bias_v, vm),
            ("i_wout", w_out, any_spec),
            ("i_bout", bias_out, vm),
            ("i_g1", ln1_gain, vm),
            ("i_b1", ln1_bias, vm),
            ("i_wup", w_up, any_spec),
            ("i_bup", bias_up, vm),
            ("i_wdn", w_down, any_spec),
            ("i_bdn", bias_down, vm),
            ("i_g2", ln2_gain, vm),
            ("i_b2", ln2_bias, vm),
            ("i_wproj", w_proj, any_spec),
        ]
        sd = jax.ShapeDtypeStruct
        outs = [
            ("o_pe", sd((NP, E), BF), any_spec),
            ("o_qe", sd((NQ, E), BF), any_spec),
            ("o_loss", sd((8, 128), F32), vm),
            ("o_gp", sd((NP, D), F32), any_spec),
            ("o_gq", sd((NQ, D), F32), any_spec),
            ("o_p", sd((npair, PW, 256), BF), any_spec),
        ]
        n_dev = n_dp * n_psg
        if cfg.sums:
            outs += [
                ("o_dn", sd((FF // n_dev, D), F32), vm),
                ("o_up", sd((D // n_dev, FF), F32), vm),
                ("o_out", sd((D // n_dev, D), F32), vm),
                ("o_qkv", sd((D // n_dev, 3 * D), F32), vm),
                ("o_misc", sd((D // n_dev, 256), F32), vm),
            ]
        else:
            outs += [
                ("o_dn", sd((FF, D), BF), any_spec),
                ("o_up", sd((D, FF), BF), any_spec),
                ("o_out", sd((D, D), BF), any_spec),
                ("o_q", sd((3, D, D), BF), any_spec),
                ("o_misc", sd((D, 256), BF), any_spec),
                ("o_bup", sd((1, FF), F32), vm),
                ("o_vr", sd((8, D), F32), vm),
            ]
        V = pltpu.VMEM
        DMA = pltpu.SemaphoreType.DMA
        scratch = [
            ("x", V((T, D), BF)),
            ("wqkv", V((D, 3 * D), BF)),
            ("wout", V((D, D), BF)),
            ("wup", V((D, FF), BF)),
            ("wdn", V((FF, D), BF)),
            ("wproj", V((D, E), BF)),
            ("bqkv", V((8, 3 * D), F32)),
            ("vin", V((8, D), F32)),
            ("tsq", V((128, 128), F32)),
            ("mixed", V((T, 3 * D), BF)),
            ("pbuf", V((2, PW, 256), BF)),
            ("pq", V((H // 2, NQ, 256), BF)),
            ("koh", V((T, 128), BF)),
            ("qoh", V((128, T), BF)),
            ("qt", V((128, LEN), BF)),
            ("vt", V((128, LEN), BF)),
            ("kt", V((128, LEN), BF)),
            ("ctx", V((T, D), BF)),
            ("y1", V((T, D), BF)),
            ("fb", V((T, D), BF)),
            ("hid", V((T, FF), BF)),
            ("slo", V((T, FF), BF)),
            ("gs", V((T, D), F32)),
            ("gb", V((T, D), BF)),
            ("st", V((T, 128), F32)),
            ("unit", V((T, E), F32)),
            ("unitb", V((T, E), BF)),
            ("aq", V((n_psg, NQ, E), BF)),
            ("ind", V((NP, 128), BF)),
            ("tot", V((n_psg, NQ, 128), F32)),
            ("lg", V((n_psg, 2 * n_psg * qn, 128), F32)),
            ("line", V((n_psg * NQ, 128), F32)),
            ("gl", V((n_psg * qn, 128), F32)),
            ("ls", V((n_dp if cfg.loss_here else 1, 8, 128), F32)),
            ("gsim", V((n_psg * NQ, NP), BF)),
            ("qs", V((n_psg, NQ, E), BF)),
            ("qr", V((n_psg, NQ, E), BF)),
            ("own", V((NQ, E), F32)),
            ("gp", V((T, E), BF)),
            ("misc", V((D, 256), BF)),
            ("vr", V((8, D), F32)),
            ("vcol", V((D, 128), F32)),
            ("bup", V((8, FF), F32)),
            ("dctx", V((T, D), BF)),
            ("dq", V((LEN, 128), BF)),
            ("dka", V((LEN, 128), F32)),
            ("dva", V((LEN, 128), F32)),
            ("lsem", DMA((7,))),
            ("psem", DMA((2,))),
            ("osem", DMA((11,))),
            ("ss", DMA((3, n_psg))),
            ("rs", DMA((3, n_psg))),
            ("lss", DMA((n_dp,))),
            ("lrs", DMA((n_dp,))),
        ]
        if cfg.sums:
            b, e = D // 16, FF // 16
            scratch += [
                ("tcol", V((384, 128), F32)),
                ("mrecv", V((31 * b, 128), BF)),
                ("fd", V((e, D // 2), F32)),
                ("rd", V((e // 2, D // 2), F32)),
                ("fu", V((2, b, FF // 4), F32)),
                ("ru", V((2, b // 2, FF // 4), F32)),
                ("fq", V((4, b, D // 2), F32)),
                ("rq", V((4, b // 2, D // 2), F32)),
                ("fm", V((b, 128), F32)),
                ("rm", V((b // 2, 128), F32)),
                ("gss", DMA((8, 18))),
                ("grs", DMA((8, 18))),
                ("arecv", V((8 * e, D // 2), BF)),
                ("credit", pltpu.SemaphoreType.REGULAR((5,))),
                ("epoch", pltpu.SemaphoreType.REGULAR((2,))),
            ]
        cfg.names = [a for a, *_ in ins] + [a for a, *_ in outs] + [a for a, _ in scratch]
        res = pl.pallas_call(
            functools.partial(kernel, cfg),
            out_shape=[o[1] for o in outs],
            in_specs=[i[2] for i in ins],
            out_specs=[o[2] for o in outs],
            scratch_shapes=[v for _, v in scratch],
            compiler_params=pltpu.CompilerParams(
                collective_id=0, has_side_effects=True, vmem_limit_bytes=64 * 1024 * 1024 - 65536
            ),
        )(*[i[1] for i in ins])
        o = dict(zip([a for a, *_ in outs], res))
        if cfg.sums:
            o = finish(o)
            loss = o["o_loss"]
        else:
            loss = o["o_loss"][0, 0]
        if not cfg.loss_here:
            loss = lax.psum(loss, "dp")
        head = (
            o["o_pe"].reshape(rows, length, E),
            o["o_qe"].reshape(qn, ql, E),
            loss,
            o["o_gp"].reshape(rows, length, D),
            o["o_gq"].reshape(qn, ql, D),
        )
        if cfg.sums:
            vec = [o["o_v%d" % k] for k in range(8)]
            g_qkv, g_out, g_up, g_bup, g_dn, g_proj = [
                o["o_" + k] for k in ("qkv", "out", "up", "bup", "dn", "proj")
            ]
        else:
            q3 = o["o_q"].reshape(3, D, 3, 256)
            q3 = jnp.transpose(q3, (1, 2, 0, 3)).reshape(D, 3 * D)

            def scat(v):
                return lax.psum_scatter(v, ("dp", "psg"), scatter_dimension=0, tiled=True)

            vec = scat(o["o_vr"].T)
            vec = [vec[:, k] for k in range(8)]
            g_bup = scat(o["o_bup"].reshape(-1))
            g_qkv, g_out, g_up, g_dn, g_proj = [
                scat(v.astype(F32)) for v in (q3, o["o_out"], o["o_up"], o["o_dn"], o["o_misc"][:, 0:128])
            ]
        return head + (
            g_qkv, vec[0], vec[1], g_out, vec[2], vec[3], vec[4],
            g_up, g_bup, g_dn, vec[5], vec[6], vec[7], g_proj,
        )

    return body


def solution(mesh):
    rowspec = P(("dp", "psg"))
    three = P(("dp", "psg"), None, None)
    two = P(("dp", "psg"), None)
    in_specs = (three, two, three, P("dp", "psg")) + (P(),) * 14
    out_specs = (
        three, three, P(), three, three,
        two, rowspec, rowspec, two, rowspec, rowspec, rowspec,
        two, rowspec, two, rowspec, rowspec, rowspec, two,
    )
    body = make_body(mesh.shape["dp"], mesh.shape["psg"])
    return jax.shard_map(body, mesh=mesh, in_specs=in_specs, out_specs=out_specs, check_vma=False)
```
